512 devices in a mesh: seq: 32 (over y, z_lo), batch: 16 (over z_hi, x, core).
Axes of the slice: x: 4, y: 4, z: 16 (z_hi: 2, z_lo: 8; z = z_hi * 8 + z_lo), core: 2. Of those that a mesh axis runs over, the one named last changes fastest.
Arguments:
- activations: bfloat16 [16, 16384, 768], P('batch', 'seq'), may hold values from -96 to 96
- norm_gain: float32 [768], replicated, may hold values from 0.25 to 1.75
- dilated_tap_weight: bfloat16 [3, 768, 384], replicated, may hold values from -0.125 to 0.125
- point_weight: bfloat16 [384, 768], replicated, may hold values from -0.15625 to 0.15625
- donor_weight: bfloat16 [768, 256], replicated, may hold values from -0.013671875 to 0.013671875
- acceptor_weight: bfloat16 [768, 256], replicated, may hold values from -0.013671875 to 0.013671875
- pair_sites: int32 [16, 512, 2], P('batch', 'seq'), may hold values from 0 to 16383, as said below
- pair_count: int32 [16, 32], P('batch', 'seq'), may hold values from 8 to 16, as said below
Outputs:
- grad_conv: float32 [3, 768, 384], P(None, 'seq')
- grad_point: bfloat16 [16, 384, 768], P('batch')
- grad_donor: bfloat16 [16, 768, 256], P('batch')
- grad_acceptor: bfloat16 [16, 768, 256], P('batch')
- grad_gain: float32 [16, 768], P('batch')
- loss: float32 [16], P('batch')
The draws below stay inside these ranges and needn't reach their ends.
Inputs may be any that keep to these rules, and one draw needn't show every extreme that they name: `pair_sites`: slot j's donor position lies among the 512 positions of device j // 16; its acceptor lies on that device or on one of the next 4 devices, within the example; in every draw some live pair reaches exactly 4 devices ahead. The live slots of a device are its first pair_count slots; in every example some device has all 16 live.
All inputs are finite; a program needn't handle non-finite values.
Results may differ from the reference program's by a relative error of at most 0.018.
Values may be sent and summed in bfloat16 or wider, within the bound.
No kernel may reach another device: no remote copies, remote signals or barrier semaphores. Data moves between devices by JAX's collectives and lax.ppermute only.
A program may use at most 64 MiB of HBM per device.

```python
import jax
import jax.numpy as jnp
from jax import lax

C = 768
INNER = 384
H = 256
TAPS = 3
DILATION_STEP = 128
PANEL = 128
SPAN = 4
P_SIZE = 512
PAIR_DEV = 16
LENGTH = 16384
PAIRS = 512
BATCH = 16


def draw_activations(key, part):
    key = jax.random.fold_in(key, 5)
    first = jax.random.fold_in(key, 0)
    shape = (BATCH, LENGTH, C)
    values = jax.random.truncated_normal(first, -6.0, 6.0, shape, jnp.float32) * 16.0
    return values.astype(jnp.bfloat16)


def draw_pair_sites(key, part):
    key = jax.random.fold_in(key, 11)
    first, second, third = jax.random.split(key, 3)
    devices = PAIRS // PAIR_DEV
    owner = jnp.arange(PAIRS, dtype=jnp.int32) // PAIR_DEV
    owner = jnp.broadcast_to(owner[None, :], (BATCH, PAIRS))
    donor = owner * P_SIZE + jax.random.randint(first, (BATCH, PAIRS), 0, P_SIZE, dtype=jnp.int32)
    reach = jnp.minimum(SPAN, devices - 1 - owner)
    offset = jax.random.randint(second, (BATCH, PAIRS), 0, reach + 1, dtype=jnp.int32)
    offset = offset.at[:, 0].set(SPAN)
    acceptor = (owner + offset) * P_SIZE + jax.random.randint(third, (BATCH, PAIRS), 0, P_SIZE, dtype=jnp.int32)
    return jnp.stack([donor, acceptor], axis=-1).astype(jnp.int32)


def draw_pair_count(key, part):
    key = jax.random.fold_in(key, 23)
    first, second = jax.random.split(key)
    devices = PAIRS // PAIR_DEV
    counts = jax.random.randint(first, (BATCH, devices), PAIR_DEV // 2, PAIR_DEV + 1, dtype=jnp.int32)
    busiest = jax.random.randint(second, (BATCH, 1), 0, devices, dtype=jnp.int32)
    places = jnp.arange(devices, dtype=jnp.int32)[None, :]
    return jnp.where(places == busiest, PAIR_DEV, counts).astype(jnp.int32)


def bell_draw(own_key, dims, deviation, most, kind=jnp.bfloat16):
    return jnp.clip(deviation * jax.random.normal(own_key, dims, jnp.float32), -most, most).astype(kind)


def setup_inputs(seed: int = 0) -> dict:
    key_of = jax.random.split(jax.random.key(seed), 9)
    activations = draw_activations(jax.random.fold_in(key_of[8], 71), 0)
    norm_gain = jnp.clip(1.0 + 0.15 * jax.random.normal(key_of[1], (C,), jnp.float32), 0.25, 1.75)
    dilated_tap_weight = bell_draw(key_of[2], (TAPS, C, INNER), (TAPS * C) ** -0.5, 0.125)
    point_weight = bell_draw(key_of[3], (INNER, C), (4 * INNER) ** -0.5, 0.15625)
    donor_weight = bell_draw(key_of[4], (C, H), (256 * C) ** -0.5, 0.013671875)
    acceptor_weight = bell_draw(key_of[5], (C, H), (256 * C) ** -0.5, 0.013671875)
    pair_sites = draw_pair_sites(jax.random.fold_in(key_of[8], 71), 0)
    pair_count = draw_pair_count(jax.random.fold_in(key_of[8], 71), 0)
    return {"activations": activations, "norm_gain": norm_gain, "dilated_tap_weight": dilated_tap_weight, "point_weight": point_weight, "donor_weight": donor_weight, "acceptor_weight": acceptor_weight, "pair_sites": pair_sites, "pair_count": pair_count}


EPSILON = 1e-06
LOSS_WEIGHT = 1.0 / 128.0

def gelu_slope(values):
    return jax.vjp(jax.nn.gelu, values)[1](jnp.ones_like(values))[0]

def example_grads(operands, norm_gain, dilated_tap_weight, point_weight, donor_weight, acceptor_weight):
    tokens, sites, counts = operands
    sequence_length = tokens.shape[0]
    tap_count = dilated_tap_weight.shape[0]
    inner = dilated_tap_weight.shape[2]
    heads = donor_weight.shape[1]
    scale = heads ** (-0.5)
    tokens_f = tokens.astype(jnp.float32)
    inv_rms = lax.rsqrt(lax.optimization_barrier(jnp.mean(tokens_f * tokens_f, axis=-1, keepdims=True)) + EPSILON)
    normed = tokens_f * inv_rms * norm_gain
    hidden_state = jax.nn.gelu(normed).astype(jnp.bfloat16)
    padded_input = jnp.pad(hidden_state, ((DILATION_STEP, DILATION_STEP), (0, 0)))
    dilated_output = jnp.zeros((sequence_length, inner), jnp.float32)
    for tap_index in range(tap_count):
        dilated_output = dilated_output + jnp.dot(padded_input[tap_index * DILATION_STEP:tap_index * DILATION_STEP + sequence_length], dilated_tap_weight[tap_index], preferred_element_type=jnp.float32)
    act = jax.nn.gelu(dilated_output).astype(jnp.bfloat16)
    embed = (tokens_f + jnp.dot(act, point_weight, preferred_element_type=jnp.float32)).astype(jnp.bfloat16)
    donor_feat = jnp.dot(embed, donor_weight, preferred_element_type=jnp.float32).astype(jnp.bfloat16)
    accept_feat = jnp.dot(embed, acceptor_weight, preferred_element_type=jnp.float32).astype(jnp.bfloat16)
    donor_blocks = donor_feat.reshape(-1, PANEL, heads)
    accept_blocks = accept_feat.reshape(-1, PANEL, heads)
    donor_block = (sites[:, 0] // PANEL).astype(jnp.int32)
    accept_block = (sites[:, 1] // PANEL).astype(jnp.int32)
    donor_cell = sites[:, 0] % PANEL
    accept_cell = sites[:, 1] % PANEL
    slots = jnp.arange(sites.shape[0], dtype=jnp.int32)
    live = (slots % PAIR_DEV < counts[slots // PAIR_DEV]).astype(jnp.float32) * LOSS_WEIGHT
    donor_panel = donor_blocks[donor_block]
    accept_panel = accept_blocks[accept_block]
    scores = jnp.einsum('pqh,prh->pqr', donor_panel.astype(jnp.float32), accept_panel.astype(jnp.float32)) * scale
    cells = jnp.arange(PANEL, dtype=jnp.int32)
    target = ((cells[None, :, None] == donor_cell[:, None, None]) & (cells[None, None, :] == accept_cell[:, None, None])).astype(jnp.float32)
    loss = jnp.sum((jax.nn.softplus(scores) - target * scores) * live[:, None, None])
    dscore = ((jax.nn.sigmoid(scores) - target) * live[:, None, None]).astype(jnp.bfloat16)
    d_donor_pairs = jnp.einsum('pqr,prh->pqh', dscore.astype(jnp.float32), accept_panel.astype(jnp.float32)) * scale
    d_accept_pairs = jnp.einsum('pqr,pqh->prh', dscore.astype(jnp.float32), donor_panel.astype(jnp.float32)) * scale
    d_donor = jnp.zeros(donor_blocks.shape, jnp.float32).at[donor_block].add(d_donor_pairs)
    d_accept = jnp.zeros(accept_blocks.shape, jnp.float32).at[accept_block].add(d_accept_pairs)
    d_donor = d_donor.reshape(sequence_length, heads).astype(jnp.bfloat16)
    d_accept = d_accept.reshape(sequence_length, heads).astype(jnp.bfloat16)
    d_embed = (jnp.dot(d_donor, donor_weight.T, preferred_element_type=jnp.float32) + jnp.dot(d_accept, acceptor_weight.T, preferred_element_type=jnp.float32)).astype(jnp.bfloat16)
    grad_donor = jnp.dot(embed.T, d_donor, preferred_element_type=jnp.float32)
    grad_accept = jnp.dot(embed.T, d_accept, preferred_element_type=jnp.float32)
    grad_point = jnp.dot(act.T, d_embed, preferred_element_type=jnp.float32)
    d_act = jnp.dot(d_embed, point_weight.T, preferred_element_type=jnp.float32)
    dilated_output_gradient = (d_act * gelu_slope(dilated_output)).astype(jnp.bfloat16)
    trailing_padding = jnp.pad(dilated_output_gradient, ((DILATION_STEP, DILATION_STEP), (0, 0)))
    tap_gradient_rows = []
    d_hidden = jnp.zeros((sequence_length, tokens.shape[1]), jnp.float32)
    for tap_index in range(tap_count):
        tap_gradient_rows.append(jnp.dot(padded_input[tap_index * DILATION_STEP:tap_index * DILATION_STEP + sequence_length].T, dilated_output_gradient, preferred_element_type=jnp.float32))
        window_start = (tap_count - 1 - tap_index) * DILATION_STEP
        d_hidden = d_hidden + jnp.dot(trailing_padding[window_start:window_start + sequence_length], dilated_tap_weight[tap_index].T, preferred_element_type=jnp.float32)
    grad_conv = jnp.stack(tap_gradient_rows)
    d_normed = d_hidden * gelu_slope(normed)
    grad_gain = lax.optimization_barrier(jnp.sum(d_normed * tokens_f * inv_rms, axis=0))
    return (grad_conv, grad_point, grad_donor, grad_accept, grad_gain, loss)

def reference(activations, norm_gain, dilated_tap_weight, point_weight, donor_weight, acceptor_weight, pair_sites, pair_count):

    def per_example(operands):
        return example_grads(operands, norm_gain, dilated_tap_weight, point_weight, donor_weight, acceptor_weight)
    grad_conv, grad_point, grad_donor, grad_accept, grad_gain, loss = lax.map(per_example, (activations, pair_sites, pair_count))
    return (lax.optimization_barrier(jnp.sum(grad_conv, axis=0)), grad_point.astype(jnp.bfloat16), grad_donor.astype(jnp.bfloat16), grad_accept.astype(jnp.bfloat16), grad_gain, loss)
```

```python
import jax
import jax.numpy as jnp
import numpy as np
from jax import lax
from jax.experimental import pallas as pl
from jax.experimental.pallas import tpu as pltpu
from jax.sharding import Mesh
from jax.sharding import PartitionSpec as P

STEP = 128
PANEL = 128
SPAN = 4
SLOTS = 16
EPSILON = 1e-06
LOSS_WEIGHT = 1.0 / 128.0
SEQ = ("y", "zb", "zq")
BATCH = ("zhi", "x", "core")
F32 = jnp.float32
BF16 = jnp.bfloat16
ROOT = 0.7978845608028654
CUBIC = 0.044715
VMEM_BYTES = 56 * 1024 * 1024
PIECE = 96
CHUNK_ROWS = 288
EXTRA_ROWS = 16


def dot(a, b):
    return lax.dot_general(a, b, (((1,), (0,)), ((), ())), preferred_element_type=F32)


def dot_t(a, b):
    return lax.dot_general(a, b, (((1,), (1,)), ((), ())), preferred_element_type=F32)


def gelu(v):
    return 0.5 * v * (1.0 + jnp.tanh(ROOT * (v + CUBIC * (v * v * v))))


def gelu_slope(v):
    square = v * v
    t = jnp.tanh(ROOT * (v + CUBIC * (square * v)))
    return 0.5 * (1.0 + t) + 0.5 * v * (1.0 - t * t) * (ROOT * (1.0 + 3.0 * CUBIC * square))


def rms(v):
    return lax.rsqrt(jnp.mean(v * v, axis=-1, keepdims=True) + EPSILON)


def call(kernel, outs, flops, n_bytes, specs=None, scratch=()):
    vmem = pl.BlockSpec(memory_space=pltpu.VMEM)
    return pl.pallas_call(
        kernel,
        out_shape=outs,
        in_specs=specs,
        out_specs=[vmem] * len(outs),
        scratch_shapes=list(scratch),
        compiler_params=pltpu.CompilerParams(vmem_limit_bytes=VMEM_BYTES),
        cost_estimate=pl.CostEstimate(flops=flops, bytes_accessed=n_bytes, transcendentals=0),
    )


VM = pl.BlockSpec(memory_space=pltpu.VMEM)
SM = pl.BlockSpec(memory_space=pltpu.SMEM)


def forward_kernel(
    tok, low, high, gain, taps, point, donor_w, accept_w, meta,
    hidden, conv_out, act_out, embed_out, donor_out, accept_out,
):
    rows = tok.shape[0]

    def activate(src, start, at):
        v = src[pl.ds(start, STEP), :].astype(F32)
        hidden[pl.ds(at, STEP), :] = gelu(v * rms(v) * gain[...]).astype(BF16)

    activate(low, 0, 0)
    activate(high, 0, STEP + rows)

    @pl.loop(0, rows // STEP)
    def _(i):
        start = pl.multiple_of(i * STEP, STEP)
        activate(tok, start, pl.multiple_of(start + STEP, STEP))

    @pl.loop(0, rows // 256)
    def _(i):
        start = pl.multiple_of(i * 256, 256)
        here = pl.ds(start, 256)
        conv = dot(hidden[here, :], taps[0])
        for tap in range(1, taps.shape[0]):
            at = pl.multiple_of(start + tap * STEP, STEP)
            conv = conv + dot(hidden[pl.ds(at, 256), :], taps[tap])
        conv_out[here, :] = conv
        act = gelu(conv).astype(BF16)
        act_out[here, :] = act
        embed = (tok[here, :].astype(F32) + dot(act, point[...])).astype(BF16)
        embed_out[here, :] = embed
        donor_out[here, :] = dot(embed, donor_w[...]).astype(BF16)
        accept_out[here, :] = dot(embed, accept_w[...]).astype(BF16)

    donor_out[pl.ds(rows, SLOTS), :] = meta[...]


def side_kernel(
    tok, low, high, gain, hidden, conv, act, embed, order, eye,
    factor, slope, hidden_t, act_t, embed_t,
):
    rows = tok.shape[0]

    def weigh(src, start, at):
        v = src[pl.ds(start, STEP), :].astype(F32)
        unit = v * rms(v)
        factor[pl.ds(at, STEP), :] = (gelu_slope(unit * gain[...]) * unit).astype(BF16)

    weigh(low, 0, 0)
    weigh(high, 0, STEP + rows)

    @pl.loop(0, rows // STEP)
    def _(i):
        start = pl.multiple_of(i * STEP, STEP)
        weigh(tok, start, pl.multiple_of(start + STEP, STEP))
        slope[pl.ds(start, STEP), :] = gelu_slope(conv[pl.ds(start, STEP), :])

    @pl.loop(0, hidden_t.shape[0] // 256)
    def _(i):
        here = pl.ds(pl.multiple_of(i * 256, 256), 256)
        hidden_t[here, :] = dot_t(order[here, :], hidden[...]).astype(BF16)
        embed_t[here, :] = dot_t(eye[here, :], embed[...]).astype(BF16)

    inner = act.shape[1]

    @pl.loop(0, inner // 128)
    def _(i):
        here = pl.ds(pl.multiple_of(i * 128, 128), 128)
        act_t[here, :] = dot_t(eye[here, :inner], act[...]).astype(BF16)


def pair_kernel(distance, *refs):
    if distance == 0:
        own, dfeat, afeat, d_donor, d_accept, loss = refs
        d_donor[...] = jnp.zeros_like(d_donor)
        d_accept[...] = jnp.zeros_like(d_accept)
        loss[...] = jnp.zeros_like(loss)
        far, afar, dfar = None, afeat, None
    else:
        own, far, dfeat, afeat, dfar, afar, dd_in, da_in, loss_in, d_donor, d_accept, loss = refs
        d_donor[...] = dd_in[...]
        d_accept[...] = da_in[...]
        loss[...] = loss_in[...]
    scale = dfeat.shape[1] ** (-0.5)
    per_device = afeat.shape[0] // PANEL
    row = lax.broadcasted_iota(jnp.int32, (PANEL, PANEL), 0)
    col = lax.broadcasted_iota(jnp.int32, (PANEL, PANEL), 1)

    def panel(ref, block):
        return ref.at[pl.ds(pl.multiple_of(block * PANEL, PANEL), PANEL), :]

    def visit(meta, j, donors, acceptors, is_owner):
        accept_block = meta[j, 2] - distance * per_device
        here = (meta[j, 4] > 0) & (accept_block >= 0) & (accept_block < per_device)

        @pl.when(here)
        def _():
            donor_block = meta[j, 0]
            dpan = panel(donors, donor_block)[...]
            apan = panel(acceptors, accept_block)[...]
            scores = dot_t(dpan, apan) * scale
            target = ((row == meta[j, 1]) & (col == meta[j, 3])).astype(F32)
            small = jnp.exp(-jnp.abs(scores))
            inverse = 1.0 / (1.0 + small)
            sigmoid = jnp.where(scores >= 0, inverse, small * inverse)
            dscore = ((sigmoid - target) * LOSS_WEIGHT).astype(BF16)
            if is_owner:
                loss[...] += (jnp.maximum(scores, 0.0) + jnp.log1p(small)) - target * scores
                into = panel(d_donor, donor_block)
                into[...] += dot(dscore, apan) * scale
            if distance == 0 or not is_owner:
                into = panel(d_accept, accept_block)
                into[...] += (
                    lax.dot_general(
                        dscore, dpan, (((0,), (0,)), ((), ())), preferred_element_type=F32
                    )
                    * scale
                )

    @pl.loop(0, SLOTS)
    def _(j):
        visit(own, j, dfeat, afar, True)
        if distance > 0:
            visit(far, j, dfar, afeat, False)


def backward_kernel(
    d_donor, d_accept, loss, taps, point, donor_w, accept_w, factor, slope, hidden_t, act_t, embed_t,
    conv_sum, head_sum, d_conv, d_feat,
):
    rows = d_donor.shape[0]
    heads = d_donor.shape[1]
    channels = hidden_t.shape[0]
    inner = act_t.shape[0]

    @pl.loop(0, rows // 256)
    def _(i):
        here = pl.ds(pl.multiple_of(i * 256, 256), 256)
        dd = d_donor[here, :].astype(BF16)
        da = d_accept[here, :].astype(BF16)
        d_feat[here, :heads] = dd
        d_feat[here, heads:] = da
        d_embed = (dot_t(dd, donor_w[...]) + dot_t(da, accept_w[...])).astype(BF16)
        d_conv[here, :] = (dot_t(d_embed, point[...]) * slope[here, :]).astype(BF16)

    lanes = inner // 128
    for tap in range(taps.shape[0]):

        @pl.loop(0, channels // (2 * PIECE))
        def _(i):
            here = pl.ds(pl.multiple_of(i * 2 * PIECE, 2 * PIECE), 2 * PIECE)
            part = dot(hidden_t[here, tap * STEP : tap * STEP + rows], d_conv[...]).astype(BF16)
            for half in range(2):
                for lane in range(lanes):
                    conv_sum[i * 2 + half, tap * lanes + lane] = part[
                        half * PIECE : (half + 1) * PIECE, lane * 128 : (lane + 1) * 128
                    ]

    def put(part, base, group_rows, first):
        for lane in range(4):
            for k in range(part.shape[0] // PIECE):
                at = lane * (group_rows // PIECE) + k + base
                piece = first + at
                chunk, place = piece // 3, piece % 3
                head_sum[chunk, place * PIECE : (place + 1) * PIECE, :] = part[
                    k * PIECE : (k + 1) * PIECE, lane * 128 : (lane + 1) * 128
                ]

    for i in range(channels // (2 * PIECE)):
        part = dot(embed_t[i * 2 * PIECE : (i + 1) * 2 * PIECE, :], d_feat[...]).astype(BF16)
        put(part, 2 * i, channels, 0)
    for i in range(inner // (2 * PIECE)):
        part = dot(act_t[i * 2 * PIECE : (i + 1) * 2 * PIECE, :], d_feat[...]).astype(BF16)
        put(part, 2 * i, inner, 4 * channels // PIECE)

    def gain_part(i, total):
        start = pl.multiple_of(i * STEP, STEP)
        for tap in range(taps.shape[0]):
            at = pl.multiple_of(start + tap * STEP, STEP)
            product = dot_t(d_conv[pl.ds(start, STEP), :], taps[tap]) * factor[
                pl.ds(at, STEP), :
            ].astype(F32)
            total = total + jnp.sum(product.reshape(STEP // 8, 8, channels), axis=0)
        return total

    total = lax.fori_loop(0, rows // STEP, gain_part, jnp.zeros((8, channels), F32))
    gain = jnp.sum(total, axis=0, keepdims=True)
    loss_row = jnp.sum(loss[...], axis=0, keepdims=True) * LOSS_WEIGHT
    loss_all = jnp.broadcast_to(jnp.sum(loss_row, axis=1, keepdims=True), (1, 128))
    for chunk in range(head_sum.shape[0]):
        at_row = lax.broadcasted_iota(jnp.int32, (EXTRA_ROWS, 128), 0)
        if chunk < channels // 128:
            value = gain[:, chunk * 128 : (chunk + 1) * 128]
        elif chunk == channels // 128:
            value = loss_all
        else:
            value = jnp.zeros((1, 128), F32)
        coarse = value.astype(BF16).astype(F32)
        block = jnp.where(at_row == 0, coarse, 0.0) + jnp.where(at_row == 8, value - coarse, 0.0)
        head_sum[chunk, CHUNK_ROWS:, :] = block.astype(BF16)


def shifted(block, distance):
    count = lax.axis_size(SEQ)
    route = [(i, i + distance) for i in range(count) if 0 <= i + distance < count]
    return lax.ppermute(block, SEQ, route)


def swap_parts(parts, axis):
    return lax.all_to_all(parts, axis, 0, 0, tiled=True)


def gather_parts(part, axis):
    count = lax.axis_size(axis)
    return swap_parts(jnp.broadcast_to(part[None], (count,) + part.shape), axis)


def summed(parts):
    return jnp.sum(parts.astype(F32), axis=0)


def resplit(total):
    body = total[..., :CHUNK_ROWS, :].astype(BF16)
    value = (
        total[..., CHUNK_ROWS : CHUNK_ROWS + 8, :] + total[..., CHUNK_ROWS + 8 : CHUNK_ROWS + 16, :]
    )
    coarse = lax.reduce_precision(value, 8, 7)
    return jnp.concatenate([body, coarse.astype(BF16), (value - coarse).astype(BF16)], axis=-2)


def on_device(
    activations, norm_gain, dilated_tap_weight, point_weight, donor_weight, acceptor_weight,
    pair_sites, pair_count, order, eye,
):
    tokens = activations[0]
    rows, channels = tokens.shape
    tap_count, _, inner = dilated_tap_weight.shape
    heads = donor_weight.shape[1]
    blocks = rows // PANEL
    shape = jax.ShapeDtypeStruct
    low = shifted(tokens[rows - STEP :], 1)
    high = shifted(tokens[:STEP], -1)
    gain = norm_gain[None]
    sites = pair_sites[0]
    first = lax.axis_index(SEQ) * blocks
    live = (jnp.arange(SLOTS, dtype=jnp.int32) < pair_count[0, 0]).astype(jnp.int32)
    meta = jnp.stack(
        [
            sites[:, 0] // PANEL - first,
            sites[:, 0] % PANEL,
            sites[:, 1] // PANEL - first,
            sites[:, 1] % PANEL,
            live,
        ]
        + [jnp.zeros_like(live)] * 3,
        axis=1,
    )
    meta_rows = jnp.pad(meta.astype(BF16), ((0, 0), (0, heads - meta.shape[1])))

    hidden, conv, act, embed, donor_feat, accept_feat = call(
        forward_kernel,
        [
            shape((rows + 2 * STEP, channels), BF16),
            shape((rows, inner), F32),
            shape((rows, inner), BF16),
            shape((rows, channels), BF16),
            shape((rows + SLOTS, heads), BF16),
            shape((rows, heads), BF16),
        ],
        1_700_000_000,
        8_000_000,
        [VM] * 9,
    )(
        tokens, low, high, gain, dilated_tap_weight, point_weight, donor_weight, acceptor_weight,
        meta_rows,
    )

    acc = call(
        lambda *refs: pair_kernel(0, *refs),
        [shape((rows, heads), F32), shape((rows, heads), F32), shape((PANEL, PANEL), F32)],
        1_000_000_000,
        4_000_000,
        [SM] + [VM] * 2,
    )(meta, donor_feat, accept_feat)
    factor, slope, hidden_t, act_t, embed_t = call(
        side_kernel,
        [
            shape((rows + 2 * STEP, channels), BF16),
            shape((rows, inner), F32),
            shape((channels, rows + 2 * STEP), BF16),
            shape((inner, rows), BF16),
            shape((channels, rows), BF16),
        ],
        4_000_000_000,
        10_000_000,
        [VM] * 10,
    )(tokens, low, high, gain, hidden, conv, act, embed, order, eye)
    far_accept, far_donor = accept_feat, donor_feat
    for distance in range(1, SPAN + 1):
        far_accept = shifted(far_accept, -1)
        far_donor = shifted(far_donor, 1)
        far_meta = far_donor[rows:, :8].astype(jnp.int32)
        acc = call(
            lambda *refs, distance=distance: pair_kernel(distance, *refs),
            [shape((rows, heads), F32), shape((rows, heads), F32), shape((PANEL, PANEL), F32)],
            1_000_000_000,
            4_000_000,
            [SM] * 2 + [VM] * 7,
        )(meta, far_meta, donor_feat, accept_feat, far_donor, far_accept, *acc)

    chunk = CHUNK_ROWS + EXTRA_ROWS
    lanes = inner // 128
    slabs = tap_count * lanes
    conv_sum, head_sum = call(
        backward_kernel,
        [shape((8, slabs, PIECE, 128), BF16), shape((16, chunk, 128), BF16)],
        5_000_000_000,
        12_000_000,
        [VM] * 12,
        [pltpu.VMEM((rows, inner), BF16), pltpu.VMEM((rows, 2 * heads), BF16)],
    )(
        *acc, dilated_tap_weight, point_weight, donor_weight, acceptor_weight,
        factor, slope, hidden_t, act_t, embed_t,
    )

    conv_sum = summed(swap_parts(conv_sum.reshape(2, 4, slabs, PIECE, 128), "core")).astype(BF16)
    conv_sum = summed(swap_parts(conv_sum, "x")).astype(BF16)
    conv_sum = conv_sum.reshape(slabs, 4, 24, 128).transpose(1, 0, 2, 3).reshape(4, slabs * 24, 128)
    head_rows = 4 * chunk
    both = jnp.concatenate([head_sum.reshape(4, head_rows, 128), conv_sum], axis=1)
    both = summed(swap_parts(both, "y"))
    head_sum = resplit(both[:head_rows].reshape(4, chunk, 128))
    conv_sum = both[head_rows:].astype(BF16)
    conv_sum = conv_sum.reshape(slabs, 4, 6, 128).transpose(1, 0, 2, 3).reshape(4, slabs * 6, 128)
    both = jnp.concatenate([head_sum, conv_sum], axis=1)
    both = summed(swap_parts(both, "zq"))
    both = jnp.concatenate([resplit(both[:chunk]), both[chunk:].astype(BF16)], axis=0)
    other = lax.ppermute(both, "zb", [(0, 1), (1, 0)])
    both = both.astype(F32) + other.astype(F32)
    head_sum = resplit(both[:chunk])
    conv_sum = both[chunk:].astype(BF16).reshape(slabs, 2, 3, 128)
    conv_sum = lax.dynamic_index_in_dim(conv_sum, lax.axis_index("zb"), 1, keepdims=False)
    pieces = gather_parts(conv_sum, BATCH).astype(F32)
    pieces = jnp.sum(pieces.reshape(2, 4, 2, tap_count, lanes, 3, 128), axis=0)
    grad_conv = pieces.transpose(2, 1, 0, 4, 3, 5).reshape(tap_count, 24, inner)

    head_sum = gather_parts(head_sum, "zq").reshape(4 * chunk, 128)
    head_sum = gather_parts(head_sum, "y").reshape(16, chunk, 128)
    body = head_sum[:, :CHUNK_ROWS].reshape(16 * CHUNK_ROWS, 128)
    extra = head_sum[:, CHUNK_ROWS].astype(F32) + head_sum[:, CHUNK_ROWS + 8].astype(F32)
    gain_chunks = channels // 128

    def heads_of(start, count):
        return jnp.concatenate([body[start : start + count], body[start + count : start + 2 * count]], axis=1)

    grad_donor = heads_of(0, channels)
    grad_accept = heads_of(2 * channels, channels)
    act_donor = heads_of(4 * channels, inner)
    act_accept = heads_of(4 * channels + 2 * inner, inner)
    grad_point = (dot_t(act_donor, donor_weight) + dot_t(act_accept, acceptor_weight)).astype(BF16)
    grad_gain = extra[:gain_chunks].reshape(1, channels)
    loss = extra[gain_chunks, :1]
    return grad_conv, grad_point[None], grad_donor[None], grad_accept[None], grad_gain, loss


def channel_order():
    core, x, y, zq, zb, k = np.meshgrid(*[np.arange(n) for n in (2, 4, 4, 4, 2, 3)], indexing="ij")
    channel = (24 * (8 * y + 4 * zb + zq) + 12 * core + 3 * x + k).reshape(-1)
    return np.eye(channel.size, dtype=np.float32)[channel]


def solution(mesh):
    fine = Mesh(mesh.devices.reshape(4, 2, 4, 2, 4, 2), SEQ + BATCH)
    placed = jax.shard_map(
        on_device,
        mesh=fine,
        in_specs=(
            P(BATCH, SEQ, None),
            P(),
            P(),
            P(),
            P(),
            P(),
            P(BATCH, SEQ, None),
            P(BATCH, SEQ),
            P(),
            P(),
        ),
        out_specs=(
            P(None, SEQ, None),
            P(BATCH, None, None),
            P(BATCH, None, None),
            P(BATCH, None, None),
            P(BATCH, None),
            P(BATCH),
        ),
        check_vma=False,
    )

    def run(*arrays):
        order = jnp.asarray(channel_order(), BF16)
        eye = jnp.eye(order.shape[0], dtype=BF16)
        return placed(*arrays, order, eye)

    return run
```

```python
import jax
import jax.numpy as jnp
import numpy as np
from jax import lax
from jax.experimental import pallas as pl
from jax.experimental.pallas import tpu as pltpu
from jax.sharding import Mesh
from jax.sharding import PartitionSpec as P

STEP = 128
PANEL = 128
SPAN = 4
SLOTS = 16
EPSILON = 1e-06
LOSS_WEIGHT = 1.0 / 128.0
SEQ = ("y", "zb", "zq")
BATCH = ("zhi", "x", "core")
F32 = jnp.float32
BF16 = jnp.bfloat16
ROOT = 0.7978845608028654
CUBIC = 0.044715
PIECE = 96
CHUNK_ROWS = 288
EXTRA_ROWS = 16


def dot(a, b):
    return lax.dot_general(a, b, (((1,), (0,)), ((), ())), preferred_element_type=F32)


def dot_t(a, b):
    return lax.dot_general(a, b, (((1,), (1,)), ((), ())), preferred_element_type=F32)


def gelu(v):
    return 0.5 * v * (1.0 + jnp.tanh(ROOT * (v + CUBIC * (v * v * v))))


def gelu_both(v):
    square = v * v
    t = jnp.tanh(ROOT * (v + CUBIC * (square * v)))
    half = 0.5 * (1.0 + t)
    return v * half, half + 0.5 * v * (1.0 - t * t) * (ROOT * (1.0 + 3.0 * CUBIC * square))


def rms(v):
    return lax.rsqrt(jnp.mean(v * v, axis=-1, keepdims=True) + EPSILON)


def call(kernel, outs, specs, megabytes, flops, scratch=()):
    return pl.pallas_call(
        kernel,
        out_shape=outs,
        in_specs=specs,
        out_specs=[VM] * len(outs),
        scratch_shapes=list(scratch),
        compiler_params=pltpu.CompilerParams(vmem_limit_bytes=megabytes * 1024 * 1024),
        cost_estimate=pl.CostEstimate(flops=flops, bytes_accessed=1_000_000, transcendentals=0),
    )


VM = pl.BlockSpec(memory_space=pltpu.VMEM)
SM = pl.BlockSpec(memory_space=pltpu.SMEM)


def own_kernel(tok, gain, hidden, factor):
    @pl.loop(0, tok.shape[0] // STEP)
    def _(i):
        here = pl.ds(pl.multiple_of(i * STEP, STEP), STEP)
        v = tok[here, :].astype(F32)
        unit = v * rms(v)
        value, slope = gelu_both(unit * gain[...])
        hidden[here, :] = value.astype(BF16)
        factor[here, :] = (slope * unit).astype(BF16)


def forward_kernel(
    odd, tok, mine, even_edge, odd_edge, gain, taps, point, donor_w, accept_w, meta,
    hidden, conv_out, act_out, embed_out, even_feat, odd_feat,
):
    rows = tok.shape[0]
    is_odd = odd[0] > 0
    low = jnp.where(is_odd, even_edge[...], odd_edge[...])
    high = jnp.where(is_odd, odd_edge[...], even_edge[...])
    for edge, at in ((low, 0), (high, STEP + rows)):
        v = edge.astype(F32)
        hidden[pl.ds(at, STEP), :] = gelu(v * rms(v) * gain[...]).astype(BF16)
    hidden[pl.ds(STEP, rows), :] = mine[...]

    @pl.loop(0, rows // 256)
    def _(i):
        start = pl.multiple_of(i * 256, 256)
        here = pl.ds(start, 256)
        conv = dot(hidden[here, :], taps[0])
        for tap in range(1, taps.shape[0]):
            at = pl.multiple_of(start + tap * STEP, STEP)
            conv = conv + dot(hidden[pl.ds(at, 256), :], taps[tap])
        conv_out[here, :] = conv
        act = gelu(conv).astype(BF16)
        act_out[here, :] = act
        embed = (tok[here, :].astype(F32) + dot(act, point[...])).astype(BF16)
        embed_out[here, :] = embed
        donor = dot(embed, donor_w[...]).astype(BF16)
        accept = dot(embed, accept_w[...]).astype(BF16)
        even_feat[here, :] = jnp.where(is_odd, accept, donor)
        odd_feat[here, :] = jnp.where(is_odd, donor, accept)

    even_feat[pl.ds(rows, SLOTS), :] = meta[...]
    odd_feat[pl.ds(rows, SLOTS), :] = meta[...]


def side_kernel(
    odd, even_edge, odd_edge, gain, hidden, conv, act, embed, order, eye,
    factor, slope, hidden_t, act_t, embed_t,
):
    is_odd = odd[0] > 0
    low = jnp.where(is_odd, even_edge[...], odd_edge[...])
    high = jnp.where(is_odd, odd_edge[...], even_edge[...])
    for edge, at in ((low, 0), (high, STEP)):
        v = edge.astype(F32)
        unit = v * rms(v)
        factor[pl.ds(at, STEP), :] = (gelu_both(unit * gain[...])[1] * unit).astype(BF16)

    @pl.loop(0, conv.shape[0] // STEP)
    def _(i):
        here = pl.ds(pl.multiple_of(i * STEP, STEP), STEP)
        slope[here, :] = gelu_both(conv[here, :])[1]

    @pl.loop(0, hidden_t.shape[0] // 256)
    def _(i):
        here = pl.ds(pl.multiple_of(i * 256, 256), 256)
        hidden_t[here, :] = dot_t(order[here, :], hidden[...]).astype(BF16)
        embed_t[here, :] = dot_t(eye[here, :], embed[...]).astype(BF16)

    inner = act.shape[1]

    @pl.loop(0, inner // 128)
    def _(i):
        here = pl.ds(pl.multiple_of(i * 128, 128), 128)
        act_t[here, :] = dot_t(eye[here, :inner], act[...]).astype(BF16)


def pair_kernel(distance, *refs):
    if distance == 0:
        odd, own, even0, odd0, d_donor, d_accept, loss = refs
        d_donor[...] = jnp.zeros_like(d_donor)
        d_accept[...] = jnp.zeros_like(d_accept)
        loss[...] = jnp.zeros_like(loss)
    else:
        odd, own, far, even0, odd0, even1, odd1, dd_in, da_in, loss_in, d_donor, d_accept, loss = refs
        d_donor[...] = dd_in[...]
        d_accept[...] = da_in[...]
        loss[...] = loss_in[...]
    is_odd = odd[0] > 0
    scale = even0.shape[1] ** (-0.5)
    per_device = d_donor.shape[0] // PANEL
    row = lax.broadcasted_iota(jnp.int32, (PANEL, PANEL), 0)
    col = lax.broadcasted_iota(jnp.int32, (PANEL, PANEL), 1)

    def place(block):
        return pl.ds(pl.multiple_of(block * PANEL, PANEL), PANEL)

    def own_donor(block):
        return jnp.where(is_odd, odd0[place(block), :], even0[place(block), :])

    def own_accept(block):
        return jnp.where(is_odd, even0[place(block), :], odd0[place(block), :])

    if distance == 0:
        far_accept, far_donor = own_accept, None
    else:

        def far_accept(block):
            return jnp.where(is_odd, odd1[place(block), :], even1[place(block), :])

        def far_donor(block):
            return jnp.where(is_odd, even1[place(block), :], odd1[place(block), :])

    def visit(meta, j, donors, acceptors, is_owner):
        accept_block = meta[j, 2] - distance * per_device
        here = (meta[j, 4] > 0) & (accept_block >= 0) & (accept_block < per_device)

        @pl.when(here)
        def _():
            donor_block = meta[j, 0]
            dpan = donors(donor_block)
            apan = acceptors(accept_block)
            scores = dot_t(dpan, apan) * scale
            target = ((row == meta[j, 1]) & (col == meta[j, 3])).astype(F32)
            small = jnp.exp(-jnp.abs(scores))
            inverse = 1.0 / (1.0 + small)
            sigmoid = jnp.where(scores >= 0, inverse, small * inverse)
            dscore = ((sigmoid - target) * LOSS_WEIGHT).astype(BF16)
            if is_owner:
                loss[...] += (jnp.maximum(scores, 0.0) + jnp.log1p(small)) - target * scores
                d_donor[place(donor_block), :] += dot(dscore, apan) * scale
            if distance == 0 or not is_owner:
                d_accept[place(accept_block), :] += scale * lax.dot_general(
                    dscore, dpan, (((0,), (0,)), ((), ())), preferred_element_type=F32
                )

    @pl.loop(0, SLOTS)
    def _(j):
        visit(own, j, own_donor, far_accept, True)
        if distance > 0:
            visit(far, j, far_donor, own_accept, False)


def tap_grad_kernel(
    core, d_donor, d_accept, point, donor_w, accept_w, slope, hidden_t,
    keep, send, d_conv, d_feat,
):
    rows, heads = d_donor.shape
    channels = hidden_t.shape[0]

    @pl.loop(0, rows // 256)
    def _(i):
        here = pl.ds(pl.multiple_of(i * 256, 256), 256)
        dd = d_donor[here, :].astype(BF16)
        da = d_accept[here, :].astype(BF16)
        d_feat[here, :heads] = dd
        d_feat[here, heads:] = da
        d_embed = (dot_t(dd, donor_w[...]) + dot_t(da, accept_w[...])).astype(BF16)
        d_conv[here, :] = (dot_t(d_embed, point[...]) * slope[here, :]).astype(BF16)

    lanes = d_conv.shape[1] // 128
    half_rows = channels // 2
    for tap in range(3):
        for half in range(2):
            into_keep = core[0] == half

            @pl.loop(0, half_rows // (2 * PIECE))
            def _(i):
                at = pl.multiple_of(half * half_rows + i * 2 * PIECE, 2 * PIECE)
                part = dot(
                    hidden_t[pl.ds(at, 2 * PIECE), tap * STEP : tap * STEP + rows], d_conv[...]
                ).astype(BF16)

                def store(into):
                    for k in range(2):
                        for lane in range(lanes):
                            into[i * 2 + k, tap * lanes + lane] = part[
                                k * PIECE : (k + 1) * PIECE, lane * 128 : (lane + 1) * 128
                            ]

                pl.when(into_keep)(lambda: store(keep))
                pl.when(jnp.logical_not(into_keep))(lambda: store(send))


def head_grad_kernel(
    d_conv, d_feat, loss, taps, factor, edge_factor, act_t, embed_t, head_sum,
):
    rows = d_conv.shape[0]
    channels = embed_t.shape[0]
    inner = act_t.shape[0]

    def put(part, base, group_rows, first):
        for lane in range(4):
            for k in range(part.shape[0] // PIECE):
                piece = first + lane * (group_rows // PIECE) + k + base
                chunk, place = piece // 3, piece % 3
                head_sum[chunk, place * PIECE : (place + 1) * PIECE, :] = part[
                    k * PIECE : (k + 1) * PIECE, lane * 128 : (lane + 1) * 128
                ]

    for i in range(channels // (2 * PIECE)):
        part = dot(embed_t[i * 2 * PIECE : (i + 1) * 2 * PIECE, :], d_feat[...]).astype(BF16)
        put(part, 2 * i, channels, 0)
    for i in range(inner // (2 * PIECE)):
        part = dot(act_t[i * 2 * PIECE : (i + 1) * 2 * PIECE, :], d_feat[...]).astype(BF16)
        put(part, 2 * i, inner, 4 * channels // PIECE)

    total = jnp.zeros((8, channels), F32)
    last = taps.shape[0] - 1
    blocks = rows // STEP

    def weighed(block, tap, weights):
        product = dot_t(d_conv[block * STEP : (block + 1) * STEP, :], taps[tap]) * weights.astype(F32)
        return jnp.sum(product.reshape(STEP // 8, 8, channels), axis=0)

    for block in range(blocks):
        for tap in range(taps.shape[0]):
            at = block + tap - 1
            if at < 0:
                weights = edge_factor[:STEP, :]
            elif at >= blocks:
                weights = edge_factor[STEP:, :]
            else:
                weights = factor[at * STEP : (at + 1) * STEP, :]
            total = total + weighed(block, tap, weights)
    gain = jnp.sum(total, axis=0, keepdims=True)
    loss_row = jnp.sum(loss[...], axis=0, keepdims=True) * LOSS_WEIGHT
    loss_all = jnp.broadcast_to(jnp.sum(loss_row, axis=1, keepdims=True), (1, 128))
    at_row = lax.broadcasted_iota(jnp.int32, (EXTRA_ROWS, 128), 0)
    for chunk in range(head_sum.shape[0]):
        if chunk < channels // 128:
            value = gain[:, chunk * 128 : (chunk + 1) * 128]
        elif chunk == channels // 128:
            value = loss_all
        else:
            value = jnp.zeros((1, 128), F32)
        coarse = value.astype(BF16).astype(F32)
        block = jnp.where(at_row == 0, coarse, 0.0) + jnp.where(at_row == 8, value - coarse, 0.0)
        head_sum[chunk, CHUNK_ROWS:, :] = block.astype(BF16)


def finish_kernel(
    place_y, own, one, two, three, donor_w, accept_w,
    grad_donor, grad_accept, grad_point, gain, loss, held, act_donor, act_accept,
):
    count = held.shape[0]
    for back, part in enumerate((own, one, two, three)):
        held[lax.rem(place_y[0] + count - back, count)] = part[...]
    channels = grad_donor.shape[0]
    inner = act_donor.shape[0]
    chunk_rows = CHUNK_ROWS + EXTRA_ROWS
    piece = 0
    for into in (grad_donor, grad_accept, act_donor, act_accept):
        for lane in range(2):
            for k in range(into.shape[0] // PIECE):
                chunk, place = piece // 3, piece % 3
                at = (chunk % 4) * chunk_rows + place * PIECE
                into[k * PIECE : (k + 1) * PIECE, lane * 128 : (lane + 1) * 128] = held[
                    chunk // 4, at : at + PIECE, :
                ]
                piece += 1

    @pl.loop(0, inner // 128)
    def _(i):
        here = pl.ds(pl.multiple_of(i * 128, 128), 128)
        grad_point[here, :] = (
            dot_t(act_donor[here, :], donor_w[...]) + dot_t(act_accept[here, :], accept_w[...])
        ).astype(BF16)

    for chunk in range(channels // 128 + 1):
        at = (chunk % 4) * chunk_rows + CHUNK_ROWS
        block = held[chunk // 4, at : at + EXTRA_ROWS, :].astype(F32)
        value = block[0:1, :] + block[8:9, :]
        if chunk < channels // 128:
            gain[:, chunk * 128 : (chunk + 1) * 128] = value
        else:
            loss[...] = value


def swapped(block, first):
    count = lax.axis_size(SEQ)
    pairs = [(i, i + 1) for i in range(first, count - 1, 2)]
    return lax.ppermute(block, SEQ, pairs + [(j, i) for i, j in pairs])


def swap_parts(parts, axis):
    return lax.all_to_all(parts, axis, 0, 0, tiled=True)


def gather_parts(part, axis):
    count = lax.axis_size(axis)
    return swap_parts(jnp.broadcast_to(part[None], (count,) + part.shape), axis)


def summed(parts):
    return jnp.sum(parts.astype(F32), axis=0)


def resplit(total):
    body = total[..., :CHUNK_ROWS, :].astype(BF16)
    value = (
        total[..., CHUNK_ROWS : CHUNK_ROWS + 8, :] + total[..., CHUNK_ROWS + 8 : CHUNK_ROWS + 16, :]
    )
    coarse = lax.reduce_precision(value, 8, 7)
    return jnp.concatenate([body, coarse.astype(BF16), (value - coarse).astype(BF16)], axis=-2)


def on_device(
    activations, norm_gain, dilated_tap_weight, point_weight, donor_weight, acceptor_weight,
    pair_sites, pair_count, order, eye,
):
    tokens = activations[0]
    rows, channels = tokens.shape
    tap_count, _, inner = dilated_tap_weight.shape
    heads = donor_weight.shape[1]
    blocks = rows // PANEL
    shape = jax.ShapeDtypeStruct
    here = lax.axis_index(SEQ)
    odd = (here % 2).astype(jnp.int32)[None]
    is_odd = odd[0] > 0
    start, end = tokens[:STEP], tokens[rows - STEP :]
    even_edge = swapped(jnp.where(is_odd, start, end), 0)
    odd_edge = swapped(jnp.where(is_odd, end, start), 1)
    gain = norm_gain[None]
    sites = pair_sites[0]
    first = here * blocks
    live = (jnp.arange(SLOTS, dtype=jnp.int32) < pair_count[0, 0]).astype(jnp.int32)
    meta = jnp.stack(
        [
            sites[:, 0] // PANEL - first,
            sites[:, 0] % PANEL,
            sites[:, 1] // PANEL - first,
            sites[:, 1] % PANEL,
            live,
        ]
        + [jnp.zeros_like(live)] * 3,
        axis=1,
    )
    meta_rows = jnp.pad(meta.astype(BF16), ((0, 0), (0, heads - meta.shape[1])))

    mine, factor = call(
        own_kernel, [shape((rows, channels), BF16)] * 2, [VM] * 2, 12, 2_000_000_000
    )(tokens, gain)
    feat = shape((rows + SLOTS, heads), BF16)
    hidden, conv, act, embed, even_feat, odd_feat = call(
        forward_kernel,
        [
            shape((rows + 2 * STEP, channels), BF16),
            shape((rows, inner), F32),
            shape((rows, inner), BF16),
            shape((rows, channels), BF16),
            feat,
            feat,
        ],
        [SM] + [VM] * 10,
        20,
        4_000_000_000,
    )(
        odd, tokens, mine, even_edge, odd_edge, gain, dilated_tap_weight, point_weight,
        donor_weight, acceptor_weight, meta_rows,
    )

    acc_shapes = [shape((rows, heads), F32), shape((rows, heads), F32), shape((PANEL, PANEL), F32)]
    acc = call(
        lambda *refs: pair_kernel(0, *refs), acc_shapes, [SM] * 2 + [VM] * 2, 12, 2_000_000_000
    )(odd, meta, even_feat, odd_feat)
    edge_factor, slope, hidden_t, act_t, embed_t = call(
        side_kernel,
        [
            shape((2 * STEP, channels), BF16),
            shape((rows, inner), F32),
            shape((channels, rows + 2 * STEP), BF16),
            shape((inner, rows), BF16),
            shape((channels, rows), BF16),
        ],
        [SM] + [VM] * 9,
        20,
        6_000_000_000,
    )(odd, even_edge, odd_edge, gain, hidden, conv, act, embed, order, eye)
    even_far, odd_far = even_feat, odd_feat
    for distance in range(1, SPAN + 1):
        if distance == 1:
            even_far, odd_far = swapped(even_feat, 0), swapped(odd_feat, 1)
        else:
            even_far, odd_far = swapped(odd_far, 0), swapped(even_far, 1)
        far_meta = jnp.where(is_odd, even_far[rows:, :8], odd_far[rows:, :8]).astype(jnp.int32)
        acc = call(
            lambda *refs, distance=distance: pair_kernel(distance, *refs),
            acc_shapes,
            [SM] * 3 + [VM] * 7,
            12,
            2_500_000_000,
        )(odd, meta, far_meta, even_feat, odd_feat, even_far, odd_far, *acc)

    chunk = CHUNK_ROWS + EXTRA_ROWS
    lanes = inner // 128
    slabs = tap_count * lanes
    half = shape((4, slabs, PIECE, 128), BF16)
    keep, send, d_conv, d_feat = call(
        tap_grad_kernel,
        [half, half, shape((rows, inner), BF16), shape((rows, 2 * heads), BF16)],
        [SM] + [VM] * 7,
        20,
        4_000_000_000,
    )(
        lax.axis_index("core").astype(jnp.int32)[None], acc[0], acc[1], point_weight, donor_weight,
        acceptor_weight, slope, hidden_t,
    )
    received = lax.ppermute(send, "core", [(0, 1), (1, 0)])
    (head_sum,) = call(
        head_grad_kernel, [shape((16, chunk, 128), BF16)], [VM] * 8, 20, 4_000_000_000
    )(d_conv, d_feat, acc[2], dilated_tap_weight, factor, edge_factor, act_t, embed_t)

    conv_sum = (keep.astype(F32) + received.astype(F32)).astype(BF16)
    head_rows = 4 * chunk
    both = jnp.concatenate(
        [head_sum.reshape(4, head_rows, 128), conv_sum.reshape(4, slabs * PIECE, 128)], axis=1
    )
    both = summed(swap_parts(both, "y"))
    head_sum = resplit(both[:head_rows].reshape(4, chunk, 128))
    conv_sum = both[head_rows:].astype(BF16)
    conv_sum = conv_sum.reshape(slabs, 4, 24, 128).transpose(1, 0, 2, 3).reshape(4, slabs * 24, 128)
    both = jnp.concatenate([head_sum, conv_sum], axis=1)
    both = summed(swap_parts(both, "zq"))
    both = jnp.concatenate([resplit(both[:chunk]), both[chunk:].astype(BF16)], axis=0)
    other = lax.ppermute(both, "zb", [(0, 1), (1, 0)])
    both = both.astype(F32) + other.astype(F32)
    head_sum = resplit(both[:chunk])
    conv_sum = both[chunk:].astype(BF16).reshape(slabs, 2, 12, 128)
    conv_sum = lax.dynamic_index_in_dim(conv_sum, lax.axis_index("zb"), 1, keepdims=False)
    other = lax.ppermute(conv_sum, "zhi", [(0, 1), (1, 0)])

    head_sum = gather_parts(head_sum, "zq").reshape(head_rows, 128)
    ring = [
        lax.ppermute(head_sum, "y", [(i, (i + ahead) % 4) for i in range(4)]) for ahead in (1, 2, 3)
    ]
    conv_sum = (conv_sum.astype(F32) + other.astype(F32)).astype(BF16)
    pieces = gather_parts(conv_sum, ("x", "core")).astype(F32)
    pieces = jnp.sum(pieces.reshape(4, 2, tap_count, lanes, 12, 128), axis=0)
    grad_conv = pieces.transpose(1, 0, 3, 2, 4).reshape(tap_count, 24, inner)
    head_weight = shape((channels, heads), BF16)
    grad_donor, grad_accept, grad_point, grad_gain, loss = call(
        finish_kernel,
        [head_weight, head_weight, shape((inner, channels), BF16), shape((1, channels), F32), shape((1, 128), F32)],
        [SM] + [VM] * 6,
        16,
        1_000_000_000,
        [
            pltpu.VMEM((4, head_rows, 128), BF16),
            pltpu.VMEM((inner, heads), BF16),
            pltpu.VMEM((inner, heads), BF16),
        ],
    )(lax.axis_index("y").astype(jnp.int32)[None], head_sum, *ring, donor_weight, acceptor_weight)
    return grad_conv, grad_point[None], grad_donor[None], grad_accept[None], grad_gain, loss[0, :1]


def channel_order():
    core, y, zq, zb, k = np.meshgrid(*[np.arange(n) for n in (2, 4, 4, 2, 12)], indexing="ij")
    channel = (24 * (8 * y + 4 * zb + zq) + 12 * core + k).reshape(-1)
    return np.eye(channel.size, dtype=np.float32)[channel]


def solution(mesh):
    fine = Mesh(mesh.devices.reshape(4, 2, 4, 2, 4, 2), SEQ + BATCH)
    placed = jax.shard_map(
        on_device,
        mesh=fine,
        in_specs=(
            P(BATCH, SEQ, None),
            P(),
            P(),
            P(),
            P(),
            P(),
            P(BATCH, SEQ, None),
            P(BATCH, SEQ),
            P(),
            P(),
        ),
        out_specs=(
            P(None, SEQ, None),
            P(BATCH, None, None),
            P(BATCH, None, None),
            P(BATCH, None, None),
            P(BATCH, None),
            P(BATCH),
        ),
        check_vma=False,
    )

    def run(*arrays):
        order = jnp.asarray(channel_order(), BF16)
        eye = jnp.eye(order.shape[0], dtype=BF16)
        return placed(*arrays, order, eye)

    return run
```

```python
import jax
import jax.numpy as jnp
import numpy as np
from jax import lax
from jax.experimental import pallas as pl
from jax.experimental.pallas import tpu as pltpu
from jax.sharding import Mesh
from jax.sharding import PartitionSpec as P

STEP = 128
PANEL = 128
SPAN = 4
SLOTS = 16
EPSILON = 1e-06
LOSS_WEIGHT = 1.0 / 128.0
SEQ = ("y", "zb", "zq")
BATCH = ("zhi", "x", "core")
F32 = jnp.float32
BF16 = jnp.bfloat16
ROOT = 0.7978845608028654
CUBIC = 0.044715
PIECE = 96
CHUNK_ROWS = 288
EXTRA_ROWS = 16


def dot(a, b):
    return lax.dot_general(a, b, (((1,), (0,)), ((), ())), preferred_element_type=F32)


def dot_t(a, b):
    return lax.dot_general(a, b, (((1,), (1,)), ((), ())), preferred_element_type=F32)


def gelu(v):
    return 0.5 * v * (1.0 + jnp.tanh(ROOT * (v + CUBIC * (v * v * v))))


def gelu_both(v):
    square = v * v
    t = jnp.tanh(ROOT * (v + CUBIC * (square * v)))
    half = 0.5 * (1.0 + t)
    return v * half, half + 0.5 * v * (1.0 - t * t) * (ROOT * (1.0 + 3.0 * CUBIC * square))


def rms(v):
    return lax.rsqrt(jnp.mean(v * v, axis=-1, keepdims=True) + EPSILON)


def call(kernel, outs, specs, megabytes, flops, scratch=()):
    return pl.pallas_call(
        kernel,
        out_shape=outs,
        in_specs=specs,
        out_specs=[VM] * len(outs),
        scratch_shapes=list(scratch),
        compiler_params=pltpu.CompilerParams(vmem_limit_bytes=megabytes * 1024 * 1024),
        cost_estimate=pl.CostEstimate(flops=flops, bytes_accessed=1_000_000, transcendentals=0),
    )


VM = pl.BlockSpec(memory_space=pltpu.VMEM)
SM = pl.BlockSpec(memory_space=pltpu.SMEM)


def own_kernel(tok, gain, hidden, factor):
    @pl.loop(0, tok.shape[0] // STEP)
    def _(i):
        here = pl.ds(pl.multiple_of(i * STEP, STEP), STEP)
        v = tok[here, :].astype(F32)
        unit = v * rms(v)
        value, slope = gelu_both(unit * gain[...])
        hidden[here, :] = value.astype(BF16)
        factor[here, :] = (slope * unit).astype(BF16)


def forward_kernel(
    odd, tok, mine, even_edge, odd_edge, gain, taps, point, donor_w, accept_w, meta,
    hidden, conv_out, act_out, embed_out, even_feat, odd_feat,
):
    rows = tok.shape[0]
    is_odd = odd[0] > 0
    low = jnp.where(is_odd, even_edge[...], odd_edge[...])
    high = jnp.where(is_odd, odd_edge[...], even_edge[...])
    for edge, at in ((low, 0), (high, STEP + rows)):
        v = edge.astype(F32)
        hidden[pl.ds(at, STEP), :] = gelu(v * rms(v) * gain[...]).astype(BF16)
    hidden[pl.ds(STEP, rows), :] = mine[...]

    @pl.loop(0, rows // 256)
    def _(i):
        start = pl.multiple_of(i * 256, 256)
        here = pl.ds(start, 256)
        conv = dot(hidden[here, :], taps[0])
        for tap in range(1, taps.shape[0]):
            at = pl.multiple_of(start + tap * STEP, STEP)
            conv = conv + dot(hidden[pl.ds(at, 256), :], taps[tap])
        conv_out[here, :] = conv
        act = gelu(conv).astype(BF16)
        act_out[here, :] = act
        embed = (tok[here, :].astype(F32) + dot(act, point[...])).astype(BF16)
        embed_out[here, :] = embed
        donor = dot(embed, donor_w[...]).astype(BF16)
        accept = dot(embed, accept_w[...]).astype(BF16)
        even_feat[here, :] = jnp.where(is_odd, donor, accept)
        odd_feat[here, :] = jnp.where(is_odd, accept, donor)

    even_feat[pl.ds(rows, SLOTS), :] = meta[...]
    odd_feat[pl.ds(rows, SLOTS), :] = meta[...]


def side_kernel(
    odd, even_edge, odd_edge, gain, hidden, conv, act, embed, order, eye,
    factor, slope, hidden_t, act_t, embed_t,
):
    is_odd = odd[0] > 0
    low = jnp.where(is_odd, even_edge[...], odd_edge[...])
    high = jnp.where(is_odd, odd_edge[...], even_edge[...])
    for edge, at in ((low, 0), (high, STEP)):
        v = edge.astype(F32)
        unit = v * rms(v)
        factor[pl.ds(at, STEP), :] = (gelu_both(unit * gain[...])[1] * unit).astype(BF16)

    @pl.loop(0, conv.shape[0] // STEP)
    def _(i):
        here = pl.ds(pl.multiple_of(i * STEP, STEP), STEP)
        slope[here, :] = gelu_both(conv[here, :])[1]

    @pl.loop(0, hidden_t.shape[0] // 256)
    def _(i):
        here = pl.ds(pl.multiple_of(i * 256, 256), 256)
        hidden_t[here, :] = dot_t(order[here, :], hidden[...]).astype(BF16)
        embed_t[here, :] = dot_t(eye[here, :], embed[...]).astype(BF16)

    inner = act.shape[1]

    @pl.loop(0, inner // 128)
    def _(i):
        here = pl.ds(pl.multiple_of(i * 128, 128), 128)
        act_t[here, :] = dot_t(eye[here, :inner], act[...]).astype(BF16)


def pair_kernel(distance, *refs):
    if distance == 1:
        odd, own, far, even0, odd0, even1, odd1, d_donor, d_accept, loss = refs
        d_donor[...] = jnp.zeros_like(d_donor)
        d_accept[...] = jnp.zeros_like(d_accept)
        loss[...] = jnp.zeros_like(loss)
    else:
        odd, own, far, even0, odd0, even1, odd1, dd_in, da_in, loss_in, d_donor, d_accept, loss = refs
        d_donor[...] = dd_in[...]
        d_accept[...] = da_in[...]
        loss[...] = loss_in[...]
    is_odd = odd[0] > 0
    scale = even0.shape[1] ** (-0.5)
    per_device = d_donor.shape[0] // PANEL
    row = lax.broadcasted_iota(jnp.int32, (PANEL, PANEL), 0)
    col = lax.broadcasted_iota(jnp.int32, (PANEL, PANEL), 1)

    def place(block):
        return pl.ds(pl.multiple_of(block * PANEL, PANEL), PANEL)

    def own_donor(block):
        return jnp.where(is_odd, odd0[place(block), :], even0[place(block), :])

    def own_accept(block):
        return jnp.where(is_odd, even0[place(block), :], odd0[place(block), :])

    def far_accept(block):
        return jnp.where(is_odd, odd1[place(block), :], even1[place(block), :])

    def far_donor(block):
        return jnp.where(is_odd, even1[place(block), :], odd1[place(block), :])

    def visit(meta, j, donors, acceptors, distance, is_owner):
        accept_block = meta[j, 2] - distance * per_device
        here = (meta[j, 4] > 0) & (accept_block >= 0) & (accept_block < per_device)

        @pl.when(here)
        def _():
            donor_block = meta[j, 0]
            dpan = donors(donor_block)
            apan = acceptors(accept_block)
            scores = dot_t(dpan, apan) * scale
            target = ((row == meta[j, 1]) & (col == meta[j, 3])).astype(F32)
            small = jnp.exp(-jnp.abs(scores))
            inverse = 1.0 / (1.0 + small)
            sigmoid = jnp.where(scores >= 0, inverse, small * inverse)
            dscore = ((sigmoid - target) * LOSS_WEIGHT).astype(BF16)
            if is_owner:
                loss[...] += (jnp.maximum(scores, 0.0) + jnp.log1p(small)) - target * scores
                d_donor[place(donor_block), :] += dot(dscore, apan) * scale
            if distance == 0 or not is_owner:
                d_accept[place(accept_block), :] += scale * lax.dot_general(
                    dscore, dpan, (((0,), (0,)), ((), ())), preferred_element_type=F32
                )

    @pl.loop(0, SLOTS)
    def _(j):
        if distance == 1:
            visit(own, j, own_donor, own_accept, 0, True)
        visit(own, j, own_donor, far_accept, distance, True)
        visit(far, j, far_donor, own_accept, distance, False)


def relative(target, y, first):
    code = (target ^ (target >> 1)) ^ (y ^ (y >> 1))
    low, high = code & 1, code >> 1
    return low * 2 + high if first == 0 else high * 2 + low


def tap_grad_kernel(
    place, d_donor, d_accept, point, donor_w, accept_w, slope, hidden_t,
    keep, send, d_conv, d_feat,
):
    rows, heads = d_donor.shape
    channels = hidden_t.shape[0]

    @pl.loop(0, rows // 256)
    def _(i):
        here = pl.ds(pl.multiple_of(i * 256, 256), 256)
        dd = d_donor[here, :].astype(BF16)
        da = d_accept[here, :].astype(BF16)
        d_feat[here, :heads] = dd
        d_feat[here, heads:] = da
        d_embed = (dot_t(dd, donor_w[...]) + dot_t(da, accept_w[...])).astype(BF16)
        d_conv[here, :] = (dot_t(d_embed, point[...]) * slope[here, :]).astype(BF16)

    lanes = d_conv.shape[1] // 128
    half_rows = channels // 2
    for tap in range(3):
        for half in range(2):
            into_keep = place[0] == half

            @pl.loop(0, half_rows // (2 * PIECE))
            def _(i):
                at = pl.multiple_of(half * half_rows + i * 2 * PIECE, 2 * PIECE)
                part = dot(
                    hidden_t[pl.ds(at, 2 * PIECE), tap * STEP : tap * STEP + rows], d_conv[...]
                ).astype(BF16)

                def store(into):
                    for k in range(2):
                        for lane in range(lanes):
                            into[relative(i * 2 + k, place[1], 1), tap * lanes + lane] = part[
                                k * PIECE : (k + 1) * PIECE, lane * 128 : (lane + 1) * 128
                            ]

                pl.when(into_keep)(lambda: store(keep))
                pl.when(jnp.logical_not(into_keep))(lambda: store(send))


def head_grad_kernel(
    place, d_conv, d_feat, loss, taps, factor, edge_factor, act_t, embed_t, head_sum,
):
    rows = d_conv.shape[0]
    channels = embed_t.shape[0]
    inner = act_t.shape[0]
    slab = [relative(target, place[1], 0) for target in range(4)]

    def put(part, base, group_rows, first):
        for lane in range(4):
            for k in range(part.shape[0] // PIECE):
                piece = first + lane * (group_rows // PIECE) + k + base
                chunk, third = piece // 3, piece % 3
                head_sum[slab[chunk // 4], chunk % 4, third * PIECE : (third + 1) * PIECE, :] = part[
                    k * PIECE : (k + 1) * PIECE, lane * 128 : (lane + 1) * 128
                ]

    for i in range(channels // (2 * PIECE)):
        part = dot(embed_t[i * 2 * PIECE : (i + 1) * 2 * PIECE, :], d_feat[...]).astype(BF16)
        put(part, 2 * i, channels, 0)
    for i in range(inner // (2 * PIECE)):
        part = dot(act_t[i * 2 * PIECE : (i + 1) * 2 * PIECE, :], d_feat[...]).astype(BF16)
        put(part, 2 * i, inner, 4 * channels // PIECE)

    total = jnp.zeros((8, channels), F32)
    last = taps.shape[0] - 1
    blocks = rows // STEP

    def weighed(block, tap, weights):
        product = dot_t(d_conv[block * STEP : (block + 1) * STEP, :], taps[tap]) * weights.astype(F32)
        return jnp.sum(product.reshape(STEP // 8, 8, channels), axis=0)

    for block in range(blocks):
        for tap in range(taps.shape[0]):
            at = block + tap - 1
            if at < 0:
                weights = edge_factor[:STEP, :]
            elif at >= blocks:
                weights = edge_factor[STEP:, :]
            else:
                weights = factor[at * STEP : (at + 1) * STEP, :]
            total = total + weighed(block, tap, weights)
    gain = jnp.sum(total, axis=0, keepdims=True)
    loss_row = jnp.sum(loss[...], axis=0, keepdims=True) * LOSS_WEIGHT
    loss_all = jnp.broadcast_to(jnp.sum(loss_row, axis=1, keepdims=True), (1, 128))
    at_row = lax.broadcasted_iota(jnp.int32, (EXTRA_ROWS, 128), 0)
    for chunk in range(16):
        if chunk < channels // 128:
            value = gain[:, chunk * 128 : (chunk + 1) * 128]
        elif chunk == channels // 128:
            value = loss_all
        else:
            value = jnp.zeros((1, 128), F32)
        coarse = value.astype(BF16).astype(F32)
        block = jnp.where(at_row == 0, coarse, 0.0) + jnp.where(at_row == 8, value - coarse, 0.0)
        head_sum[slab[chunk // 4], chunk % 4, CHUNK_ROWS:, :] = block.astype(BF16)


def split_rows(total):
    value = total[CHUNK_ROWS : CHUNK_ROWS + 8] + total[CHUNK_ROWS + 8 : CHUNK_ROWS + 16]
    coarse = value.astype(BF16).astype(F32)
    return jnp.concatenate([total[:CHUNK_ROWS], coarse, value - coarse], axis=0).astype(BF16)


def core_sum_kernel(keep, received, kept, send):
    for k in range(2):
        for slab in range(keep.shape[1]):
            kept[k, slab] = keep[k, slab].astype(F32) + received[k, slab].astype(F32)
            send[k, slab] = (keep[k + 2, slab].astype(F32) + received[k + 2, slab].astype(F32)).astype(BF16)


def head_sum_kernel(head, received, kept, send):
    for zq in range(4):
        kept[zq] = head[0, zq].astype(F32) + received[0, zq].astype(F32)
        send[zq] = split_rows(head[1, zq].astype(F32) + received[1, zq].astype(F32))


def tap_sum_kernel(before, received, kept, send):
    for slab in range(before.shape[1]):
        kept[slab] = before[0, slab] + received[0, slab].astype(F32)
        send[slab] = (before[1, slab] + received[1, slab].astype(F32)).astype(BF16)


def join_kernel(head, head_in, taps, taps_in, both):
    chunk_rows = head.shape[1]
    for zq in range(4):
        both[zq, :chunk_rows, :] = split_rows(head[zq] + head_in[zq].astype(F32))
        here = slice(zq * 24, (zq + 1) * 24)
        parts = [taps[k, here] + taps_in[k, here].astype(F32) for k in range(taps.shape[0])]
        parts.append(jnp.zeros((8, 128), F32))
        both[zq, chunk_rows:, :] = jnp.concatenate(parts, axis=0).astype(BF16)


def line_sum_kernel(place, parts, pick, send, mine):
    total = parts[0].astype(F32)
    for zq in range(1, 4):
        total = total + parts[zq].astype(F32)
    chunk_rows = CHUNK_ROWS + EXTRA_ROWS
    send[:chunk_rows, :] = split_rows(total[:chunk_rows])
    taps = total[chunk_rows:].astype(BF16)
    half = mine.shape[0]
    zb = place[2]

    def picked(which):
        return dot(pick[pl.ds(pl.multiple_of(which * half, half), half), :], taps).astype(BF16)

    send[chunk_rows:, :] = picked(1 - zb)
    mine[...] = picked(zb)


def far_sum_kernel(sent, received, mine, head, taps):
    chunk_rows = CHUNK_ROWS + EXTRA_ROWS
    total = split_rows(sent[:chunk_rows, :].astype(F32) + received[:chunk_rows, :].astype(F32))
    for zq in range(head.shape[0]):
        head[zq] = total
    taps[...] = (mine[...].astype(F32) + received[chunk_rows:, :].astype(F32)).astype(BF16)


def finish_kernel(
    place, own, one, two, three, donor_w, accept_w,
    grad_donor, grad_accept, grad_point, gain, loss, held, act_donor, act_accept,
):
    count = held.shape[0]
    for back, part in enumerate((own, one, two, three)):
        held[lax.rem(place[1] + count - back, count)] = part[...]
    channels = grad_donor.shape[0]
    inner = act_donor.shape[0]
    chunk_rows = CHUNK_ROWS + EXTRA_ROWS
    piece = 0
    for into in (grad_donor, grad_accept, act_donor, act_accept):
        for lane in range(2):
            for k in range(into.shape[0] // PIECE):
                chunk, third = piece // 3, piece % 3
                at = (chunk % 4) * chunk_rows + third * PIECE
                into[k * PIECE : (k + 1) * PIECE, lane * 128 : (lane + 1) * 128] = held[
                    chunk // 4, at : at + PIECE, :
                ]
                piece += 1

    @pl.loop(0, inner // 128)
    def _(i):
        here = pl.ds(pl.multiple_of(i * 128, 128), 128)
        grad_point[here, :] = (
            dot_t(act_donor[here, :], donor_w[...]) + dot_t(act_accept[here, :], accept_w[...])
        ).astype(BF16)

    for chunk in range(channels // 128 + 1):
        at = (chunk % 4) * chunk_rows + CHUNK_ROWS
        block = held[chunk // 4, at : at + EXTRA_ROWS, :].astype(F32)
        value = block[0:1, :] + block[8:9, :]
        if chunk < channels // 128:
            gain[:, chunk * 128 : (chunk + 1) * 128] = value
        else:
            loss[...] = value


def swapped(block, first):
    count = lax.axis_size(SEQ)
    pairs = [(i, i + 1) for i in range(first, count - 1, 2)]
    return lax.ppermute(block, SEQ, pairs + [(j, i) for i, j in pairs])


def swap_parts(parts, axis):
    return lax.all_to_all(parts, axis, 0, 0, tiled=True)


def gather_parts(part, axis):
    count = lax.axis_size(axis)
    return swap_parts(jnp.broadcast_to(part[None], (count,) + part.shape), axis)


def on_device(
    activations, norm_gain, dilated_tap_weight, point_weight, donor_weight, acceptor_weight,
    pair_sites, pair_count, order, eye, pick,
):
    tokens = activations[0]
    rows, channels = tokens.shape
    tap_count, _, inner = dilated_tap_weight.shape
    heads = donor_weight.shape[1]
    blocks = rows // PANEL
    shape = jax.ShapeDtypeStruct
    here = lax.axis_index(SEQ)
    odd = (here % 2).astype(jnp.int32)[None]
    is_odd = odd[0] > 0
    start, end = tokens[:STEP], tokens[rows - STEP :]
    even_edge = swapped(jnp.where(is_odd, start, end), 0)
    odd_edge = swapped(jnp.where(is_odd, end, start), 1)
    gain = norm_gain[None]
    sites = pair_sites[0]
    first = here * blocks
    live = (jnp.arange(SLOTS, dtype=jnp.int32) < pair_count[0, 0]).astype(jnp.int32)
    meta = jnp.stack(
        [
            sites[:, 0] // PANEL - first,
            sites[:, 0] % PANEL,
            sites[:, 1] // PANEL - first,
            sites[:, 1] % PANEL,
            live,
        ]
        + [jnp.zeros_like(live)] * 3,
        axis=1,
    )
    meta_rows = jnp.pad(meta.astype(BF16), ((0, 0), (0, heads - meta.shape[1])))

    mine, factor = call(
        own_kernel, [shape((rows, channels), BF16)] * 2, [VM] * 2, 12, 2_000_000_000
    )(tokens, gain)
    feat = shape((rows + SLOTS, heads), BF16)
    hidden, conv, act, embed, even_feat, odd_feat = call(
        forward_kernel,
        [
            shape((rows + 2 * STEP, channels), BF16),
            shape((rows, inner), F32),
            shape((rows, inner), BF16),
            shape((rows, channels), BF16),
            feat,
            feat,
        ],
        [SM] + [VM] * 10,
        20,
        4_000_000_000,
    )(
        odd, tokens, mine, even_edge, odd_edge, gain, dilated_tap_weight, point_weight,
        donor_weight, acceptor_weight, meta_rows,
    )

    acc_shapes = [shape((rows, heads), F32), shape((rows, heads), F32), shape((PANEL, PANEL), F32)]
    acc = ()
    edge_factor, slope, hidden_t, act_t, embed_t = call(
        side_kernel,
        [
            shape((2 * STEP, channels), BF16),
            shape((rows, inner), F32),
            shape((channels, rows + 2 * STEP), BF16),
            shape((inner, rows), BF16),
            shape((channels, rows), BF16),
        ],
        [SM] + [VM] * 9,
        20,
        6_000_000_000,
    )(odd, even_edge, odd_edge, gain, hidden, conv, act, embed, order, eye)
    even_far, odd_far = even_feat, odd_feat
    for distance in range(1, SPAN + 1):
        if distance == 1:
            odd_far, even_far = swapped(odd_feat, 0), swapped(even_feat, 1)
        else:
            odd_far, even_far = swapped(even_far, 0), swapped(odd_far, 1)
        far_meta = jnp.where(is_odd, odd_far[rows:, :8], even_far[rows:, :8]).astype(jnp.int32)
        acc = call(
            lambda *refs, distance=distance: pair_kernel(distance, *refs),
            acc_shapes,
            [SM] * 3 + [VM] * (4 + len(acc)),
            12,
            2_500_000_000,
        )(1 - odd, meta, far_meta, even_feat, odd_feat, even_far, odd_far, *acc)

    chunk = CHUNK_ROWS + EXTRA_ROWS
    lanes = inner // 128
    slabs = tap_count * lanes
    half = shape((4, slabs, PIECE, 128), BF16)
    y = lax.axis_index("y")
    place = jnp.stack([lax.axis_index("core"), y, lax.axis_index("zb")]).astype(jnp.int32)
    keep, send, d_conv, d_feat = call(
        tap_grad_kernel,
        [half, half, shape((rows, inner), BF16), shape((rows, 2 * heads), BF16)],
        [SM] + [VM] * 7,
        20,
        4_000_000_000,
    )(place, acc[0], acc[1], point_weight, donor_weight, acceptor_weight, slope, hidden_t)
    received = lax.ppermute(send, "core", [(0, 1), (1, 0)])
    (head_sum,) = call(
        head_grad_kernel, [shape((4, 4, chunk, 128), BF16)], [SM] + [VM] * 8, 20, 4_000_000_000
    )(place, d_conv, d_feat, acc[2], dilated_tap_weight, factor, edge_factor, act_t, embed_t)

    first_pairs = [(0, 1), (1, 0), (2, 3), (3, 2)]
    second_pairs = [(1, 2), (2, 1), (3, 0), (0, 3)]
    quick = 1_000_000
    conv_kept, conv_send = call(
        core_sum_kernel, [shape((2, slabs, PIECE, 128), F32), shape((2, slabs, PIECE, 128), BF16)],
        [VM] * 2, 12, quick,
    )(keep, received)
    other = lax.ppermute(head_sum[2:], "y", first_pairs)
    heads_kept, heads_send = call(
        head_sum_kernel, [shape((4, chunk, 128), F32), shape((4, chunk, 128), BF16)], [VM] * 2, 12, quick
    )(head_sum, other)
    other = lax.ppermute(conv_send, "y", second_pairs)
    conv_kept, conv_send = call(
        tap_sum_kernel, [shape((slabs, PIECE, 128), F32), shape((slabs, PIECE, 128), BF16)],
        [VM] * 2, 12, quick,
    )(conv_kept, other)
    heads_in = lax.ppermute(heads_send, "y", second_pairs)
    conv_in = lax.ppermute(conv_send, "y", first_pairs)

    joint = chunk + 224
    (both,) = call(join_kernel, [shape((4, joint, 128), BF16)], [VM] * 4, 12, quick)(
        heads_kept, heads_in, conv_kept, conv_in
    )
    parts = swap_parts(both, "zq")
    sent, mine = call(
        line_sum_kernel, [shape((chunk + 112, 128), BF16), shape((112, 128), BF16)],
        [SM] + [VM] * 2, 8, quick,
    )(place, parts, pick)
    received = lax.ppermute(sent, "zb", [(0, 1), (1, 0)])
    head_parts, conv_sum = call(
        far_sum_kernel, [shape((4, chunk, 128), BF16), shape((112, 128), BF16)], [VM] * 3, 8, quick
    )(sent, received, mine)
    other = lax.ppermute(conv_sum, "zhi", [(0, 1), (1, 0)])

    head_rows = 4 * chunk
    head_sum = swap_parts(head_parts, "zq").reshape(head_rows, 128)
    ring = [
        lax.ppermute(head_sum, "y", [(i, (i + ahead) % 4) for i in range(4)]) for ahead in (1, 2, 3)
    ]
    other, head_sum = lax.optimization_barrier((other, head_sum))
    conv_sum = (conv_sum.astype(F32) + other.astype(F32)).astype(BF16)
    pieces = gather_parts(conv_sum, ("x", "core")).astype(F32)
    pieces = jnp.sum(pieces.reshape(4, 2, 112, 128), axis=0)[:, : slabs * 12]
    pieces = pieces.reshape(2, tap_count, lanes, 12, 128)
    grad_conv = pieces.transpose(1, 0, 3, 2, 4).reshape(tap_count, 24, inner)
    head_weight = shape((channels, heads), BF16)
    grad_donor, grad_accept, grad_point, grad_gain, loss = call(
        finish_kernel,
        [head_weight, head_weight, shape((inner, channels), BF16), shape((1, channels), F32), shape((1, 128), F32)],
        [SM] + [VM] * 6,
        16,
        1_000_000_000,
        [
            pltpu.VMEM((4, head_rows, 128), BF16),
            pltpu.VMEM((inner, heads), BF16),
            pltpu.VMEM((inner, heads), BF16),
        ],
    )(place, head_sum, *ring, donor_weight, acceptor_weight)
    return grad_conv, grad_point[None], grad_donor[None], grad_accept[None], grad_gain, loss[0, :1]


def channel_order():
    core, y, zq, zb, k = np.meshgrid(*[np.arange(n) for n in (2, 4, 4, 2, 12)], indexing="ij")
    channel = (24 * (8 * y + 4 * zb + zq) + 12 * core + k).reshape(-1)
    return np.eye(channel.size, dtype=np.float32)[channel]


def zb_halves():
    pick = np.zeros((224, 224), np.float32)
    for zb in range(2):
        for slab in range(9):
            for k in range(12):
                pick[112 * zb + 12 * slab + k, 24 * slab + 12 * zb + k] = 1.0
    return pick


def solution(mesh):
    fine = Mesh(mesh.devices.reshape(4, 2, 4, 2, 4, 2), SEQ + BATCH)
    placed = jax.shard_map(
        on_device,
        mesh=fine,
        in_specs=(
            P(BATCH, SEQ, None),
            P(),
            P(),
            P(),
            P(),
            P(),
            P(BATCH, SEQ, None),
            P(BATCH, SEQ),
            P(),
            P(),
            P(),
        ),
        out_specs=(
            P(None, SEQ, None),
            P(BATCH, None, None),
            P(BATCH, None, None),
            P(BATCH, None, None),
            P(BATCH, None),
            P(BATCH),
        ),
        check_vma=False,
    )

    def run(*arrays):
        order = jnp.asarray(channel_order(), BF16)
        eye = jnp.eye(order.shape[0], dtype=BF16)
        return placed(*arrays, order, eye, jnp.asarray(zb_halves(), BF16))

    return run
```

```python
import jax
import jax.numpy as jnp
import numpy as np
from jax import lax
from jax.experimental import pallas as pl
from jax.experimental.pallas import tpu as pltpu
from jax.sharding import Mesh
from jax.sharding import PartitionSpec as P

STEP = 128
PANEL = 128
SPAN = 4
SLOTS = 16
EPSILON = 1e-06
LOSS_WEIGHT = 1.0 / 128.0
SEQ = ("y", "zb", "zq")
BATCH = ("zhi", "x", "core")
F32 = jnp.float32
BF16 = jnp.bfloat16
ROOT = 0.7978845608028654
CUBIC = 0.044715
PIECE = 96
CHUNK_ROWS = 288
EXTRA_ROWS = 16


def dot(a, b):
    return lax.dot_general(a, b, (((1,), (0,)), ((), ())), preferred_element_type=F32)


def dot_t(a, b):
    return lax.dot_general(a, b, (((1,), (1,)), ((), ())), preferred_element_type=F32)


def gelu(v):
    return 0.5 * v * (1.0 + jnp.tanh(ROOT * (v + CUBIC * (v * v * v))))


def gelu_both(v):
    square = v * v
    t = jnp.tanh(ROOT * (v + CUBIC * (square * v)))
    half = 0.5 * (1.0 + t)
    return v * half, half + 0.5 * v * (1.0 - t * t) * (ROOT * (1.0 + 3.0 * CUBIC * square))


def rms(v):
    return lax.rsqrt(jnp.mean(v * v, axis=-1, keepdims=True) + EPSILON)


def call(kernel, outs, specs, megabytes, flops, scratch=()):
    return pl.pallas_call(
        kernel,
        out_shape=outs,
        in_specs=specs,
        out_specs=[VM] * len(outs),
        scratch_shapes=list(scratch),
        compiler_params=pltpu.CompilerParams(vmem_limit_bytes=megabytes * 1024 * 1024),
        cost_estimate=pl.CostEstimate(flops=flops, bytes_accessed=1_000_000, transcendentals=0),
    )


VM = pl.BlockSpec(memory_space=pltpu.VMEM)
SM = pl.BlockSpec(memory_space=pltpu.SMEM)


def own_kernel(tok, gain, hidden, factor):
    @pl.loop(0, tok.shape[0] // STEP)
    def _(i):
        here = pl.ds(pl.multiple_of(i * STEP, STEP), STEP)
        v = tok[here, :].astype(F32)
        unit = v * rms(v)
        value, slope = gelu_both(unit * gain[...])
        hidden[here, :] = value.astype(BF16)
        factor[here, :] = (slope * unit).astype(BF16)


def forward_kernel(
    odd, tok, mine, even_edge, odd_edge, gain, taps, point, donor_w, accept_w, meta,
    hidden, conv_out, act_out, embed_out, even_feat, odd_feat,
):
    rows = tok.shape[0]
    is_odd = odd[0] > 0
    low = jnp.where(is_odd, even_edge[...], odd_edge[...])
    high = jnp.where(is_odd, odd_edge[...], even_edge[...])
    for edge, at in ((low, 0), (high, STEP + rows)):
        v = edge.astype(F32)
        hidden[pl.ds(at, STEP), :] = gelu(v * rms(v) * gain[...]).astype(BF16)
    hidden[pl.ds(STEP, rows), :] = mine[...]

    conv = dot(hidden[:rows, :], taps[0])
    for tap in range(1, taps.shape[0]):
        conv = conv + dot(hidden[tap * STEP : tap * STEP + rows, :], taps[tap])
    conv_out[...] = conv
    act = gelu(conv).astype(BF16)
    act_out[...] = act
    embed = (tok[...].astype(F32) + dot(act, point[...])).astype(BF16)
    embed_out[...] = embed
    donor = dot(embed, donor_w[...]).astype(BF16)
    accept = dot(embed, accept_w[...]).astype(BF16)
    even_feat[:rows, :] = jnp.where(is_odd, donor, accept)
    odd_feat[:rows, :] = jnp.where(is_odd, accept, donor)
    even_feat[pl.ds(rows, SLOTS), :] = meta[...]
    odd_feat[pl.ds(rows, SLOTS), :] = meta[...]


def side_kernel(
    odd, even_edge, odd_edge, gain, hidden, conv, act, embed, order, eye,
    factor, slope, hidden_t, act_t, embed_t,
):
    is_odd = odd[0] > 0
    low = jnp.where(is_odd, even_edge[...], odd_edge[...])
    high = jnp.where(is_odd, odd_edge[...], even_edge[...])
    for edge, at in ((low, 0), (high, STEP)):
        v = edge.astype(F32)
        unit = v * rms(v)
        factor[pl.ds(at, STEP), :] = (gelu_both(unit * gain[...])[1] * unit).astype(BF16)

    @pl.loop(0, conv.shape[0] // STEP)
    def _(i):
        here = pl.ds(pl.multiple_of(i * STEP, STEP), STEP)
        slope[here, :] = gelu_both(conv[here, :])[1]

    hidden_t[...] = dot_t(order[...], hidden[...]).astype(BF16)
    embed_t[...] = dot_t(eye[...], embed[...]).astype(BF16)
    inner = act.shape[1]
    act_t[...] = dot_t(eye[:inner, :inner], act[...]).astype(BF16)


def pair_kernel(distance, *refs):
    if distance == 0:
        odd, own, even0, odd0, d_donor, d_accept, loss = refs
        d_donor[...] = jnp.zeros_like(d_donor)
        d_accept[...] = jnp.zeros_like(d_accept)
        loss[...] = jnp.zeros_like(loss)
    else:
        odd, own, far, even0, odd0, even1, odd1, dd_in, da_in, loss_in, d_donor, d_accept, loss = refs
        d_donor[...] = dd_in[...]
        d_accept[...] = da_in[...]
        loss[...] = loss_in[...]
    is_odd = odd[0] > 0
    scale = even0.shape[1] ** (-0.5)
    per_device = d_donor.shape[0] // PANEL
    row = lax.broadcasted_iota(jnp.int32, (PANEL, PANEL), 0)
    col = lax.broadcasted_iota(jnp.int32, (PANEL, PANEL), 1)

    def place(block):
        return pl.ds(pl.multiple_of(block * PANEL, PANEL), PANEL)

    def own_donor(block):
        return jnp.where(is_odd, odd0[place(block), :], even0[place(block), :])

    def own_accept(block):
        return jnp.where(is_odd, even0[place(block), :], odd0[place(block), :])

    if distance == 0:
        far_accept, far_donor = own_accept, None
    else:

        def far_accept(block):
            return jnp.where(is_odd, odd1[place(block), :], even1[place(block), :])

        def far_donor(block):
            return jnp.where(is_odd, even1[place(block), :], odd1[place(block), :])

    def visit(meta, j, donors, acceptors, is_owner):
        accept_block = meta[j, 2] - distance * per_device
        here = (meta[j, 4] > 0) & (accept_block >= 0) & (accept_block < per_device)

        @pl.when(here)
        def _():
            donor_block = meta[j, 0]
            dpan = donors(donor_block)
            apan = acceptors(accept_block)
            scores = dot_t(dpan, apan) * scale
            target = ((row == meta[j, 1]) & (col == meta[j, 3])).astype(F32)
            small = jnp.exp(-jnp.abs(scores))
            inverse = 1.0 / (1.0 + small)
            sigmoid = jnp.where(scores >= 0, inverse, small * inverse)
            dscore = ((sigmoid - target) * LOSS_WEIGHT).astype(BF16)
            if is_owner:
                loss[...] += (jnp.maximum(scores, 0.0) + jnp.log1p(small)) - target * scores
                d_donor[place(donor_block), :] += dot(dscore, apan) * scale
            if distance == 0 or not is_owner:
                d_accept[place(accept_block), :] += scale * lax.dot_general(
                    dscore, dpan, (((0,), (0,)), ((), ())), preferred_element_type=F32
                )

    @pl.loop(0, SLOTS)
    def _(j):
        visit(own, j, own_donor, far_accept, True)
        if distance > 0:
            visit(far, j, far_donor, own_accept, False)


def relative(target, y, first):
    code = (target ^ (target >> 1)) ^ (y ^ (y >> 1))
    low, high = code & 1, code >> 1
    return low * 2 + high if first == 0 else high * 2 + low


def tap_grad_kernel(
    place, d_donor, d_accept, point, donor_w, accept_w, slope, hidden_t,
    keep, send, d_conv, d_feat,
):
    rows, heads = d_donor.shape
    channels = hidden_t.shape[0]

    dd = d_donor[...].astype(BF16)
    da = d_accept[...].astype(BF16)
    d_feat[:, :heads] = dd
    d_feat[:, heads:] = da
    d_embed = (dot_t(dd, donor_w[...]) + dot_t(da, accept_w[...])).astype(BF16)
    d_conv[...] = (dot_t(d_embed, point[...]) * slope[...]).astype(BF16)

    lanes = d_conv.shape[1] // 128
    half_rows = channels // 2
    slab = [relative(target, place[1], 1) for target in range(4)]
    for tap in range(3):
        for half in range(2):
            part = dot(
                hidden_t[half * half_rows : (half + 1) * half_rows, tap * STEP : tap * STEP + rows],
                d_conv[...],
            ).astype(BF16)

            def store(into, part=part, tap=tap):
                for k in range(4):
                    for lane in range(lanes):
                        into[slab[k], tap * lanes + lane] = part[
                            k * PIECE : (k + 1) * PIECE, lane * 128 : (lane + 1) * 128
                        ]

            pl.when(place[0] == half)(lambda: store(keep))
            pl.when(place[0] != half)(lambda: store(send))


def head_grad_kernel(
    place, d_conv, d_feat, loss, taps, factor, edge_factor, act_t, embed_t, head_sum,
):
    rows = d_conv.shape[0]
    channels = embed_t.shape[0]
    inner = act_t.shape[0]
    slab = [relative(target, place[1], 0) for target in range(4)]

    def put(part, base, group_rows, first):
        for lane in range(4):
            for k in range(part.shape[0] // PIECE):
                piece = first + lane * (group_rows // PIECE) + k + base
                chunk, third = piece // 3, piece % 3
                head_sum[slab[chunk // 4], chunk % 4, third * PIECE : (third + 1) * PIECE, :] = part[
                    k * PIECE : (k + 1) * PIECE, lane * 128 : (lane + 1) * 128
                ]

    for i in range(2):
        part = dot(embed_t[i * 4 * PIECE : (i + 1) * 4 * PIECE, :], d_feat[...]).astype(BF16)
        put(part, 4 * i, channels, 0)
    put(dot(act_t[...], d_feat[...]).astype(BF16), 0, inner, 4 * channels // PIECE)

    total = jnp.zeros((8, channels), F32)
    edge = edge_factor.shape[0] // 2
    for tap in range(taps.shape[0]):
        product = dot_t(d_conv[...], taps[tap])
        if tap == 0:
            weights = jnp.concatenate([edge_factor[:edge, :], factor[: rows - edge, :]], axis=0)
        elif tap == 1:
            weights = factor[...]
        else:
            weights = jnp.concatenate([factor[edge:, :], edge_factor[edge:, :]], axis=0)
        product = product * weights.astype(F32)
        total = total + jnp.sum(product.reshape(rows // 8, 8, channels), axis=0)
    gain = jnp.sum(total, axis=0, keepdims=True)
    loss_row = jnp.sum(loss[...], axis=0, keepdims=True) * LOSS_WEIGHT
    loss_all = jnp.broadcast_to(jnp.sum(loss_row, axis=1, keepdims=True), (1, 128))
    at_row = lax.broadcasted_iota(jnp.int32, (EXTRA_ROWS, 128), 0)
    for chunk in range(16):
        if chunk < channels // 128:
            value = gain[:, chunk * 128 : (chunk + 1) * 128]
        elif chunk == channels // 128:
            value = loss_all
        else:
            value = jnp.zeros((1, 128), F32)
        coarse = value.astype(BF16).astype(F32)
        block = jnp.where(at_row == 0, coarse, 0.0) + jnp.where(at_row == 8, value - coarse, 0.0)
        head_sum[slab[chunk // 4], chunk % 4, CHUNK_ROWS:, :] = block.astype(BF16)


def split_rows(total):
    value = total[CHUNK_ROWS : CHUNK_ROWS + 8] + total[CHUNK_ROWS + 8 : CHUNK_ROWS + 16]
    coarse = value.astype(BF16).astype(F32)
    return jnp.concatenate([total[:CHUNK_ROWS], coarse, value - coarse], axis=0).astype(BF16)


def core_sum_kernel(taps, received, kept, send):
    for k in range(2):
        for slab in range(taps.shape[1]):
            kept[k, slab] = taps[k, slab].astype(F32) + received[k, slab].astype(F32)
            send[k, slab] = (
                taps[k + 2, slab].astype(F32) + received[k + 2, slab].astype(F32)
            ).astype(BF16)


def head_sum_kernel(head, received, kept, send):
    for zq in range(4):
        kept[zq] = head[0, zq].astype(F32) + received[0, zq].astype(F32)
        send[zq] = split_rows(head[1, zq].astype(F32) + received[1, zq].astype(F32))


def tap_sum_kernel(before, received, kept, send):
    for slab in range(before.shape[1]):
        kept[slab] = before[0, slab] + received[0, slab].astype(F32)
        send[slab] = (before[1, slab] + received[1, slab].astype(F32)).astype(BF16)


def join_kernel(head, head_in, taps, taps_in, both):
    chunk_rows = head.shape[1]
    for zq in range(4):
        both[zq, :chunk_rows, :] = split_rows(head[zq] + head_in[zq].astype(F32))
        here = slice(zq * 24, (zq + 1) * 24)
        parts = [taps[k, here] + taps_in[k, here].astype(F32) for k in range(taps.shape[0])]
        parts.append(jnp.zeros((8, 128), F32))
        both[zq, chunk_rows:, :] = jnp.concatenate(parts, axis=0).astype(BF16)


def line_sum_kernel(place, parts, pick, send, mine):
    total = parts[0].astype(F32)
    for zq in range(1, 4):
        total = total + parts[zq].astype(F32)
    chunk_rows = CHUNK_ROWS + EXTRA_ROWS
    send[:chunk_rows, :] = split_rows(total[:chunk_rows])
    taps = total[chunk_rows:].astype(BF16)
    half = mine.shape[0]
    zb = place[2]

    def picked(which):
        return dot(pick[pl.ds(pl.multiple_of(which * half, half), half), :], taps).astype(BF16)

    send[chunk_rows:, :] = picked(1 - zb)
    mine[...] = picked(zb)


def far_sum_kernel(sent, received, mine, one, two, head, taps):
    chunk_rows = head.shape[1]
    total = split_rows(sent[:chunk_rows, :].astype(F32) + received[:chunk_rows, :].astype(F32))
    for zq in range(head.shape[0]):
        head[zq] = total
    near = mine[...].astype(F32) + received[chunk_rows:, :].astype(F32)
    taps[...] = (near + (one[...].astype(F32) + two[...].astype(F32))).astype(BF16)


def line_total_kernel(own, one, two, three, total):
    even = own[...].astype(F32) + two[...].astype(F32)
    total[...] = even + (one[...].astype(F32) + three[...].astype(F32))


def finish_kernel(
    place, own, behind, ahead, low, high, donor_w, accept_w,
    grad_donor, grad_accept, grad_point, gain, loss, held, act_donor, act_accept,
):
    count = held.shape[0]
    for step, part in ((0, own), (3, behind), (1, ahead)):
        held[lax.rem(place[1] + step, count)] = part[...]
    opposite = lax.rem(place[1] + 2, count)
    middle = low.shape[0]
    held[opposite, :middle, :] = low[...]
    held[opposite, middle:, :] = high[...]
    channels = grad_donor.shape[0]
    inner = act_donor.shape[0]
    chunk_rows = CHUNK_ROWS + EXTRA_ROWS
    piece = 0
    for into in (grad_donor, grad_accept, act_donor, act_accept):
        for lane in range(2):
            for k in range(into.shape[0] // PIECE):
                chunk, third = piece // 3, piece % 3
                at = (chunk % 4) * chunk_rows + third * PIECE
                into[k * PIECE : (k + 1) * PIECE, lane * 128 : (lane + 1) * 128] = held[
                    chunk // 4, at : at + PIECE, :
                ]
                piece += 1

    grad_point[...] = (
        dot_t(act_donor[...], donor_w[...]) + dot_t(act_accept[...], accept_w[...])
    ).astype(BF16)

    for chunk in range(channels // 128 + 1):
        at = (chunk % 4) * chunk_rows + CHUNK_ROWS
        block = held[chunk // 4, at : at + EXTRA_ROWS, :].astype(F32)
        value = block[0:1, :] + block[8:9, :]
        if chunk < channels // 128:
            gain[:, chunk * 128 : (chunk + 1) * 128] = value
        else:
            loss[...] = value


def swapped(block, first):
    count = lax.axis_size(SEQ)
    pairs = [(i, i + 1) for i in range(first, count - 1, 2)]
    return lax.ppermute(block, SEQ, pairs + [(j, i) for i, j in pairs])


def swap_parts(parts, axis):
    return lax.all_to_all(parts, axis, 0, 0, tiled=True)


def on_device(
    activations, norm_gain, dilated_tap_weight, point_weight, donor_weight, acceptor_weight,
    pair_sites, pair_count, order, eye, pick,
):
    tokens = activations[0]
    rows, channels = tokens.shape
    tap_count, _, inner = dilated_tap_weight.shape
    heads = donor_weight.shape[1]
    blocks = rows // PANEL
    shape = jax.ShapeDtypeStruct
    here = lax.axis_index(SEQ)
    odd = (here % 2).astype(jnp.int32)[None]
    is_odd = odd[0] > 0
    start, end = tokens[:STEP], tokens[rows - STEP :]
    even_edge = swapped(jnp.where(is_odd, start, end), 0)
    odd_edge = swapped(jnp.where(is_odd, end, start), 1)
    gain = norm_gain[None]
    sites = pair_sites[0]
    first = here * blocks
    live = (jnp.arange(SLOTS, dtype=jnp.int32) < pair_count[0, 0]).astype(jnp.int32)
    meta = jnp.stack(
        [
            sites[:, 0] // PANEL - first,
            sites[:, 0] % PANEL,
            sites[:, 1] // PANEL - first,
            sites[:, 1] % PANEL,
            live,
        ]
        + [jnp.zeros_like(live)] * 3,
        axis=1,
    )
    meta_rows = jnp.pad(meta.astype(BF16), ((0, 0), (0, heads - meta.shape[1])))

    mine, factor = call(
        own_kernel, [shape((rows, channels), BF16)] * 2, [VM] * 2, 12, 2_000_000_000
    )(tokens, gain)
    feat = shape((rows + SLOTS, heads), BF16)
    hidden, conv, act, embed, even_feat, odd_feat = call(
        forward_kernel,
        [
            shape((rows + 2 * STEP, channels), BF16),
            shape((rows, inner), F32),
            shape((rows, inner), BF16),
            shape((rows, channels), BF16),
            feat,
            feat,
        ],
        [SM] + [VM] * 10,
        20,
        4_000_000_000,
    )(
        odd, tokens, mine, even_edge, odd_edge, gain, dilated_tap_weight, point_weight,
        donor_weight, acceptor_weight, meta_rows,
    )

    acc_shapes = [shape((rows, heads), F32), shape((rows, heads), F32), shape((PANEL, PANEL), F32)]
    acc = call(
        lambda *refs: pair_kernel(0, *refs), acc_shapes, [SM] * 2 + [VM] * 2, 12, 2_000_000_000
    )(1 - odd, meta, even_feat, odd_feat)
    edge_factor, slope, hidden_t, act_t, embed_t = call(
        side_kernel,
        [
            shape((2 * STEP, channels), BF16),
            shape((rows, inner), F32),
            shape((channels, rows + 2 * STEP), BF16),
            shape((inner, rows), BF16),
            shape((channels, rows), BF16),
        ],
        [SM] + [VM] * 9,
        20,
        6_000_000_000,
    )(odd, even_edge, odd_edge, gain, hidden, conv, act, embed, order, eye)
    even_far, odd_far = even_feat, odd_feat
    for distance in range(1, SPAN + 1):
        if distance == 1:
            odd_far, even_far = swapped(odd_feat, 0), swapped(even_feat, 1)
        else:
            odd_far, even_far = swapped(even_far, 0), swapped(odd_far, 1)
        far_meta = jnp.where(is_odd, odd_far[rows:, :8], even_far[rows:, :8]).astype(jnp.int32)
        acc = call(
            lambda *refs, distance=distance: pair_kernel(distance, *refs),
            acc_shapes,
            [SM] * 3 + [VM] * 7,
            12,
            2_500_000_000,
        )(1 - odd, meta, far_meta, even_feat, odd_feat, even_far, odd_far, *acc)

    chunk = CHUNK_ROWS + EXTRA_ROWS
    lanes = inner // 128
    slabs = tap_count * lanes
    y = lax.axis_index("y")
    place = jnp.stack([lax.axis_index("core"), y, lax.axis_index("zb")]).astype(jnp.int32)
    half = shape((4, slabs, PIECE, 128), BF16)
    keep, send, d_conv, d_feat = call(
        tap_grad_kernel,
        [half, half, shape((rows, inner), BF16), shape((rows, 2 * heads), BF16)],
        [SM] + [VM] * 7,
        24,
        4_000_000_000,
    )(place, acc[0], acc[1], point_weight, donor_weight, acceptor_weight, slope, hidden_t)
    received = lax.ppermute(send, "core", [(0, 1), (1, 0)])
    (head_sum,) = call(
        head_grad_kernel, [shape((4, 4, chunk, 128), BF16)], [SM] + [VM] * 8, 20, 4_000_000_000
    )(place, d_conv, d_feat, acc[2], dilated_tap_weight, factor, edge_factor, act_t, embed_t)

    first_pairs = [(0, 1), (1, 0), (2, 3), (3, 2)]
    second_pairs = [(1, 2), (2, 1), (3, 0), (0, 3)]
    quick = 1_000_000
    conv_kept, conv_send = call(
        core_sum_kernel, [shape((2, slabs, PIECE, 128), F32), shape((2, slabs, PIECE, 128), BF16)],
        [VM] * 2, 12, quick,
    )(keep, received)
    other = lax.ppermute(head_sum[2:], "y", first_pairs)
    heads_kept, heads_send = call(
        head_sum_kernel, [shape((4, chunk, 128), F32), shape((4, chunk, 128), BF16)], [VM] * 2, 12, quick
    )(head_sum, other)
    other = lax.ppermute(conv_send, "y", second_pairs)
    conv_kept, conv_send = call(
        tap_sum_kernel, [shape((slabs, PIECE, 128), F32), shape((slabs, PIECE, 128), BF16)],
        [VM] * 2, 12, quick,
    )(conv_kept, other)
    heads_in = lax.ppermute(heads_send, "y", second_pairs)
    conv_in = lax.ppermute(conv_send, "y", first_pairs)

    joint = chunk + 224
    (both,) = call(join_kernel, [shape((4, joint, 128), BF16)], [VM] * 4, 12, quick)(
        heads_kept, heads_in, conv_kept, conv_in
    )
    parts = swap_parts(both, "zq")
    sent, mine = call(
        line_sum_kernel, [shape((chunk + 112, 128), BF16), shape((112, 128), BF16)],
        [SM] + [VM] * 2, 8, quick,
    )(place, parts, pick)
    received = lax.ppermute(sent, "zb", [(0, 1), (1, 0)])
    across = lax.ppermute(mine, "zhi", [(0, 1), (1, 0)])
    corner = lax.ppermute(
        sent[chunk:], ("zb", "zhi"), [(0, 3), (3, 0), (1, 2), (2, 1)]
    )
    head_parts, conv_sum = call(
        far_sum_kernel, [shape((4, chunk, 128), BF16), shape((112, 128), BF16)], [VM] * 5, 8, quick
    )(sent, received, mine, across, corner)

    head_rows = 4 * chunk
    head_sum = swap_parts(head_parts, "zq").reshape(head_rows, 128)
    line = [
        lax.ppermute(conv_sum, "x", [(i, (i + step) % 4) for i in range(4)]) for step in (1, 2, 3)
    ]
    (conv_sum,) = call(line_total_kernel, [shape((112, 128), F32)], [VM] * 4, 8, quick)(conv_sum, *line)
    head_sum, conv_sum = lax.optimization_barrier((head_sum, conv_sum))
    other = lax.ppermute(conv_sum, "core", [(0, 1), (1, 0)])
    around = [(i, (i + 1) % 4) for i in range(4)]
    back = [(j, i) for i, j in around]
    behind = lax.ppermute(head_sum, "y", around)
    ahead = lax.ppermute(head_sum, "y", back)
    low = lax.ppermute(behind[: head_rows // 2], "y", around)
    high = lax.ppermute(ahead[head_rows // 2 :], "y", back)
    is_first = lax.axis_index("core") == 0
    pieces = jnp.stack([jnp.where(is_first, conv_sum, other), jnp.where(is_first, other, conv_sum)])
    pieces = pieces[:, : slabs * 12].reshape(2, tap_count, lanes, 12, 128)
    grad_conv = pieces.transpose(1, 0, 3, 2, 4).reshape(tap_count, 24, inner)
    head_weight = shape((channels, heads), BF16)
    grad_donor, grad_accept, grad_point, grad_gain, loss = call(
        finish_kernel,
        [head_weight, head_weight, shape((inner, channels), BF16), shape((1, channels), F32), shape((1, 128), F32)],
        [SM] + [VM] * 7,
        20,
        1_000_000_000,
        [
            pltpu.VMEM((4, head_rows, 128), BF16),
            pltpu.VMEM((inner, heads), BF16),
            pltpu.VMEM((inner, heads), BF16),
        ],
    )(place, head_sum, behind, ahead, low, high, donor_weight, acceptor_weight)
    return grad_conv, grad_point[None], grad_donor[None], grad_accept[None], grad_gain, loss[0, :1]


def channel_order():
    core, y, zq, zb, k = np.meshgrid(*[np.arange(n) for n in (2, 4, 4, 2, 12)], indexing="ij")
    channel = (24 * (8 * y + 4 * zb + zq) + 12 * core + k).reshape(-1)
    return np.eye(channel.size, dtype=np.float32)[channel]


def zb_halves():
    pick = np.zeros((224, 224), np.float32)
    for zb in range(2):
        for slab in range(9):
            for k in range(12):
                pick[112 * zb + 12 * slab + k, 24 * slab + 12 * zb + k] = 1.0
    return pick


def solution(mesh):
    fine = Mesh(mesh.devices.reshape(4, 2, 4, 2, 4, 2), SEQ + BATCH)
    placed = jax.shard_map(
        on_device,
        mesh=fine,
        in_specs=(
            P(BATCH, SEQ, None),
            P(),
            P(),
            P(),
            P(),
            P(),
            P(BATCH, SEQ, None),
            P(BATCH, SEQ),
            P(),
            P(),
            P(),
        ),
        out_specs=(
            P(None, SEQ, None),
            P(BATCH, None, None),
            P(BATCH, None, None),
            P(BATCH, None, None),
            P(BATCH, None),
            P(BATCH),
        ),
        check_vma=False,
    )

    def run(*arrays):
        order = jnp.asarray(channel_order(), BF16)
        eye = jnp.eye(order.shape[0], dtype=BF16)
        return placed(*arrays, order, eye, jnp.asarray(zb_halves(), BF16))

    return run
```

```python
import jax
import jax.numpy as jnp
import numpy as np
from jax import lax
from jax.experimental import pallas as pl
from jax.experimental.pallas import tpu as pltpu
from jax.sharding import Mesh
from jax.sharding import PartitionSpec as P

STEP = 128
PANEL = 128
SPAN = 4
SLOTS = 16
EPSILON = 1e-06
LOSS_WEIGHT = 1.0 / 128.0
SEQ = ("y", "zb", "zq")
BATCH = ("zhi", "x", "core")
F32 = jnp.float32
BF16 = jnp.bfloat16
ROOT = 0.7978845608028654
CUBIC = 0.044715
PIECE = 96
CHUNK_ROWS = 288
EXTRA_ROWS = 16


def dot(a, b):
    return lax.dot_general(a, b, (((1,), (0,)), ((), ())), preferred_element_type=F32)


def dot_t(a, b):
    return lax.dot_general(a, b, (((1,), (1,)), ((), ())), preferred_element_type=F32)


def gelu(v):
    return 0.5 * v * (1.0 + jnp.tanh(ROOT * (v + CUBIC * (v * v * v))))


def gelu_both(v):
    square = v * v
    t = jnp.tanh(ROOT * (v + CUBIC * (square * v)))
    half = 0.5 * (1.0 + t)
    return v * half, half + 0.5 * v * (1.0 - t * t) * (ROOT * (1.0 + 3.0 * CUBIC * square))


def rms(v):
    return lax.rsqrt(jnp.mean(v * v, axis=-1, keepdims=True) + EPSILON)


def call(kernel, outs, specs, megabytes, flops, scratch=()):
    return pl.pallas_call(
        kernel,
        out_shape=outs,
        in_specs=specs,
        out_specs=[VM] * len(outs),
        scratch_shapes=list(scratch),
        compiler_params=pltpu.CompilerParams(vmem_limit_bytes=megabytes * 1024 * 1024),
        cost_estimate=pl.CostEstimate(flops=flops, bytes_accessed=1_000_000, transcendentals=0),
    )


VM = pl.BlockSpec(memory_space=pltpu.VMEM)
SM = pl.BlockSpec(memory_space=pltpu.SMEM)


def own_kernel(tok, gain, hidden, factor):
    @pl.loop(0, tok.shape[0] // STEP)
    def _(i):
        here = pl.ds(pl.multiple_of(i * STEP, STEP), STEP)
        v = tok[here, :].astype(F32)
        unit = v * rms(v)
        value, slope = gelu_both(unit * gain[...])
        hidden[here, :] = value.astype(BF16)
        factor[here, :] = (slope * unit).astype(BF16)


def forward_kernel(
    odd, tok, mine, even_edge, odd_edge, gain, taps, point, donor_w, accept_w, meta,
    hidden, conv_out, act_out, embed_out, even_feat, odd_feat,
):
    rows = tok.shape[0]
    is_odd = odd[0] > 0
    low = jnp.where(is_odd, even_edge[...], odd_edge[...])
    high = jnp.where(is_odd, odd_edge[...], even_edge[...])
    for edge, at in ((low, 0), (high, STEP + rows)):
        v = edge.astype(F32)
        hidden[pl.ds(at, STEP), :] = gelu(v * rms(v) * gain[...]).astype(BF16)
    hidden[pl.ds(STEP, rows), :] = mine[...]

    conv = dot(hidden[:rows, :], taps[0])
    for tap in range(1, taps.shape[0]):
        conv = conv + dot(hidden[tap * STEP : tap * STEP + rows, :], taps[tap])
    conv_out[...] = conv
    act = gelu(conv).astype(BF16)
    act_out[...] = act
    embed = (tok[...].astype(F32) + dot(act, point[...])).astype(BF16)
    embed_out[...] = embed
    donor = dot(embed, donor_w[...]).astype(BF16)
    accept = dot(embed, accept_w[...]).astype(BF16)
    even_feat[:rows, :] = jnp.where(is_odd, donor, accept)
    odd_feat[:rows, :] = jnp.where(is_odd, accept, donor)
    even_feat[pl.ds(rows, SLOTS), :] = meta[...]
    odd_feat[pl.ds(rows, SLOTS), :] = meta[...]


def side_kernel(
    odd, even_edge, odd_edge, gain, hidden, conv, act, embed, order, eye,
    factor, slope, hidden_t, act_t, embed_t,
):
    is_odd = odd[0] > 0
    low = jnp.where(is_odd, even_edge[...], odd_edge[...])
    high = jnp.where(is_odd, odd_edge[...], even_edge[...])
    for edge, at in ((low, 0), (high, STEP)):
        v = edge.astype(F32)
        unit = v * rms(v)
        factor[pl.ds(at, STEP), :] = (gelu_both(unit * gain[...])[1] * unit).astype(BF16)

    @pl.loop(0, conv.shape[0] // STEP)
    def _(i):
        here = pl.ds(pl.multiple_of(i * STEP, STEP), STEP)
        slope[here, :] = gelu_both(conv[here, :])[1]

    hidden_t[...] = dot_t(order[...], hidden[...]).astype(BF16)
    embed_t[...] = dot_t(eye[...], embed[...]).astype(BF16)
    inner = act.shape[1]
    act_t[...] = dot_t(eye[:inner, :inner], act[...]).astype(BF16)


def pair_kernel(distance, *refs):
    if distance == 0:
        flag, own, first0, second0, d_donor, d_accept, loss, own_list, _ = refs
        d_donor[...] = jnp.zeros_like(d_donor)
        d_accept[...] = jnp.zeros_like(d_accept)
        loss[...] = jnp.zeros_like(loss)
        first1, second1, far, far_list = second0, first0, None, None
    else:
        (
            flag, own, far, first0, second0, first1, second1, dd_in, da_in, loss_in,
            d_donor, d_accept, loss, own_list, far_list,
        ) = refs
        d_donor[...] = dd_in[...]
        d_accept[...] = da_in[...]
        loss[...] = loss_in[...]
    scale = first0.shape[1] ** (-0.5)
    per_device = d_donor.shape[0] // PANEL
    row = lax.broadcasted_iota(jnp.int32, (PANEL, PANEL), 0)
    col = lax.broadcasted_iota(jnp.int32, (PANEL, PANEL), 1)

    def collect(meta, into):
        def step(j, count):
            block = meta[j, 2] - distance * per_device
            here = (meta[j, 4] > 0) & (block >= 0) & (block < per_device)
            into[count, 0] = meta[j, 0]
            into[count, 1] = meta[j, 1]
            into[count, 2] = jnp.clip(block, 0, per_device - 1)
            into[count, 3] = meta[j, 3]
            return count + here.astype(jnp.int32)

        return lax.fori_loop(0, SLOTS, step, jnp.int32(0), unroll=True)

    def place(block):
        return pl.ds(pl.multiple_of(block * PANEL, PANEL), PANEL)

    def visit(slots, i, count, donors, acceptors, is_owner):
        j = jnp.minimum(i, jnp.maximum(count - 1, 0))
        used = jnp.where(i < count, 1.0, 0.0).astype(F32)
        donor_block, accept_block = slots[j, 0], slots[j, 2]
        dpan = donors[place(donor_block), :]
        apan = acceptors[place(accept_block), :]
        scores = dot_t(dpan, apan) * scale
        target = ((row == slots[j, 1]) & (col == slots[j, 3])).astype(F32)
        small = jnp.exp(-jnp.abs(scores))
        inverse = 1.0 / (1.0 + small)
        sigmoid = jnp.where(scores >= 0, inverse, small * inverse)
        dscore = ((sigmoid - target) * (used * LOSS_WEIGHT)).astype(BF16)
        results = []
        if is_owner:
            term = (jnp.maximum(scores, 0.0) + jnp.log1p(small)) - target * scores
            results.append((d_donor, donor_block, dot(dscore, apan) * scale))
            results.append((loss, None, term * used))
        if distance == 0 or not is_owner:
            back = lax.dot_general(
                dscore, dpan, (((0,), (0,)), ((), ())), preferred_element_type=F32
            )
            results.append((d_accept, accept_block, back * scale))
        return results

    def add(results):
        for ref, block, value in results:
            if block is None:
                ref[...] += value
            else:
                ref[place(block), :] += value

    def run(donors, own_accept, far_donor, far_accept):
        count = collect(own, own_list)
        if distance == 0:

            @pl.loop(0, count)
            def _(i):
                add(visit(own_list, i, count, donors, own_accept, True))

        else:
            far_count = collect(far, far_list)

            @pl.loop(0, jnp.maximum(count, far_count))
            def _(i):
                mine = visit(own_list, i, count, donors, far_accept, True)
                theirs = visit(far_list, i, far_count, far_donor, own_accept, False)
                add(mine)
                add(theirs)

    pl.when(flag[0] > 0)(lambda: run(second0, first0, first1, second1))
    pl.when(flag[0] <= 0)(lambda: run(first0, second0, second1, first1))


def relative(target, y, first):
    code = (target ^ (target >> 1)) ^ (y ^ (y >> 1))
    low, high = code & 1, code >> 1
    return low * 2 + high if first == 0 else high * 2 + low


def tap_grad_kernel(
    place, d_donor, d_accept, point, donor_w, accept_w, slope, hidden_t,
    keep, send, d_conv, d_feat,
):
    rows, heads = d_donor.shape
    channels = hidden_t.shape[0]

    dd = d_donor[...].astype(BF16)
    da = d_accept[...].astype(BF16)
    d_feat[:, :heads] = dd
    d_feat[:, heads:] = da
    d_embed = (dot_t(dd, donor_w[...]) + dot_t(da, accept_w[...])).astype(BF16)
    d_conv[...] = (dot_t(d_embed, point[...]) * slope[...]).astype(BF16)

    lanes = d_conv.shape[1] // 128
    half_rows = channels // 2
    slab = [relative(target, place[1], 1) for target in range(4)]
    for tap in range(3):
        for half in range(2):
            part = dot(
                hidden_t[half * half_rows : (half + 1) * half_rows, tap * STEP : tap * STEP + rows],
                d_conv[...],
            ).astype(BF16)

            def store(into, part=part, tap=tap):
                for k in range(4):
                    for lane in range(lanes):
                        into[slab[k], tap * lanes + lane] = part[
                            k * PIECE : (k + 1) * PIECE, lane * 128 : (lane + 1) * 128
                        ]

            pl.when(place[0] == half)(lambda: store(keep))
            pl.when(place[0] != half)(lambda: store(send))


def head_grad_kernel(
    place, d_conv, d_feat, loss, taps, factor, edge_factor, act_t, embed_t, head_sum,
):
    rows = d_conv.shape[0]
    channels = embed_t.shape[0]
    inner = act_t.shape[0]
    slab = [relative(target, place[1], 0) for target in range(4)]

    def put(part, base, group_rows, first):
        for lane in range(4):
            for k in range(part.shape[0] // PIECE):
                piece = first + lane * (group_rows // PIECE) + k + base
                chunk, third = piece // 3, piece % 3
                head_sum[slab[chunk // 4], chunk % 4, third * PIECE : (third + 1) * PIECE, :] = part[
                    k * PIECE : (k + 1) * PIECE, lane * 128 : (lane + 1) * 128
                ]

    for i in range(2):
        part = dot(embed_t[i * 4 * PIECE : (i + 1) * 4 * PIECE, :], d_feat[...]).astype(BF16)
        put(part, 4 * i, channels, 0)
    put(dot(act_t[...], d_feat[...]).astype(BF16), 0, inner, 4 * channels // PIECE)

    total = jnp.zeros((8, channels), F32)
    edge = edge_factor.shape[0] // 2
    for tap in range(taps.shape[0]):
        product = dot_t(d_conv[...], taps[tap])
        if tap == 0:
            weights = jnp.concatenate([edge_factor[:edge, :], factor[: rows - edge, :]], axis=0)
        elif tap == 1:
            weights = factor[...]
        else:
            weights = jnp.concatenate([factor[edge:, :], edge_factor[edge:, :]], axis=0)
        product = product * weights.astype(F32)
        total = total + jnp.sum(product.reshape(rows // 8, 8, channels), axis=0)
    gain = jnp.sum(total, axis=0, keepdims=True)
    loss_row = jnp.sum(loss[...], axis=0, keepdims=True) * LOSS_WEIGHT
    loss_all = jnp.broadcast_to(jnp.sum(loss_row, axis=1, keepdims=True), (1, 128))
    at_row = lax.broadcasted_iota(jnp.int32, (EXTRA_ROWS, 128), 0)
    for chunk in range(16):
        if chunk < channels // 128:
            value = gain[:, chunk * 128 : (chunk + 1) * 128]
        elif chunk == channels // 128:
            value = loss_all
        else:
            value = jnp.zeros((1, 128), F32)
        coarse = value.astype(BF16).astype(F32)
        block = jnp.where(at_row == 0, coarse, 0.0) + jnp.where(at_row == 8, value - coarse, 0.0)
        head_sum[slab[chunk // 4], chunk % 4, CHUNK_ROWS:, :] = block.astype(BF16)


def split_rows(total):
    value = total[CHUNK_ROWS : CHUNK_ROWS + 8] + total[CHUNK_ROWS + 8 : CHUNK_ROWS + 16]
    coarse = value.astype(BF16).astype(F32)
    return jnp.concatenate([total[:CHUNK_ROWS], coarse, value - coarse], axis=0).astype(BF16)


def core_sum_kernel(taps, received, kept, send):
    for k in range(2):
        for slab in range(taps.shape[1]):
            kept[k, slab] = taps[k, slab].astype(F32) + received[k, slab].astype(F32)
            send[k, slab] = (
                taps[k + 2, slab].astype(F32) + received[k + 2, slab].astype(F32)
            ).astype(BF16)


def head_sum_kernel(head, received, kept, send):
    for zq in range(4):
        kept[zq] = head[0, zq].astype(F32) + received[0, zq].astype(F32)
        send[zq] = split_rows(head[1, zq].astype(F32) + received[1, zq].astype(F32))


def tap_sum_kernel(before, received, kept, send):
    for slab in range(before.shape[1]):
        kept[slab] = before[0, slab] + received[0, slab].astype(F32)
        send[slab] = (before[1, slab] + received[1, slab].astype(F32)).astype(BF16)


def join_kernel(head, head_in, taps, taps_in, both):
    chunk_rows = head.shape[1]
    for zq in range(4):
        both[zq, :chunk_rows, :] = split_rows(head[zq] + head_in[zq].astype(F32))
        here = slice(zq * 24, (zq + 1) * 24)
        parts = [taps[k, here] + taps_in[k, here].astype(F32) for k in range(taps.shape[0])]
        parts.append(jnp.zeros((8, 128), F32))
        both[zq, chunk_rows:, :] = jnp.concatenate(parts, axis=0).astype(BF16)


def line_sum_kernel(place, parts, pick, send, mine):
    total = parts[0].astype(F32)
    for zq in range(1, 4):
        total = total + parts[zq].astype(F32)
    chunk_rows = CHUNK_ROWS + EXTRA_ROWS
    send[:chunk_rows, :] = split_rows(total[:chunk_rows])
    taps = total[chunk_rows:].astype(BF16)
    half = mine.shape[0]
    zb = place[2]

    def picked(which):
        return dot(pick[pl.ds(pl.multiple_of(which * half, half), half), :], taps).astype(BF16)

    send[chunk_rows:, :] = picked(1 - zb)
    mine[...] = picked(zb)


def far_sum_kernel(sent, received, mine, head, taps):
    chunk_rows = head.shape[1]
    total = split_rows(sent[:chunk_rows, :].astype(F32) + received[:chunk_rows, :].astype(F32))
    for zq in range(head.shape[0]):
        head[zq] = total
    taps[...] = (mine[...].astype(F32) + received[chunk_rows:, :].astype(F32)).astype(BF16)


def line_total_kernel(own, one, two, three, parts):
    even = own[...].astype(F32) + two[...].astype(F32)
    total = (even + (one[...].astype(F32) + three[...].astype(F32))).astype(BF16)
    for k in range(parts.shape[0]):
        parts[k] = total


def finish_kernel(
    place, own, behind, ahead, low, high, donor_w, accept_w,
    grad_donor, grad_accept, grad_point, gain, loss, held, act_donor, act_accept,
):
    count = held.shape[0]
    for step, part in ((0, own), (3, behind), (1, ahead)):
        held[lax.rem(place[1] + step, count)] = part[...]
    opposite = lax.rem(place[1] + 2, count)
    middle = low.shape[0]
    held[opposite, :middle, :] = low[...]
    held[opposite, middle:, :] = high[...]
    channels = grad_donor.shape[0]
    inner = act_donor.shape[0]
    chunk_rows = CHUNK_ROWS + EXTRA_ROWS
    piece = 0
    for into in (grad_donor, grad_accept, act_donor, act_accept):
        for lane in range(2):
            for k in range(into.shape[0] // PIECE):
                chunk, third = piece // 3, piece % 3
                at = (chunk % 4) * chunk_rows + third * PIECE
                into[k * PIECE : (k + 1) * PIECE, lane * 128 : (lane + 1) * 128] = held[
                    chunk // 4, at : at + PIECE, :
                ]
                piece += 1

    grad_point[...] = (
        dot_t(act_donor[...], donor_w[...]) + dot_t(act_accept[...], accept_w[...])
    ).astype(BF16)

    for chunk in range(channels // 128 + 1):
        at = (chunk % 4) * chunk_rows + CHUNK_ROWS
        block = held[chunk // 4, at : at + EXTRA_ROWS, :].astype(F32)
        value = block[0:1, :] + block[8:9, :]
        if chunk < channels // 128:
            gain[:, chunk * 128 : (chunk + 1) * 128] = value
        else:
            loss[...] = value


def swapped(block, first):
    count = lax.axis_size(SEQ)
    pairs = [(i, i + 1) for i in range(first, count - 1, 2)]
    return lax.ppermute(block, SEQ, pairs + [(j, i) for i, j in pairs])


def swap_parts(parts, axis):
    return lax.all_to_all(parts, axis, 0, 0, tiled=True)


def on_device(
    activations, norm_gain, dilated_tap_weight, point_weight, donor_weight, acceptor_weight,
    pair_sites, pair_count, order, eye, pick,
):
    tokens = activations[0]
    rows, channels = tokens.shape
    tap_count, _, inner = dilated_tap_weight.shape
    heads = donor_weight.shape[1]
    blocks = rows // PANEL
    shape = jax.ShapeDtypeStruct
    here = lax.axis_index(SEQ)
    odd = (here % 2).astype(jnp.int32)[None]
    is_odd = odd[0] > 0
    start, end = tokens[:STEP], tokens[rows - STEP :]
    even_edge = swapped(jnp.where(is_odd, start, end), 0)
    odd_edge = swapped(jnp.where(is_odd, end, start), 1)
    gain = norm_gain[None]
    sites = pair_sites[0]
    first = here * blocks
    live = (jnp.arange(SLOTS, dtype=jnp.int32) < pair_count[0, 0]).astype(jnp.int32)
    meta = jnp.stack(
        [
            sites[:, 0] // PANEL - first,
            sites[:, 0] % PANEL,
            sites[:, 1] // PANEL - first,
            sites[:, 1] % PANEL,
            live,
        ]
        + [jnp.zeros_like(live)] * 3,
        axis=1,
    )
    meta_rows = jnp.pad(meta.astype(BF16), ((0, 0), (0, heads - meta.shape[1])))

    mine, factor = call(
        own_kernel, [shape((rows, channels), BF16)] * 2, [VM] * 2, 12, 2_000_000_000
    )(tokens, gain)
    feat = shape((rows + SLOTS, heads), BF16)
    hidden, conv, act, embed, even_feat, odd_feat = call(
        forward_kernel,
        [
            shape((rows + 2 * STEP, channels), BF16),
            shape((rows, inner), F32),
            shape((rows, inner), BF16),
            shape((rows, channels), BF16),
            feat,
            feat,
        ],
        [SM] + [VM] * 10,
        20,
        4_000_000_000,
    )(
        odd, tokens, mine, even_edge, odd_edge, gain, dilated_tap_weight, point_weight,
        donor_weight, acceptor_weight, meta_rows,
    )

    lists = [pltpu.SMEM((SLOTS, 4), jnp.int32)] * 2
    acc_shapes = [shape((rows, heads), F32), shape((rows, heads), F32), shape((PANEL, PANEL), F32)]
    acc = call(
        lambda *refs: pair_kernel(0, *refs), acc_shapes, [SM] * 2 + [VM] * 2, 12, 2_000_000_000, lists
    )(1 - odd, meta, even_feat, odd_feat)
    def pairs_at(distance, short_far, long_far, acc):
        far_meta = jnp.where(is_odd, short_far[rows:, :8], long_far[rows:, :8]).astype(jnp.int32)
        return call(
            lambda *refs: pair_kernel(distance, *refs), acc_shapes, [SM] * 3 + [VM] * 7, 12, 2_500_000_000,
            lists,
        )(1 - odd, meta, far_meta, even_feat, odd_feat, long_far, short_far, *acc)

    barrier = lax.optimization_barrier
    short1 = swapped(odd_feat, 0)
    late_feat, acc = barrier((even_feat, acc))
    long1 = swapped(late_feat, 1)
    long2 = swapped(short1, 1)
    conv, _ = barrier((conv, short1))
    edge_factor, slope, hidden_t, act_t, embed_t = call(
        side_kernel,
        [
            shape((2 * STEP, channels), BF16),
            shape((rows, inner), F32),
            shape((channels, rows + 2 * STEP), BF16),
            shape((inner, rows), BF16),
            shape((channels, rows), BF16),
        ],
        [SM] + [VM] * 9,
        20,
        6_000_000_000,
    )(odd, even_edge, odd_edge, gain, hidden, conv, act, embed, order, eye)
    short2 = swapped(long1, 0)
    acc = pairs_at(1, short1, long1, acc)
    short3, long3 = swapped(long2, 0), swapped(short2, 1)
    _, acc = barrier((short3, tuple(acc)))
    acc = pairs_at(2, short2, long2, acc)
    short4, long4 = swapped(long3, 0), swapped(short3, 1)
    acc = pairs_at(3, short3, long3, acc)
    acc = pairs_at(4, short4, long4, acc)

    chunk = CHUNK_ROWS + EXTRA_ROWS
    lanes = inner // 128
    slabs = tap_count * lanes
    y = lax.axis_index("y")
    place = jnp.stack([lax.axis_index("core"), y, lax.axis_index("zb")]).astype(jnp.int32)
    half = shape((4, slabs, PIECE, 128), BF16)
    keep, send, d_conv, d_feat = call(
        tap_grad_kernel,
        [half, half, shape((rows, inner), BF16), shape((rows, 2 * heads), BF16)],
        [SM] + [VM] * 7,
        24,
        4_000_000_000,
    )(place, acc[0], acc[1], point_weight, donor_weight, acceptor_weight, slope, hidden_t)
    received = lax.ppermute(send, "core", [(0, 1), (1, 0)])
    (head_sum,) = call(
        head_grad_kernel, [shape((4, 4, chunk, 128), BF16)], [SM] + [VM] * 8, 20, 4_000_000_000
    )(place, d_conv, d_feat, acc[2], dilated_tap_weight, factor, edge_factor, act_t, embed_t)

    first_pairs = [(0, 1), (1, 0), (2, 3), (3, 2)]
    second_pairs = [(1, 2), (2, 1), (3, 0), (0, 3)]
    quick = 1_000_000
    conv_kept, conv_send = call(
        core_sum_kernel, [shape((2, slabs, PIECE, 128), F32), shape((2, slabs, PIECE, 128), BF16)],
        [VM] * 2, 12, quick,
    )(keep, received)
    other = lax.ppermute(head_sum[2:], "y", first_pairs)
    heads_kept, heads_send = call(
        head_sum_kernel, [shape((4, chunk, 128), F32), shape((4, chunk, 128), BF16)], [VM] * 2, 12, quick
    )(head_sum, other)
    other = lax.ppermute(conv_send, "y", second_pairs)
    conv_kept, conv_send = call(
        tap_sum_kernel, [shape((slabs, PIECE, 128), F32), shape((slabs, PIECE, 128), BF16)],
        [VM] * 2, 12, quick,
    )(conv_kept, other)
    heads_in = lax.ppermute(heads_send, "y", second_pairs)
    conv_in = lax.ppermute(conv_send, "y", first_pairs)

    joint = chunk + 224
    (both,) = call(join_kernel, [shape((4, joint, 128), BF16)], [VM] * 4, 12, quick)(
        heads_kept, heads_in, conv_kept, conv_in
    )
    parts = swap_parts(both, "zq")
    sent, mine = call(
        line_sum_kernel, [shape((chunk + 112, 128), BF16), shape((112, 128), BF16)],
        [SM] + [VM] * 2, 8, quick,
    )(place, parts, pick)
    received = lax.ppermute(sent, "zb", [(0, 1), (1, 0)])
    head_parts, conv_sum = call(
        far_sum_kernel, [shape((4, chunk, 128), BF16), shape((112, 128), BF16)], [VM] * 3, 8, quick
    )(sent, received, mine)

    head_rows = 4 * chunk
    head_sum = swap_parts(head_parts, "zq").reshape(head_rows, 128)
    line = [
        lax.ppermute(conv_sum, "x", [(i, (i + step) % 4) for i in range(4)]) for step in (1, 2, 3)
    ]
    (conv_sum,) = call(line_total_kernel, [shape((4, 112, 128), BF16)], [VM] * 4, 8, quick)(conv_sum, *line)
    head_sum, conv_sum = lax.optimization_barrier((head_sum, conv_sum))
    around = [(i, (i + 1) % 4) for i in range(4)]
    back = [(j, i) for i, j in around]
    behind = lax.ppermute(head_sum, "y", around)
    ahead = lax.ppermute(head_sum, "y", back)
    low = lax.ppermute(behind[: head_rows // 2], "y", around)
    high = lax.ppermute(ahead[head_rows // 2 :], "y", back)
    pieces = swap_parts(conv_sum, ("zhi", "core")).astype(F32).reshape(2, 2, 112, 128)
    pieces = pieces[0] + pieces[1]
    pieces = pieces[:, : slabs * 12].reshape(2, tap_count, lanes, 12, 128)
    grad_conv = pieces.transpose(1, 0, 3, 2, 4).reshape(tap_count, 24, inner)
    head_weight = shape((channels, heads), BF16)
    grad_donor, grad_accept, grad_point, grad_gain, loss = call(
        finish_kernel,
        [head_weight, head_weight, shape((inner, channels), BF16), shape((1, channels), F32), shape((1, 128), F32)],
        [SM] + [VM] * 7,
        20,
        1_000_000_000,
        [
            pltpu.VMEM((4, head_rows, 128), BF16),
            pltpu.VMEM((inner, heads), BF16),
            pltpu.VMEM((inner, heads), BF16),
        ],
    )(place, head_sum, behind, ahead, low, high, donor_weight, acceptor_weight)
    return grad_conv, grad_point[None], grad_donor[None], grad_accept[None], grad_gain, loss[0, :1]


def channel_order():
    core, y, zq, zb, k = np.meshgrid(*[np.arange(n) for n in (2, 4, 4, 2, 12)], indexing="ij")
    channel = (24 * (8 * y + 4 * zb + zq) + 12 * core + k).reshape(-1)
    return np.eye(channel.size, dtype=np.float32)[channel]


def zb_halves():
    pick = np.zeros((224, 224), np.float32)
    for zb in range(2):
        for slab in range(9):
            for k in range(12):
                pick[112 * zb + 12 * slab + k, 24 * slab + 12 * zb + k] = 1.0
    return pick


def solution(mesh):
    fine = Mesh(mesh.devices.reshape(4, 2, 4, 2, 4, 2), SEQ + BATCH)
    placed = jax.shard_map(
        on_device,
        mesh=fine,
        in_specs=(
            P(BATCH, SEQ, None),
            P(),
            P(),
            P(),
            P(),
            P(),
            P(BATCH, SEQ, None),
            P(BATCH, SEQ),
            P(),
            P(),
            P(),
        ),
        out_specs=(
            P(None, SEQ, None),
            P(BATCH, None, None),
            P(BATCH, None, None),
            P(BATCH, None, None),
            P(BATCH, None),
            P(BATCH),
        ),
        check_vma=False,
    )

    def run(*arrays):
        order = jnp.asarray(channel_order(), BF16)
        eye = jnp.eye(order.shape[0], dtype=BF16)
        return placed(*arrays, order, eye, jnp.asarray(zb_halves(), BF16))

    return run
```

```python
import jax
import jax.numpy as jnp
import numpy as np
from jax import lax
from jax.experimental import pallas as pl
from jax.experimental.pallas import tpu as pltpu
from jax.sharding import Mesh
from jax.sharding import PartitionSpec as P

STEP = 128
PANEL = 128
SPAN = 4
SLOTS = 16
EPSILON = 1e-06
LOSS_WEIGHT = 1.0 / 128.0
SEQ = ("y", "zb", "zq")
BATCH = ("zhi", "x", "core")
F32 = jnp.float32
BF16 = jnp.bfloat16
ROOT = 0.7978845608028654
CUBIC = 0.044715
PIECE = 96
CHUNK_ROWS = 288
EXTRA_ROWS = 16


def dot(a, b):
    return lax.dot_general(a, b, (((1,), (0,)), ((), ())), preferred_element_type=F32)


def dot_t(a, b):
    return lax.dot_general(a, b, (((1,), (1,)), ((), ())), preferred_element_type=F32)


def gelu(v):
    return 0.5 * v * (1.0 + jnp.tanh(ROOT * (v + CUBIC * (v * v * v))))


def gelu_both(v):
    square = v * v
    t = jnp.tanh(ROOT * (v + CUBIC * (square * v)))
    half = 0.5 * (1.0 + t)
    return v * half, half + 0.5 * v * (1.0 - t * t) * (ROOT * (1.0 + 3.0 * CUBIC * square))


def rms(v):
    return lax.rsqrt(jnp.mean(v * v, axis=-1, keepdims=True) + EPSILON)


def call(kernel, outs, specs, megabytes, flops, scratch=()):
    return pl.pallas_call(
        kernel,
        out_shape=outs,
        in_specs=specs,
        out_specs=[VM] * len(outs),
        scratch_shapes=list(scratch),
        compiler_params=pltpu.CompilerParams(vmem_limit_bytes=megabytes * 1024 * 1024),
        cost_estimate=pl.CostEstimate(flops=flops, bytes_accessed=1_000_000, transcendentals=0),
    )


VM = pl.BlockSpec(memory_space=pltpu.VMEM)
SM = pl.BlockSpec(memory_space=pltpu.SMEM)


def own_kernel(tok, gain, hidden, factor):
    @pl.loop(0, tok.shape[0] // STEP)
    def _(i):
        here = pl.ds(pl.multiple_of(i * STEP, STEP), STEP)
        v = tok[here, :].astype(F32)
        unit = v * rms(v)
        value, slope = gelu_both(unit * gain[...])
        hidden[here, :] = value.astype(BF16)
        factor[here, :] = (slope * unit).astype(BF16)


def forward_kernel(
    odd, tok, mine, even_edge, odd_edge, gain, taps, point, donor_w, accept_w, meta,
    hidden, conv_out, act_out, embed_out, even_feat, odd_feat, wide_feat,
):
    rows = tok.shape[0]
    is_odd = odd[0] > 0
    low = jnp.where(is_odd, even_edge[...], odd_edge[...])
    high = jnp.where(is_odd, odd_edge[...], even_edge[...])
    for edge, at in ((low, 0), (high, STEP + rows)):
        v = edge.astype(F32)
        hidden[pl.ds(at, STEP), :] = gelu(v * rms(v) * gain[...]).astype(BF16)
    hidden[pl.ds(STEP, rows), :] = mine[...]

    conv = dot(hidden[:rows, :], taps[0])
    for tap in range(1, taps.shape[0]):
        conv = conv + dot(hidden[tap * STEP : tap * STEP + rows, :], taps[tap])
    conv_out[...] = conv
    act = gelu(conv).astype(BF16)
    act_out[...] = act
    embed = (tok[...].astype(F32) + dot(act, point[...])).astype(BF16)
    embed_out[...] = embed
    donor = dot(embed, donor_w[...]).astype(BF16)
    accept = dot(embed, accept_w[...]).astype(BF16)
    even_feat[:rows, :] = jnp.where(is_odd, donor, accept)
    odd_feat[:rows, :] = jnp.where(is_odd, accept, donor)
    wide_feat[:rows, :] = jnp.where(odd[1] < 4, accept, donor)
    even_feat[pl.ds(rows, SLOTS), :] = meta[...]
    odd_feat[pl.ds(rows, SLOTS), :] = meta[...]
    wide_feat[pl.ds(rows, SLOTS), :] = meta[...]


def side_kernel(
    odd, even_edge, odd_edge, gain, hidden, conv, act, embed, order, eye,
    factor, slope, hidden_t, act_t, embed_t,
):
    is_odd = odd[0] > 0
    low = jnp.where(is_odd, even_edge[...], odd_edge[...])
    high = jnp.where(is_odd, odd_edge[...], even_edge[...])
    for edge, at in ((low, 0), (high, STEP)):
        v = edge.astype(F32)
        unit = v * rms(v)
        factor[pl.ds(at, STEP), :] = (gelu_both(unit * gain[...])[1] * unit).astype(BF16)

    @pl.loop(0, conv.shape[0] // STEP)
    def _(i):
        here = pl.ds(pl.multiple_of(i * STEP, STEP), STEP)
        slope[here, :] = gelu_both(conv[here, :])[1]

    hidden_t[...] = dot_t(order[...], hidden[...]).astype(BF16)
    embed_t[...] = dot_t(eye[...], embed[...]).astype(BF16)
    inner = act.shape[1]
    act_t[...] = dot_t(eye[:inner, :inner], act[...]).astype(BF16)


def pair_kernel(distance, *refs):
    if distance == 0:
        odd, own, even0, odd0, d_donor, d_accept, loss = refs
        d_donor[...] = jnp.zeros_like(d_donor)
        d_accept[...] = jnp.zeros_like(d_accept)
        loss[...] = jnp.zeros_like(loss)
    else:
        odd, own, far, even0, odd0, even1, odd1, dd_in, da_in, loss_in, d_donor, d_accept, loss = refs
        d_donor[...] = dd_in[...]
        d_accept[...] = da_in[...]
        loss[...] = loss_in[...]
    is_odd = odd[0] > 0
    scale = even0.shape[1] ** (-0.5)
    per_device = d_donor.shape[0] // PANEL
    row = lax.broadcasted_iota(jnp.int32, (PANEL, PANEL), 0)
    col = lax.broadcasted_iota(jnp.int32, (PANEL, PANEL), 1)

    def place(block):
        return pl.ds(pl.multiple_of(block * PANEL, PANEL), PANEL)

    def own_donor(block):
        return jnp.where(is_odd, odd0[place(block), :], even0[place(block), :])

    def own_accept(block):
        return jnp.where(is_odd, even0[place(block), :], odd0[place(block), :])

    if distance == 0:
        far_accept, far_donor = own_accept, None
    else:

        def far_accept(block):
            return jnp.where(is_odd, odd1[place(block), :], even1[place(block), :])

        def far_donor(block):
            return jnp.where(is_odd, even1[place(block), :], odd1[place(block), :])

    def visit(meta, j, donors, acceptors, is_owner):
        accept_block = meta[j, 2] - distance * per_device
        here = (meta[j, 4] > 0) & (accept_block >= 0) & (accept_block < per_device)

        @pl.when(here)
        def _():
            donor_block = meta[j, 0]
            dpan = donors(donor_block)
            apan = acceptors(accept_block)
            scores = dot_t(dpan, apan) * scale
            target = ((row == meta[j, 1]) & (col == meta[j, 3])).astype(F32)
            small = jnp.exp(-jnp.abs(scores))
            inverse = 1.0 / (1.0 + small)
            sigmoid = jnp.where(scores >= 0, inverse, small * inverse)
            dscore = ((sigmoid - target) * LOSS_WEIGHT).astype(BF16)
            if is_owner:
                loss[...] += (jnp.maximum(scores, 0.0) + jnp.log1p(small)) - target * scores
                d_donor[place(donor_block), :] += dot(dscore, apan) * scale
            if distance == 0 or not is_owner:
                d_accept[place(accept_block), :] += scale * lax.dot_general(
                    dscore, dpan, (((0,), (0,)), ((), ())), preferred_element_type=F32
                )

    @pl.loop(0, SLOTS)
    def _(j):
        visit(own, j, own_donor, far_accept, True)
        if distance > 0:
            visit(far, j, far_donor, own_accept, False)


def relative(target, y, first):
    code = (target ^ (target >> 1)) ^ (y ^ (y >> 1))
    low, high = code & 1, code >> 1
    return low * 2 + high if first == 0 else high * 2 + low


def tap_grad_kernel(
    place, d_donor, d_accept, point, donor_w, accept_w, slope, hidden_t,
    keep, send, d_conv, d_feat,
):
    rows, heads = d_donor.shape
    channels = hidden_t.shape[0]

    dd = d_donor[...].astype(BF16)
    da = d_accept[...].astype(BF16)
    d_feat[:, :heads] = dd
    d_feat[:, heads:] = da
    d_embed = (dot_t(dd, donor_w[...]) + dot_t(da, accept_w[...])).astype(BF16)
    d_conv[...] = (dot_t(d_embed, point[...]) * slope[...]).astype(BF16)

    lanes = d_conv.shape[1] // 128
    half_rows = channels // 2
    slab = [relative(target, place[1], 1) for target in range(4)]
    for tap in range(3):
        for half in range(2):
            part = dot(
                hidden_t[half * half_rows : (half + 1) * half_rows, tap * STEP : tap * STEP + rows],
                d_conv[...],
            ).astype(BF16)

            def store(into, part=part, tap=tap):
                for k in range(4):
                    for lane in range(lanes):
                        into[slab[k], tap * lanes + lane] = part[
                            k * PIECE : (k + 1) * PIECE, lane * 128 : (lane + 1) * 128
                        ]

            pl.when(place[0] == half)(lambda: store(keep))
            pl.when(place[0] != half)(lambda: store(send))


def head_grad_kernel(
    place, d_conv, d_feat, loss, taps, factor, edge_factor, act_t, embed_t, head_sum,
):
    rows = d_conv.shape[0]
    channels = embed_t.shape[0]
    inner = act_t.shape[0]
    slab = [relative(target, place[1], 0) for target in range(4)]

    def put(part, base, group_rows, first):
        for lane in range(4):
            for k in range(part.shape[0] // PIECE):
                piece = first + lane * (group_rows // PIECE) + k + base
                chunk, third = piece // 3, piece % 3
                head_sum[slab[chunk // 4], chunk % 4, third * PIECE : (third + 1) * PIECE, :] = part[
                    k * PIECE : (k + 1) * PIECE, lane * 128 : (lane + 1) * 128
                ]

    for i in range(2):
        part = dot(embed_t[i * 4 * PIECE : (i + 1) * 4 * PIECE, :], d_feat[...]).astype(BF16)
        put(part, 4 * i, channels, 0)
    put(dot(act_t[...], d_feat[...]).astype(BF16), 0, inner, 4 * channels // PIECE)

    total = jnp.zeros((8, channels), F32)
    edge = edge_factor.shape[0] // 2
    for tap in range(taps.shape[0]):
        product = dot_t(d_conv[...], taps[tap])
        if tap == 0:
            weights = jnp.concatenate([edge_factor[:edge, :], factor[: rows - edge, :]], axis=0)
        elif tap == 1:
            weights = factor[...]
        else:
            weights = jnp.concatenate([factor[edge:, :], edge_factor[edge:, :]], axis=0)
        product = product * weights.astype(F32)
        total = total + jnp.sum(product.reshape(rows // 8, 8, channels), axis=0)
    gain = jnp.sum(total, axis=0, keepdims=True)
    loss_row = jnp.sum(loss[...], axis=0, keepdims=True) * LOSS_WEIGHT
    loss_all = jnp.broadcast_to(jnp.sum(loss_row, axis=1, keepdims=True), (1, 128))
    at_row = lax.broadcasted_iota(jnp.int32, (EXTRA_ROWS, 128), 0)
    for chunk in range(16):
        if chunk < channels // 128:
            value = gain[:, chunk * 128 : (chunk + 1) * 128]
        elif chunk == channels // 128:
            value = loss_all
        else:
            value = jnp.zeros((1, 128), F32)
        coarse = value.astype(BF16).astype(F32)
        block = jnp.where(at_row == 0, coarse, 0.0) + jnp.where(at_row == 8, value - coarse, 0.0)
        head_sum[slab[chunk // 4], chunk % 4, CHUNK_ROWS:, :] = block.astype(BF16)


def split_rows(total):
    value = total[CHUNK_ROWS : CHUNK_ROWS + 8] + total[CHUNK_ROWS + 8 : CHUNK_ROWS + 16]
    coarse = value.astype(BF16).astype(F32)
    return jnp.concatenate([total[:CHUNK_ROWS], coarse, value - coarse], axis=0).astype(BF16)


def core_sum_kernel(taps, received, kept, send):
    for k in range(2):
        for slab in range(taps.shape[1]):
            kept[k, slab] = taps[k, slab].astype(F32) + received[k, slab].astype(F32)
            send[k, slab] = (
                taps[k + 2, slab].astype(F32) + received[k + 2, slab].astype(F32)
            ).astype(BF16)


def head_sum_kernel(head, received, kept, send):
    for zq in range(4):
        kept[zq] = head[0, zq].astype(F32) + received[0, zq].astype(F32)
        send[zq] = split_rows(head[1, zq].astype(F32) + received[1, zq].astype(F32))


def tap_sum_kernel(before, received, kept, send):
    for slab in range(before.shape[1]):
        kept[slab] = before[0, slab] + received[0, slab].astype(F32)
        send[slab] = (before[1, slab] + received[1, slab].astype(F32)).astype(BF16)


def join_kernel(head, head_in, taps, taps_in, both):
    chunk_rows = head.shape[1]
    for zq in range(4):
        both[zq, :chunk_rows, :] = split_rows(head[zq] + head_in[zq].astype(F32))
        here = slice(zq * 24, (zq + 1) * 24)
        parts = [taps[k, here] + taps_in[k, here].astype(F32) for k in range(taps.shape[0])]
        parts.append(jnp.zeros((8, 128), F32))
        both[zq, chunk_rows:, :] = jnp.concatenate(parts, axis=0).astype(BF16)


def line_sum_kernel(place, parts, pick, send, mine):
    total = parts[0].astype(F32)
    for zq in range(1, 4):
        total = total + parts[zq].astype(F32)
    chunk_rows = CHUNK_ROWS + EXTRA_ROWS
    send[:chunk_rows, :] = split_rows(total[:chunk_rows])
    taps = total[chunk_rows:].astype(BF16)
    half = mine.shape[0]
    zb = place[2]

    def picked(which):
        return dot(pick[pl.ds(pl.multiple_of(which * half, half), half), :], taps).astype(BF16)

    send[chunk_rows:, :] = picked(1 - zb)
    mine[...] = picked(zb)


def far_sum_kernel(sent, received, mine, one, two, head, taps):
    chunk_rows = head.shape[1]
    total = split_rows(sent[:chunk_rows, :].astype(F32) + received[:chunk_rows, :].astype(F32))
    for zq in range(head.shape[0]):
        head[zq] = total
    near = mine[...].astype(F32) + received[chunk_rows:, :].astype(F32)
    taps[...] = (near + (one[...].astype(F32) + two[...].astype(F32))).astype(BF16)


def line_total_kernel(own, one, two, three, total):
    even = own[...].astype(F32) + two[...].astype(F32)
    total[...] = even + (one[...].astype(F32) + three[...].astype(F32))


def finish_kernel(
    place, own, behind, ahead, low, high, donor_w, accept_w,
    grad_donor, grad_accept, grad_point, gain, loss, held, act_donor, act_accept,
):
    count = held.shape[0]
    for step, part in ((0, own), (3, behind), (1, ahead)):
        held[lax.rem(place[1] + step, count)] = part[...]
    opposite = lax.rem(place[1] + 2, count)
    middle = low.shape[0]
    held[opposite, :middle, :] = low[...]
    held[opposite, middle:, :] = high[...]
    channels = grad_donor.shape[0]
    inner = act_donor.shape[0]
    chunk_rows = CHUNK_ROWS + EXTRA_ROWS
    piece = 0
    for into in (grad_donor, grad_accept, act_donor, act_accept):
        for lane in range(2):
            for k in range(into.shape[0] // PIECE):
                chunk, third = piece // 3, piece % 3
                at = (chunk % 4) * chunk_rows + third * PIECE
                into[k * PIECE : (k + 1) * PIECE, lane * 128 : (lane + 1) * 128] = held[
                    chunk // 4, at : at + PIECE, :
                ]
                piece += 1

    grad_point[...] = (
        dot_t(act_donor[...], donor_w[...]) + dot_t(act_accept[...], accept_w[...])
    ).astype(BF16)

    for chunk in range(channels // 128 + 1):
        at = (chunk % 4) * chunk_rows + CHUNK_ROWS
        block = held[chunk // 4, at : at + EXTRA_ROWS, :].astype(F32)
        value = block[0:1, :] + block[8:9, :]
        if chunk < channels // 128:
            gain[:, chunk * 128 : (chunk + 1) * 128] = value
        else:
            loss[...] = value


def swapped(block, first, between_lines=True):
    count = lax.axis_size(SEQ)
    pairs = [(i, i + 1) for i in range(first, count - 1, 2) if between_lines or i % 8 < 7]
    return lax.ppermute(block, SEQ, pairs + [(j, i) for i, j in pairs])


def swap_parts(parts, axis):
    return lax.all_to_all(parts, axis, 0, 0, tiled=True)


def on_device(
    activations, norm_gain, dilated_tap_weight, point_weight, donor_weight, acceptor_weight,
    pair_sites, pair_count, order, eye, pick,
):
    tokens = activations[0]
    rows, channels = tokens.shape
    tap_count, _, inner = dilated_tap_weight.shape
    heads = donor_weight.shape[1]
    blocks = rows // PANEL
    shape = jax.ShapeDtypeStruct
    here = lax.axis_index(SEQ)
    line = here % 8
    odd = jnp.stack([here % 2, line]).astype(jnp.int32)
    is_odd = odd[0] > 0
    start, end = tokens[:STEP], tokens[rows - STEP :]
    even_edge = swapped(jnp.where(is_odd, start, end), 0)
    odd_edge = swapped(jnp.where(is_odd, end, start), 1)
    gain = norm_gain[None]
    sites = pair_sites[0]
    first = here * blocks
    live = (jnp.arange(SLOTS, dtype=jnp.int32) < pair_count[0, 0]).astype(jnp.int32)
    meta = jnp.stack(
        [
            sites[:, 0] // PANEL - first,
            sites[:, 0] % PANEL,
            sites[:, 1] // PANEL - first,
            sites[:, 1] % PANEL,
            live,
        ]
        + [jnp.zeros_like(live)] * 3,
        axis=1,
    )
    meta_rows = jnp.pad(meta.astype(BF16), ((0, 0), (0, heads - meta.shape[1])))

    mine, factor = call(
        own_kernel, [shape((rows, channels), BF16)] * 2, [VM] * 2, 12, 2_000_000_000
    )(tokens, gain)
    feat = shape((rows + SLOTS, heads), BF16)
    hidden, conv, act, embed, even_feat, odd_feat, wide_feat = call(
        forward_kernel,
        [
            shape((rows + 2 * STEP, channels), BF16),
            shape((rows, inner), F32),
            shape((rows, inner), BF16),
            shape((rows, channels), BF16),
            feat,
            feat,
            feat,
        ],
        [SM] + [VM] * 10,
        20,
        4_000_000_000,
    )(
        odd, tokens, mine, even_edge, odd_edge, gain, dilated_tap_weight, point_weight,
        donor_weight, acceptor_weight, meta_rows,
    )

    acc_shapes = [shape((rows, heads), F32), shape((rows, heads), F32), shape((PANEL, PANEL), F32)]
    acc = call(
        lambda *refs: pair_kernel(0, *refs), acc_shapes, [SM] * 2 + [VM] * 2, 12, 2_000_000_000
    )(1 - odd[:1], meta, even_feat, odd_feat)
    edge_factor, slope, hidden_t, act_t, embed_t = call(
        side_kernel,
        [
            shape((2 * STEP, channels), BF16),
            shape((rows, inner), F32),
            shape((channels, rows + 2 * STEP), BF16),
            shape((inner, rows), BF16),
            shape((channels, rows), BF16),
        ],
        [SM] + [VM] * 9,
        20,
        6_000_000_000,
    )(odd, even_edge, odd_edge, gain, hidden, conv, act, embed, order, eye)
    count = lax.axis_size(SEQ)
    starts = range(0, count, 8)
    wide_pairs = [(i + k, i - 4 + k) for i in starts if i > 0 for k in (2, 3)]
    wide_pairs += [(i + k, i + 4 + k) for i in starts if i + 8 < count for k in (4, 5)]
    relay_pairs = [(i + 6, i + 7) for i in starts] + [(i + 1, i) for i in starts]
    wide = lax.ppermute(wide_feat, SEQ, wide_pairs)
    relay = lax.ppermute(wide, SEQ, relay_pairs)
    at_end = (line == 0) | (line == 7)
    near_end = (line == 1) | (line == 6)
    short_far, long_far = odd_feat, even_feat
    for distance in range(1, SPAN + 1):
        if distance == 1:
            short_far, long_far = swapped(odd_feat, 0), swapped(even_feat, 1)
        else:
            short_far, long_far = swapped(long_far, 0), swapped(short_far, 1, distance <= 2)
        short_use, long_use = short_far, long_far
        if distance == 3:
            long_use = jnp.where(at_end, relay, long_far)
        if distance == 4:
            short_use = jnp.where(near_end, wide, short_far)
            long_use = jnp.where(at_end, wide, long_far)
        far_meta = jnp.where(odd[0] > 0, short_use[rows:, :8], long_use[rows:, :8]).astype(jnp.int32)
        acc = call(
            lambda *refs, distance=distance: pair_kernel(distance, *refs),
            acc_shapes,
            [SM] * 3 + [VM] * 7,
            12,
            2_500_000_000,
        )(1 - odd[:1], meta, far_meta, even_feat, odd_feat, long_use, short_use, *acc)

    chunk = CHUNK_ROWS + EXTRA_ROWS
    lanes = inner // 128
    slabs = tap_count * lanes
    y = lax.axis_index("y")
    place = jnp.stack([lax.axis_index("core"), y, lax.axis_index("zb")]).astype(jnp.int32)
    half = shape((4, slabs, PIECE, 128), BF16)
    keep, send, d_conv, d_feat = call(
        tap_grad_kernel,
        [half, half, shape((rows, inner), BF16), shape((rows, 2 * heads), BF16)],
        [SM] + [VM] * 7,
        24,
        4_000_000_000,
    )(place, acc[0], acc[1], point_weight, donor_weight, acceptor_weight, slope, hidden_t)
    received = lax.ppermute(send, "core", [(0, 1), (1, 0)])
    (head_sum,) = call(
        head_grad_kernel, [shape((4, 4, chunk, 128), BF16)], [SM] + [VM] * 8, 20, 4_000_000_000
    )(place, d_conv, d_feat, acc[2], dilated_tap_weight, factor, edge_factor, act_t, embed_t)

    first_pairs = [(0, 1), (1, 0), (2, 3), (3, 2)]
    second_pairs = [(1, 2), (2, 1), (3, 0), (0, 3)]
    quick = 1_000_000
    conv_kept, conv_send = call(
        core_sum_kernel, [shape((2, slabs, PIECE, 128), F32), shape((2, slabs, PIECE, 128), BF16)],
        [VM] * 2, 12, quick,
    )(keep, received)
    other = lax.ppermute(head_sum[2:], "y", first_pairs)
    heads_kept, heads_send = call(
        head_sum_kernel, [shape((4, chunk, 128), F32), shape((4, chunk, 128), BF16)], [VM] * 2, 12, quick
    )(head_sum, other)
    other = lax.ppermute(conv_send, "y", second_pairs)
    conv_kept, conv_send = call(
        tap_sum_kernel, [shape((slabs, PIECE, 128), F32), shape((slabs, PIECE, 128), BF16)],
        [VM] * 2, 12, quick,
    )(conv_kept, other)
    heads_in = lax.ppermute(heads_send, "y", second_pairs)
    conv_in = lax.ppermute(conv_send, "y", first_pairs)

    joint = chunk + 224
    (both,) = call(join_kernel, [shape((4, joint, 128), BF16)], [VM] * 4, 12, quick)(
        heads_kept, heads_in, conv_kept, conv_in
    )
    parts = swap_parts(both, "zq")
    sent, mine = call(
        line_sum_kernel, [shape((chunk + 112, 128), BF16), shape((112, 128), BF16)],
        [SM] + [VM] * 2, 8, quick,
    )(place, parts, pick)
    received = lax.ppermute(sent, "zb", [(0, 1), (1, 0)])
    across = lax.ppermute(mine, "zhi", [(0, 1), (1, 0)])
    corner = lax.ppermute(
        sent[chunk:], ("zb", "zhi"), [(0, 3), (3, 0), (1, 2), (2, 1)]
    )
    head_parts, conv_sum = call(
        far_sum_kernel, [shape((4, chunk, 128), BF16), shape((112, 128), BF16)], [VM] * 5, 8, quick
    )(sent, received, mine, across, corner)

    head_rows = 4 * chunk
    head_sum = swap_parts(head_parts, "zq").reshape(head_rows, 128)
    line = [
        lax.ppermute(conv_sum, "x", [(i, (i + step) % 4) for i in range(4)]) for step in (1, 2, 3)
    ]
    (conv_sum,) = call(line_total_kernel, [shape((112, 128), F32)], [VM] * 4, 8, quick)(conv_sum, *line)
    head_sum, conv_sum = lax.optimization_barrier((head_sum, conv_sum))
    other = lax.ppermute(conv_sum, "core", [(0, 1), (1, 0)])
    around = [(i, (i + 1) % 4) for i in range(4)]
    back = [(j, i) for i, j in around]
    behind = lax.ppermute(head_sum, "y", around)
    ahead = lax.ppermute(head_sum, "y", back)
    low = lax.ppermute(behind[: head_rows // 2], "y", around)
    high = lax.ppermute(ahead[head_rows // 2 :], "y", back)
    is_first = lax.axis_index("core") == 0
    pieces = jnp.stack([jnp.where(is_first, conv_sum, other), jnp.where(is_first, other, conv_sum)])
    pieces = pieces[:, : slabs * 12].reshape(2, tap_count, lanes, 12, 128)
    grad_conv = pieces.transpose(1, 0, 3, 2, 4).reshape(tap_count, 24, inner)
    head_weight = shape((channels, heads), BF16)
    grad_donor, grad_accept, grad_point, grad_gain, loss = call(
        finish_kernel,
        [head_weight, head_weight, shape((inner, channels), BF16), shape((1, channels), F32), shape((1, 128), F32)],
        [SM] + [VM] * 7,
        20,
        1_000_000_000,
        [
            pltpu.VMEM((4, head_rows, 128), BF16),
            pltpu.VMEM((inner, heads), BF16),
            pltpu.VMEM((inner, heads), BF16),
        ],
    )(place, head_sum, behind, ahead, low, high, donor_weight, acceptor_weight)
    return grad_conv, grad_point[None], grad_donor[None], grad_accept[None], grad_gain, loss[0, :1]


def channel_order():
    core, y, zq, zb, k = np.meshgrid(*[np.arange(n) for n in (2, 4, 4, 2, 12)], indexing="ij")
    channel = (24 * (8 * y + 4 * zb + zq) + 12 * core + k).reshape(-1)
    return np.eye(channel.size, dtype=np.float32)[channel]


def zb_halves():
    pick = np.zeros((224, 224), np.float32)
    for zb in range(2):
        for slab in range(9):
            for k in range(12):
                pick[112 * zb + 12 * slab + k, 24 * slab + 12 * zb + k] = 1.0
    return pick


def solution(mesh):
    fine = Mesh(mesh.devices.reshape(4, 2, 4, 2, 4, 2), SEQ + BATCH)
    placed = jax.shard_map(
        on_device,
        mesh=fine,
        in_specs=(
            P(BATCH, SEQ, None),
            P(),
            P(),
            P(),
            P(),
            P(),
            P(BATCH, SEQ, None),
            P(BATCH, SEQ),
            P(),
            P(),
            P(),
        ),
        out_specs=(
            P(None, SEQ, None),
            P(BATCH, None, None),
            P(BATCH, None, None),
            P(BATCH, None, None),
            P(BATCH, None),
            P(BATCH),
        ),
        check_vma=False,
    )

    def run(*arrays):
        order = jnp.asarray(channel_order(), BF16)
        eye = jnp.eye(order.shape[0], dtype=BF16)
        return placed(*arrays, order, eye, jnp.asarray(zb_halves(), BF16))

    return run
```

```python
import jax
import jax.numpy as jnp
import numpy as np
from jax import lax
from jax.experimental import pallas as pl
from jax.experimental.pallas import tpu as pltpu
from jax.sharding import Mesh
from jax.sharding import PartitionSpec as P

STEP = 128
PANEL = 128
SPAN = 4
SLOTS = 16
EPSILON = 1e-06
LOSS_WEIGHT = 1.0 / 128.0
SEQ = ("y", "zb", "zq")
BATCH = ("zhi", "x", "core")
F32 = jnp.float32
BF16 = jnp.bfloat16
ROOT = 0.7978845608028654
CUBIC = 0.044715
PIECE = 96
CHUNK_ROWS = 288
EXTRA_ROWS = 16


def dot(a, b):
    return lax.dot_general(a, b, (((1,), (0,)), ((), ())), preferred_element_type=F32)


def dot_t(a, b):
    return lax.dot_general(a, b, (((1,), (1,)), ((), ())), preferred_element_type=F32)


def gelu(v):
    return 0.5 * v * (1.0 + jnp.tanh(ROOT * (v + CUBIC * (v * v * v))))


def gelu_both(v):
    square = v * v
    t = jnp.tanh(ROOT * (v + CUBIC * (square * v)))
    half = 0.5 * (1.0 + t)
    return v * half, half + 0.5 * v * (1.0 - t * t) * (ROOT * (1.0 + 3.0 * CUBIC * square))


def rms(v):
    return lax.rsqrt(jnp.mean(v * v, axis=-1, keepdims=True) + EPSILON)


def call(kernel, outs, specs, megabytes, flops, scratch=()):
    return pl.pallas_call(
        kernel,
        out_shape=outs,
        in_specs=specs,
        out_specs=[VM] * len(outs),
        scratch_shapes=list(scratch),
        compiler_params=pltpu.CompilerParams(vmem_limit_bytes=megabytes * 1024 * 1024),
        cost_estimate=pl.CostEstimate(flops=flops, bytes_accessed=1_000_000, transcendentals=0),
    )


VM = pl.BlockSpec(memory_space=pltpu.VMEM)
SM = pl.BlockSpec(memory_space=pltpu.SMEM)


def own_kernel(tok, gain, hidden, factor):
    @pl.loop(0, tok.shape[0] // STEP)
    def _(i):
        here = pl.ds(pl.multiple_of(i * STEP, STEP), STEP)
        v = tok[here, :].astype(F32)
        unit = v * rms(v)
        value, slope = gelu_both(unit * gain[...])
        hidden[here, :] = value.astype(BF16)
        factor[here, :] = (slope * unit).astype(BF16)


def forward_kernel(
    odd, tok, mine, even_edge, odd_edge, gain, taps, point, donor_w, accept_w, meta,
    hidden, conv_out, act_out, embed_out, even_feat, odd_feat, wide_feat,
):
    rows = tok.shape[0]
    is_odd = odd[0] > 0
    low = jnp.where(is_odd, even_edge[...], odd_edge[...])
    high = jnp.where(is_odd, odd_edge[...], even_edge[...])
    for edge, at in ((low, 0), (high, STEP + rows)):
        v = edge.astype(F32)
        hidden[pl.ds(at, STEP), :] = gelu(v * rms(v) * gain[...]).astype(BF16)
    hidden[pl.ds(STEP, rows), :] = mine[...]

    conv = dot(hidden[:rows, :], taps[0])
    for tap in range(1, taps.shape[0]):
        conv = conv + dot(hidden[tap * STEP : tap * STEP + rows, :], taps[tap])
    conv_out[...] = conv
    act = gelu(conv).astype(BF16)
    act_out[...] = act
    embed = (tok[...].astype(F32) + dot(act, point[...])).astype(BF16)
    embed_out[...] = embed
    donor = dot(embed, donor_w[...]).astype(BF16)
    accept = dot(embed, accept_w[...]).astype(BF16)

    def store(into, value):
        into[:rows, :] = value

    pl.when(odd[0] > 0)(lambda: (store(even_feat, donor), store(odd_feat, accept))[0])
    pl.when(odd[0] <= 0)(lambda: (store(even_feat, accept), store(odd_feat, donor))[0])
    pl.when(odd[1] < 4)(lambda: store(wide_feat, accept))
    pl.when(odd[1] >= 4)(lambda: store(wide_feat, donor))
    even_feat[pl.ds(rows, SLOTS), :] = meta[...]
    odd_feat[pl.ds(rows, SLOTS), :] = meta[...]
    wide_feat[pl.ds(rows, SLOTS), :] = meta[...]


def side_kernel(
    odd, even_edge, odd_edge, gain, hidden, conv, act, embed, order, eye,
    factor, slope, hidden_t, act_t, embed_t,
):
    is_odd = odd[0] > 0
    low = jnp.where(is_odd, even_edge[...], odd_edge[...])
    high = jnp.where(is_odd, odd_edge[...], even_edge[...])
    for edge, at in ((low, 0), (high, STEP)):
        v = edge.astype(F32)
        unit = v * rms(v)
        factor[pl.ds(at, STEP), :] = (gelu_both(unit * gain[...])[1] * unit).astype(BF16)

    @pl.loop(0, conv.shape[0] // STEP)
    def _(i):
        here = pl.ds(pl.multiple_of(i * STEP, STEP), STEP)
        slope[here, :] = gelu_both(conv[here, :])[1]

    hidden_t[...] = dot_t(order[...], hidden[...]).astype(BF16)
    embed_t[...] = dot_t(eye[...], embed[...]).astype(BF16)
    inner = act.shape[1]
    act_t[...] = dot_t(eye[:inner, :inner], act[...]).astype(BF16)


def pair_kernel(distance, *refs):
    if distance == 0:
        odd, own, even0, odd0, d_donor, d_accept, loss = refs
        d_donor[...] = jnp.zeros_like(d_donor)
        d_accept[...] = jnp.zeros_like(d_accept)
        loss[...] = jnp.zeros_like(loss)
    else:
        odd, own, far, even0, odd0, even1, odd1, dd_in, da_in, loss_in, d_donor, d_accept, loss = refs
        d_donor[...] = dd_in[...]
        d_accept[...] = da_in[...]
        loss[...] = loss_in[...]
    is_odd = odd[0] > 0
    scale = even0.shape[1] ** (-0.5)
    per_device = d_donor.shape[0] // PANEL
    row = lax.broadcasted_iota(jnp.int32, (PANEL, PANEL), 0)
    col = lax.broadcasted_iota(jnp.int32, (PANEL, PANEL), 1)

    def place(block):
        return pl.ds(pl.multiple_of(block * PANEL, PANEL), PANEL)

    def own_donor(block):
        return jnp.where(is_odd, odd0[place(block), :], even0[place(block), :])

    def own_accept(block):
        return jnp.where(is_odd, even0[place(block), :], odd0[place(block), :])

    if distance == 0:
        far_accept, far_donor = own_accept, None
    else:

        def far_accept(block):
            return jnp.where(is_odd, odd1[place(block), :], even1[place(block), :])

        def far_donor(block):
            return jnp.where(is_odd, even1[place(block), :], odd1[place(block), :])

    def visit(meta, j, donors, acceptors, is_owner):
        accept_block = meta[j, 2] - distance * per_device
        here = (meta[j, 4] > 0) & (accept_block >= 0) & (accept_block < per_device)

        @pl.when(here)
        def _():
            donor_block = meta[j, 0]
            dpan = donors(donor_block)
            apan = acceptors(accept_block)
            scores = dot_t(dpan, apan) * scale
            target = ((row == meta[j, 1]) & (col == meta[j, 3])).astype(F32)
            small = jnp.exp(-jnp.abs(scores))
            inverse = 1.0 / (1.0 + small)
            sigmoid = jnp.where(scores >= 0, inverse, small * inverse)
            dscore = ((sigmoid - target) * LOSS_WEIGHT).astype(BF16)
            if is_owner:
                loss[...] += (jnp.maximum(scores, 0.0) + jnp.log1p(small)) - target * scores
                d_donor[place(donor_block), :] += dot(dscore, apan) * scale
            if distance == 0 or not is_owner:
                d_accept[place(accept_block), :] += scale * lax.dot_general(
                    dscore, dpan, (((0,), (0,)), ((), ())), preferred_element_type=F32
                )

    @pl.loop(0, SLOTS)
    def _(j):
        visit(own, j, own_donor, far_accept, True)
        if distance > 0:
            visit(far, j, far_donor, own_accept, False)


def relative(target, y, first):
    code = (target ^ (target >> 1)) ^ (y ^ (y >> 1))
    low, high = code & 1, code >> 1
    return low * 2 + high if first == 0 else high * 2 + low


def tap_grad_kernel(
    place, d_donor, d_accept, point, donor_w, accept_w, slope, hidden_t,
    keep, send, d_conv, d_feat,
):
    rows, heads = d_donor.shape
    channels = hidden_t.shape[0]

    dd = d_donor[...].astype(BF16)
    da = d_accept[...].astype(BF16)
    d_feat[:, :heads] = dd
    d_feat[:, heads:] = da
    d_embed = (dot_t(dd, donor_w[...]) + dot_t(da, accept_w[...])).astype(BF16)
    d_conv[...] = (dot_t(d_embed, point[...]) * slope[...]).astype(BF16)

    lanes = d_conv.shape[1] // 128
    half_rows = channels // 2
    slab = [relative(target, place[1], 1) for target in range(4)]
    for tap in range(3):
        for half in range(2):
            part = dot(
                hidden_t[half * half_rows : (half + 1) * half_rows, tap * STEP : tap * STEP + rows],
                d_conv[...],
            ).astype(BF16)

            def store(into, part=part, tap=tap):
                for k in range(4):
                    for lane in range(lanes):
                        into[slab[k], tap * lanes + lane] = part[
                            k * PIECE : (k + 1) * PIECE, lane * 128 : (lane + 1) * 128
                        ]

            pl.when(place[0] == half)(lambda: store(keep))
            pl.when(place[0] != half)(lambda: store(send))


def head_grad_kernel(
    place, d_conv, d_feat, loss, taps, factor, edge_factor, act_t, embed_t, head_sum,
):
    rows = d_conv.shape[0]
    channels = embed_t.shape[0]
    inner = act_t.shape[0]
    slab = [relative(target, place[1], 0) for target in range(4)]

    def put(part, base, group_rows, first):
        for lane in range(4):
            for k in range(part.shape[0] // PIECE):
                piece = first + lane * (group_rows // PIECE) + k + base
                chunk, third = piece // 3, piece % 3
                head_sum[slab[chunk // 4], chunk % 4, third * PIECE : (third + 1) * PIECE, :] = part[
                    k * PIECE : (k + 1) * PIECE, lane * 128 : (lane + 1) * 128
                ]

    for i in range(2):
        part = dot(embed_t[i * 4 * PIECE : (i + 1) * 4 * PIECE, :], d_feat[...]).astype(BF16)
        put(part, 4 * i, channels, 0)
    put(dot(act_t[...], d_feat[...]).astype(BF16), 0, inner, 4 * channels // PIECE)

    total = jnp.zeros((8, channels), F32)
    edge = edge_factor.shape[0] // 2
    for tap in range(taps.shape[0]):
        product = dot_t(d_conv[...], taps[tap])
        if tap == 0:
            weights = jnp.concatenate([edge_factor[:edge, :], factor[: rows - edge, :]], axis=0)
        elif tap == 1:
            weights = factor[...]
        else:
            weights = jnp.concatenate([factor[edge:, :], edge_factor[edge:, :]], axis=0)
        product = product * weights.astype(F32)
        total = total + jnp.sum(product.reshape(rows // 8, 8, channels), axis=0)
    gain = jnp.sum(total, axis=0, keepdims=True)
    loss_row = jnp.sum(loss[...], axis=0, keepdims=True) * LOSS_WEIGHT
    loss_all = jnp.broadcast_to(jnp.sum(loss_row, axis=1, keepdims=True), (1, 128))
    at_row = lax.broadcasted_iota(jnp.int32, (EXTRA_ROWS, 128), 0)
    for chunk in range(16):
        if chunk < channels // 128:
            value = gain[:, chunk * 128 : (chunk + 1) * 128]
        elif chunk == channels // 128:
            value = loss_all
        else:
            value = jnp.zeros((1, 128), F32)
        coarse = value.astype(BF16).astype(F32)
        block = jnp.where(at_row == 0, coarse, 0.0) + jnp.where(at_row == 8, value - coarse, 0.0)
        head_sum[slab[chunk // 4], chunk % 4, CHUNK_ROWS:, :] = block.astype(BF16)


def split_rows(total):
    value = total[CHUNK_ROWS : CHUNK_ROWS + 8] + total[CHUNK_ROWS + 8 : CHUNK_ROWS + 16]
    coarse = value.astype(BF16).astype(F32)
    return jnp.concatenate([total[:CHUNK_ROWS], coarse, value - coarse], axis=0).astype(BF16)


def core_sum_kernel(taps, received, kept, send):
    for k in range(2):
        for slab in range(taps.shape[1]):
            kept[k, slab] = taps[k, slab].astype(F32) + received[k, slab].astype(F32)
            send[k, slab] = (
                taps[k + 2, slab].astype(F32) + received[k + 2, slab].astype(F32)
            ).astype(BF16)


def head_sum_kernel(head, received, kept, send):
    for zq in range(4):
        kept[zq] = head[0, zq].astype(F32) + received[0, zq].astype(F32)
        send[zq] = split_rows(head[1, zq].astype(F32) + received[1, zq].astype(F32))


def tap_sum_kernel(before, received, kept, send):
    for slab in range(before.shape[1]):
        kept[slab] = before[0, slab] + received[0, slab].astype(F32)
        send[slab] = (before[1, slab] + received[1, slab].astype(F32)).astype(BF16)


def join_kernel(head, head_in, taps, taps_in, both):
    chunk_rows = head.shape[1]
    for zq in range(4):
        both[zq, :chunk_rows, :] = split_rows(head[zq] + head_in[zq].astype(F32))
        here = slice(zq * 24, (zq + 1) * 24)
        parts = [taps[k, here] + taps_in[k, here].astype(F32) for k in range(taps.shape[0])]
        parts.append(jnp.zeros((8, 128), F32))
        both[zq, chunk_rows:, :] = jnp.concatenate(parts, axis=0).astype(BF16)


def line_sum_kernel(parts, heads, taps):
    total = parts[0].astype(F32)
    for zq in range(1, 4):
        total = total + parts[zq].astype(F32)
    chunk_rows = heads.shape[0]
    heads[...] = split_rows(total[:chunk_rows])
    taps[...] = total[chunk_rows:].astype(BF16)


def far_sum_kernel(place, sent, received, own, one, two, three, pick, head, theirs, mine):
    total = split_rows(sent[...].astype(F32) + received[...].astype(F32))
    for zq in range(head.shape[0]):
        head[zq] = total
    even = own[...].astype(F32) + two[...].astype(F32)
    total = (even + (one[...].astype(F32) + three[...].astype(F32))).astype(BF16)
    half = mine.shape[0]
    zb = place[2]

    def picked(which):
        return dot(pick[pl.ds(pl.multiple_of(which * half, half), half), :], total).astype(BF16)

    theirs[...] = picked(1 - zb)
    mine[...] = picked(zb)


def add_kernel(one, two, total):
    total[...] = (one[...].astype(F32) + two[...].astype(F32)).astype(total.dtype)


def order_kernel(place, own, other, both):
    both[place[0]] = own[...]
    both[1 - place[0]] = other[...]


def finish_kernel(
    place, own, behind, ahead, low, high, donor_w, accept_w,
    grad_donor, grad_accept, grad_point, gain, loss, held, act_donor, act_accept,
):
    count = held.shape[0]
    for step, part in ((0, own), (3, behind), (1, ahead)):
        held[lax.rem(place[1] + step, count)] = part[...]
    opposite = lax.rem(place[1] + 2, count)
    middle = low.shape[0]
    held[opposite, :middle, :] = low[...]
    held[opposite, middle:, :] = high[...]
    channels = grad_donor.shape[0]
    inner = act_donor.shape[0]
    chunk_rows = CHUNK_ROWS + EXTRA_ROWS
    piece = 0
    for into in (grad_donor, grad_accept, act_donor, act_accept):
        for lane in range(2):
            for k in range(into.shape[0] // PIECE):
                chunk, third = piece // 3, piece % 3
                at = (chunk % 4) * chunk_rows + third * PIECE
                into[k * PIECE : (k + 1) * PIECE, lane * 128 : (lane + 1) * 128] = held[
                    chunk // 4, at : at + PIECE, :
                ]
                piece += 1

    grad_point[...] = (
        dot_t(act_donor[...], donor_w[...]) + dot_t(act_accept[...], accept_w[...])
    ).astype(BF16)

    for chunk in range(channels // 128 + 1):
        at = (chunk % 4) * chunk_rows + CHUNK_ROWS
        block = held[chunk // 4, at : at + EXTRA_ROWS, :].astype(F32)
        value = block[0:1, :] + block[8:9, :]
        if chunk < channels // 128:
            gain[:, chunk * 128 : (chunk + 1) * 128] = value
        else:
            loss[...] = value


def swapped(block, first, between_lines=True):
    count = lax.axis_size(SEQ)
    pairs = [(i, i + 1) for i in range(first, count - 1, 2) if between_lines or i % 8 < 7]
    return lax.ppermute(block, SEQ, pairs + [(j, i) for i, j in pairs])


def swap_parts(parts, axis):
    return lax.all_to_all(parts, axis, 0, 0, tiled=True)


def on_device(
    activations, norm_gain, dilated_tap_weight, point_weight, donor_weight, acceptor_weight,
    pair_sites, pair_count, order, eye, pick,
):
    tokens = activations[0]
    rows, channels = tokens.shape
    tap_count, _, inner = dilated_tap_weight.shape
    heads = donor_weight.shape[1]
    blocks = rows // PANEL
    shape = jax.ShapeDtypeStruct
    here = lax.axis_index(SEQ)
    line = here % 8
    odd = jnp.stack([here % 2, line]).astype(jnp.int32)
    is_odd = here % 2 > 0
    start, end = tokens[:STEP], tokens[rows - STEP :]
    even_edge = swapped(jnp.where(is_odd, start, end), 0)
    odd_edge = swapped(jnp.where(is_odd, end, start), 1)
    gain = norm_gain[None]
    sites = pair_sites[0]
    first = here * blocks
    live = (jnp.arange(SLOTS, dtype=jnp.int32) < pair_count[0, 0]).astype(jnp.int32)
    meta = jnp.stack(
        [
            sites[:, 0] // PANEL - first,
            sites[:, 0] % PANEL,
            sites[:, 1] // PANEL - first,
            sites[:, 1] % PANEL,
            live,
        ]
        + [jnp.zeros_like(live)] * 3,
        axis=1,
    )
    meta_rows = jnp.pad(meta.astype(BF16), ((0, 0), (0, heads - meta.shape[1])))

    mine, factor = call(
        own_kernel, [shape((rows, channels), BF16)] * 2, [VM] * 2, 12, 2_000_000_000
    )(tokens, gain)
    feat = shape((rows + SLOTS, heads), BF16)
    hidden, conv, act, embed, even_feat, odd_feat, wide_feat = call(
        forward_kernel,
        [
            shape((rows + 2 * STEP, channels), BF16),
            shape((rows, inner), F32),
            shape((rows, inner), BF16),
            shape((rows, channels), BF16),
            feat,
            feat,
            feat,
        ],
        [SM] + [VM] * 10,
        20,
        4_000_000_000,
    )(
        odd, tokens, mine, even_edge, odd_edge, gain, dilated_tap_weight, point_weight,
        donor_weight, acceptor_weight, meta_rows,
    )

    acc_shapes = [shape((rows, heads), F32), shape((rows, heads), F32), shape((PANEL, PANEL), F32)]
    acc = call(
        lambda *refs: pair_kernel(0, *refs), acc_shapes, [SM] * 2 + [VM] * 2, 12, 2_000_000_000
    )(1 - odd[:1], meta, even_feat, odd_feat)
    edge_factor, slope, hidden_t, act_t, embed_t = call(
        side_kernel,
        [
            shape((2 * STEP, channels), BF16),
            shape((rows, inner), F32),
            shape((channels, rows + 2 * STEP), BF16),
            shape((inner, rows), BF16),
            shape((channels, rows), BF16),
        ],
        [SM] + [VM] * 9,
        20,
        6_000_000_000,
    )(odd, even_edge, odd_edge, gain, hidden, conv, act, embed, order, eye)
    count = lax.axis_size(SEQ)
    starts = range(0, count, 8)
    wide_pairs = [(i + k, i - 4 + k) for i in starts if i > 0 for k in (2, 3)]
    wide_pairs += [(i + k, i + 4 + k) for i in starts if i + 8 < count for k in (4, 5)]
    relay_pairs = [(i + 6, i + 7) for i in starts] + [(i + 1, i) for i in starts]
    wide = lax.ppermute(wide_feat, SEQ, wide_pairs)
    relay = lax.ppermute(wide, SEQ, relay_pairs)
    at_end = (line == 0) | (line == 7)
    near_end = (line == 1) | (line == 6)
    short_far, long_far = odd_feat, even_feat
    for distance in range(1, SPAN + 1):
        if distance == 1:
            short_far, long_far = swapped(odd_feat, 0), swapped(even_feat, 1)
        else:
            short_far, long_far = swapped(long_far, 0), swapped(short_far, 1, distance <= 2)
        short_use, long_use = short_far, long_far
        if distance == 3:
            long_use = jnp.where(at_end, relay, long_far)
        if distance == 4:
            short_use = jnp.where(near_end, wide, short_far)
            long_use = jnp.where(at_end, wide, long_far)
        far_meta = jnp.where(odd[0] > 0, short_use[rows:, :8], long_use[rows:, :8]).astype(jnp.int32)
        acc = call(
            lambda *refs, distance=distance: pair_kernel(distance, *refs),
            acc_shapes,
            [SM] * 3 + [VM] * 7,
            12,
            2_500_000_000,
        )(1 - odd[:1], meta, far_meta, even_feat, odd_feat, long_use, short_use, *acc)

    chunk = CHUNK_ROWS + EXTRA_ROWS
    lanes = inner // 128
    slabs = tap_count * lanes
    y = lax.axis_index("y")
    place = jnp.stack([lax.axis_index("core"), y, lax.axis_index("zb")]).astype(jnp.int32)
    half = shape((4, slabs, PIECE, 128), BF16)
    keep, send, d_conv, d_feat = call(
        tap_grad_kernel,
        [half, half, shape((rows, inner), BF16), shape((rows, 2 * heads), BF16)],
        [SM] + [VM] * 7,
        24,
        4_000_000_000,
    )(place, acc[0], acc[1], point_weight, donor_weight, acceptor_weight, slope, hidden_t)
    received = lax.ppermute(send, "core", [(0, 1), (1, 0)])
    (head_sum,) = call(
        head_grad_kernel, [shape((4, 4, chunk, 128), BF16)], [SM] + [VM] * 8, 20, 4_000_000_000
    )(place, d_conv, d_feat, acc[2], dilated_tap_weight, factor, edge_factor, act_t, embed_t)

    first_pairs = [(0, 1), (1, 0), (2, 3), (3, 2)]
    second_pairs = [(1, 2), (2, 1), (3, 0), (0, 3)]
    quick = 1_000_000
    conv_kept, conv_send = call(
        core_sum_kernel, [shape((2, slabs, PIECE, 128), F32), shape((2, slabs, PIECE, 128), BF16)],
        [VM] * 2, 12, quick,
    )(keep, received)
    other = lax.ppermute(head_sum[2:], "y", first_pairs)
    heads_kept, heads_send = call(
        head_sum_kernel, [shape((4, chunk, 128), F32), shape((4, chunk, 128), BF16)], [VM] * 2, 12, quick
    )(head_sum, other)
    other = lax.ppermute(conv_send, "y", second_pairs)
    conv_kept, conv_send = call(
        tap_sum_kernel, [shape((slabs, PIECE, 128), F32), shape((slabs, PIECE, 128), BF16)],
        [VM] * 2, 12, quick,
    )(conv_kept, other)
    heads_in = lax.ppermute(heads_send, "y", second_pairs)
    conv_in = lax.ppermute(conv_send, "y", first_pairs)

    joint = chunk + 224
    (both,) = call(join_kernel, [shape((4, joint, 128), BF16)], [VM] * 4, 12, quick)(
        heads_kept, heads_in, conv_kept, conv_in
    )
    parts = swap_parts(both, "zq")
    head_line, tap_line = call(
        line_sum_kernel, [shape((chunk, 128), BF16), shape((224, 128), BF16)], [VM], 8, quick
    )(parts)
    received = lax.ppermute(head_line, "zb", [(0, 1), (1, 0)])
    line = [lax.ppermute(tap_line, "x", [(i, (i + step) % 4) for i in range(4)]) for step in (1, 2, 3)]
    half_taps = shape((112, 128), BF16)
    head_parts, theirs, mine = call(
        far_sum_kernel, [shape((4, chunk, 128), BF16), half_taps, half_taps], [SM] + [VM] * 7, 8, quick
    )(place, head_line, received, tap_line, *line, pick)
    other = lax.ppermute(theirs, "zb", [(0, 1), (1, 0)])
    (conv_sum,) = call(add_kernel, [half_taps], [VM] * 2, 8, quick)(mine, other)

    head_rows = 4 * chunk
    head_sum = swap_parts(head_parts, "zq").reshape(head_rows, 128)
    other = lax.ppermute(conv_sum, "core", [(0, 1), (1, 0)])
    (pieces,) = call(order_kernel, [shape((2, 112, 128), BF16)], [SM] + [VM] * 2, 8, quick)(
        place, conv_sum, other
    )
    head_sum, pieces = lax.optimization_barrier((head_sum, pieces))
    around = [(i, (i + 1) % 4) for i in range(4)]
    back = [(j, i) for i, j in around]
    behind = lax.ppermute(head_sum, "y", around)
    ahead = lax.ppermute(head_sum, "y", back)
    low = lax.ppermute(behind[: head_rows // 2], "y", around)
    high = lax.ppermute(ahead[head_rows // 2 :], "y", back)
    other = lax.ppermute(pieces, "zhi", [(0, 1), (1, 0)])
    other, _ = lax.optimization_barrier((other, low))
    pieces = pieces.astype(F32) + other.astype(F32)
    pieces = pieces[:, : slabs * 12].reshape(2, tap_count, lanes, 12, 128)
    grad_conv = pieces.transpose(1, 0, 3, 2, 4).reshape(tap_count, 24, inner)
    head_weight = shape((channels, heads), BF16)
    grad_donor, grad_accept, grad_point, grad_gain, loss = call(
        finish_kernel,
        [head_weight, head_weight, shape((inner, channels), BF16), shape((1, channels), F32), shape((1, 128), F32)],
        [SM] + [VM] * 7,
        20,
        1_000_000_000,
        [
            pltpu.VMEM((4, head_rows, 128), BF16),
            pltpu.VMEM((inner, heads), BF16),
            pltpu.VMEM((inner, heads), BF16),
        ],
    )(place, head_sum, behind, ahead, low, high, donor_weight, acceptor_weight)
    return grad_conv, grad_point[None], grad_donor[None], grad_accept[None], grad_gain, loss[0, :1]


def channel_order():
    core, y, zq, zb, k = np.meshgrid(*[np.arange(n) for n in (2, 4, 4, 2, 12)], indexing="ij")
    channel = (24 * (8 * y + 4 * zb + zq) + 12 * core + k).reshape(-1)
    return np.eye(channel.size, dtype=np.float32)[channel]


def zb_halves():
    pick = np.zeros((224, 224), np.float32)
    for zb in range(2):
        for slab in range(9):
            for k in range(12):
                pick[112 * zb + 12 * slab + k, 24 * slab + 12 * zb + k] = 1.0
    return pick


def solution(mesh):
    fine = Mesh(mesh.devices.reshape(4, 2, 4, 2, 4, 2), SEQ + BATCH)
    placed = jax.shard_map(
        on_device,
        mesh=fine,
        in_specs=(
            P(BATCH, SEQ, None),
            P(),
            P(),
            P(),
            P(),
            P(),
            P(BATCH, SEQ, None),
            P(BATCH, SEQ),
            P(),
            P(),
            P(),
        ),
        out_specs=(
            P(None, SEQ, None),
            P(BATCH, None, None),
            P(BATCH, None, None),
            P(BATCH, None, None),
            P(BATCH, None),
            P(BATCH),
        ),
        check_vma=False,
    )

    def run(*arrays):
        order = jnp.asarray(channel_order(), BF16)
        eye = jnp.eye(order.shape[0], dtype=BF16)
        return placed(*arrays, order, eye, jnp.asarray(zb_halves(), BF16))

    return run
```

```python
import jax
import jax.numpy as jnp
import numpy as np
from jax import lax
from jax.experimental import pallas as pl
from jax.experimental.pallas import tpu as pltpu
from jax.sharding import Mesh
from jax.sharding import PartitionSpec as P

STEP = 128
PANEL = 128
SPAN = 4
SLOTS = 16
EPSILON = 1e-06
LOSS_WEIGHT = 1.0 / 128.0
SEQ = ("y", "zb", "zq")
BATCH = ("zhi", "x", "core")
F32 = jnp.float32
BF16 = jnp.bfloat16
ROOT = 0.7978845608028654
CUBIC = 0.044715
PIECE = 96
CHUNK_ROWS = 288
EXTRA_ROWS = 16


def dot(a, b):
    return lax.dot_general(a, b, (((1,), (0,)), ((), ())), preferred_element_type=F32)


def dot_t(a, b):
    return lax.dot_general(a, b, (((1,), (1,)), ((), ())), preferred_element_type=F32)


def gelu(v):
    return 0.5 * v * (1.0 + jnp.tanh(ROOT * (v + CUBIC * (v * v * v))))


def gelu_both(v):
    square = v * v
    t = jnp.tanh(ROOT * (v + CUBIC * (square * v)))
    half = 0.5 * (1.0 + t)
    return v * half, half + 0.5 * v * (1.0 - t * t) * (ROOT * (1.0 + 3.0 * CUBIC * square))


def rms(v):
    return lax.rsqrt(jnp.mean(v * v, axis=-1, keepdims=True) + EPSILON)


def call(kernel, outs, specs, megabytes, flops, scratch=()):
    return pl.pallas_call(
        kernel,
        out_shape=outs,
        in_specs=specs,
        out_specs=[VM] * len(outs),
        scratch_shapes=list(scratch),
        compiler_params=pltpu.CompilerParams(vmem_limit_bytes=megabytes * 1024 * 1024),
        cost_estimate=pl.CostEstimate(flops=flops, bytes_accessed=1_000_000, transcendentals=0),
    )


VM = pl.BlockSpec(memory_space=pltpu.VMEM)
SM = pl.BlockSpec(memory_space=pltpu.SMEM)


def own_kernel(tok, gain, hidden, factor):
    @pl.loop(0, tok.shape[0] // STEP)
    def _(i):
        here = pl.ds(pl.multiple_of(i * STEP, STEP), STEP)
        v = tok[here, :].astype(F32)
        unit = v * rms(v)
        value, slope = gelu_both(unit * gain[...])
        hidden[here, :] = value.astype(BF16)
        factor[here, :] = (slope * unit).astype(BF16)


def edge_kernel(edge, gain, hidden):
    v = edge[...].astype(F32)
    hidden[...] = gelu(v * rms(v) * gain[...]).astype(BF16)


def forward_kernel(
    odd, tok, mine, even_edge, odd_hidden, gain, taps, point, donor_w, accept_w, meta,
    hidden, conv_out, act_out, embed_out, even_feat, odd_feat,
):
    rows = tok.shape[0]
    is_odd = odd[0] > 0
    v = even_edge[...].astype(F32)
    even_hidden = gelu(v * rms(v) * gain[...]).astype(BF16)
    hidden[pl.ds(0, STEP), :] = jnp.where(is_odd, even_hidden, odd_hidden[...])
    hidden[pl.ds(STEP + rows, STEP), :] = jnp.where(is_odd, odd_hidden[...], even_hidden)
    hidden[pl.ds(STEP, rows), :] = mine[...]

    conv = dot(hidden[:rows, :], taps[0])
    for tap in range(1, taps.shape[0]):
        conv = conv + dot(hidden[tap * STEP : tap * STEP + rows, :], taps[tap])
    conv_out[...] = conv
    act = gelu(conv).astype(BF16)
    act_out[...] = act
    embed = (tok[...].astype(F32) + dot(act, point[...])).astype(BF16)
    embed_out[...] = embed
    donor = dot(embed, donor_w[...]).astype(BF16)
    accept = dot(embed, accept_w[...]).astype(BF16)
    even_feat[:rows, :] = jnp.where(is_odd, donor, accept)
    odd_feat[:rows, :] = jnp.where(is_odd, accept, donor)
    even_feat[pl.ds(rows, SLOTS), :] = meta[...]
    odd_feat[pl.ds(rows, SLOTS), :] = meta[...]


def side_kernel(
    odd, even_edge, odd_edge, gain, hidden, conv, act, embed, order, eye,
    factor, slope, hidden_t, act_t, embed_t,
):
    is_odd = odd[0] > 0
    low = jnp.where(is_odd, even_edge[...], odd_edge[...])
    high = jnp.where(is_odd, odd_edge[...], even_edge[...])
    for edge, at in ((low, 0), (high, STEP)):
        v = edge.astype(F32)
        unit = v * rms(v)
        factor[pl.ds(at, STEP), :] = (gelu_both(unit * gain[...])[1] * unit).astype(BF16)

    @pl.loop(0, conv.shape[0] // STEP)
    def _(i):
        here = pl.ds(pl.multiple_of(i * STEP, STEP), STEP)
        slope[here, :] = gelu_both(conv[here, :])[1]

    hidden_t[...] = dot_t(order[...], hidden[...]).astype(BF16)
    embed_t[...] = dot_t(eye[...], embed[...]).astype(BF16)
    inner = act.shape[1]
    act_t[...] = dot_t(eye[:inner, :inner], act[...]).astype(BF16)


def pair_kernel(distance, *refs):
    if distance == 0:
        odd, own, even0, odd0, d_donor, d_accept, loss = refs
        d_donor[...] = jnp.zeros_like(d_donor)
        d_accept[...] = jnp.zeros_like(d_accept)
        loss[...] = jnp.zeros_like(loss)
    else:
        odd, own, far, even0, odd0, even1, odd1, dd_in, da_in, loss_in, d_donor, d_accept, loss = refs
        d_donor[...] = dd_in[...]
        d_accept[...] = da_in[...]
        loss[...] = loss_in[...]
    is_odd = odd[0] > 0
    scale = even0.shape[1] ** (-0.5)
    per_device = d_donor.shape[0] // PANEL
    row = lax.broadcasted_iota(jnp.int32, (PANEL, PANEL), 0)
    col = lax.broadcasted_iota(jnp.int32, (PANEL, PANEL), 1)

    def place(block):
        return pl.ds(pl.multiple_of(block * PANEL, PANEL), PANEL)

    def own_donor(block):
        return jnp.where(is_odd, odd0[place(block), :], even0[place(block), :])

    def own_accept(block):
        return jnp.where(is_odd, even0[place(block), :], odd0[place(block), :])

    if distance == 0:
        far_accept, far_donor = own_accept, None
    else:

        def far_accept(block):
            return jnp.where(is_odd, odd1[place(block), :], even1[place(block), :])

        def far_donor(block):
            return jnp.where(is_odd, even1[place(block), :], odd1[place(block), :])

    def visit(meta, j, donors, acceptors, is_owner):
        accept_block = meta[j, 2] - distance * per_device
        here = (meta[j, 4] > 0) & (accept_block >= 0) & (accept_block < per_device)

        @pl.when(here)
        def _():
            donor_block = meta[j, 0]
            dpan = donors(donor_block)
            apan = acceptors(accept_block)
            scores = dot_t(dpan, apan) * scale
            target = ((row == meta[j, 1]) & (col == meta[j, 3])).astype(F32)
            small = jnp.exp(-jnp.abs(scores))
            inverse = 1.0 / (1.0 + small)
            sigmoid = jnp.where(scores >= 0, inverse, small * inverse)
            dscore = ((sigmoid - target) * LOSS_WEIGHT).astype(BF16)
            if is_owner:
                loss[...] += (jnp.maximum(scores, 0.0) + jnp.log1p(small)) - target * scores
                d_donor[place(donor_block), :] += dot(dscore, apan) * scale
            if distance == 0 or not is_owner:
                d_accept[place(accept_block), :] += scale * lax.dot_general(
                    dscore, dpan, (((0,), (0,)), ((), ())), preferred_element_type=F32
                )

    @pl.loop(0, SLOTS)
    def _(j):
        visit(own, j, own_donor, far_accept, True)
        if distance > 0:
            visit(far, j, far_donor, own_accept, False)


def relative(target, y, first):
    code = (target ^ (target >> 1)) ^ (y ^ (y >> 1))
    low, high = code & 1, code >> 1
    return low * 2 + high if first == 0 else high * 2 + low


def tap_grad_kernel(
    place, d_donor, d_accept, point, donor_w, accept_w, slope, hidden_t,
    keep, send, d_conv, d_feat,
):
    rows, heads = d_donor.shape
    channels = hidden_t.shape[0]

    dd = d_donor[...].astype(BF16)
    da = d_accept[...].astype(BF16)
    d_feat[:, :heads] = dd
    d_feat[:, heads:] = da
    d_embed = (dot_t(dd, donor_w[...]) + dot_t(da, accept_w[...])).astype(BF16)
    d_conv[...] = (dot_t(d_embed, point[...]) * slope[...]).astype(BF16)

    lanes = d_conv.shape[1] // 128
    half_rows = channels // 2
    slab = [relative(target, place[1], 1) for target in range(4)]
    for tap in range(3):
        for half in range(2):
            part = dot(
                hidden_t[half * half_rows : (half + 1) * half_rows, tap * STEP : tap * STEP + rows],
                d_conv[...],
            ).astype(BF16)

            def store(into, part=part, tap=tap):
                for k in range(4):
                    for lane in range(lanes):
                        into[slab[k], tap * lanes + lane] = part[
                            k * PIECE : (k + 1) * PIECE, lane * 128 : (lane + 1) * 128
                        ]

            pl.when(place[0] == half)(lambda: store(keep))
            pl.when(place[0] != half)(lambda: store(send))


def head_grad_kernel(
    place, d_conv, d_feat, loss, taps, factor, edge_factor, act_t, embed_t, head_sum,
):
    rows = d_conv.shape[0]
    channels = embed_t.shape[0]
    inner = act_t.shape[0]
    slab = [relative(target, place[1], 0) for target in range(4)]

    def put(part, base, group_rows, first):
        for lane in range(4):
            for k in range(part.shape[0] // PIECE):
                piece = first + lane * (group_rows // PIECE) + k + base
                chunk, third = piece // 3, piece % 3
                head_sum[slab[chunk // 4], chunk % 4, third * PIECE : (third + 1) * PIECE, :] = part[
                    k * PIECE : (k + 1) * PIECE, lane * 128 : (lane + 1) * 128
                ]

    for i in range(2):
        part = dot(embed_t[i * 4 * PIECE : (i + 1) * 4 * PIECE, :], d_feat[...]).astype(BF16)
        put(part, 4 * i, channels, 0)
    put(dot(act_t[...], d_feat[...]).astype(BF16), 0, inner, 4 * channels // PIECE)

    total = jnp.zeros((8, channels), F32)
    edge = edge_factor.shape[0] // 2
    for tap in range(taps.shape[0]):
        product = dot_t(d_conv[...], taps[tap])
        if tap == 0:
            weights = jnp.concatenate([edge_factor[:edge, :], factor[: rows - edge, :]], axis=0)
        elif tap == 1:
            weights = factor[...]
        else:
            weights = jnp.concatenate([factor[edge:, :], edge_factor[edge:, :]], axis=0)
        product = product * weights.astype(F32)
        total = total + jnp.sum(product.reshape(rows // 8, 8, channels), axis=0)
    gain = jnp.sum(total, axis=0, keepdims=True)
    loss_row = jnp.sum(loss[...], axis=0, keepdims=True) * LOSS_WEIGHT
    loss_all = jnp.broadcast_to(jnp.sum(loss_row, axis=1, keepdims=True), (1, 128))
    at_row = lax.broadcasted_iota(jnp.int32, (EXTRA_ROWS, 128), 0)
    for chunk in range(16):
        if chunk < channels // 128:
            value = gain[:, chunk * 128 : (chunk + 1) * 128]
        elif chunk == channels // 128:
            value = loss_all
        else:
            value = jnp.zeros((1, 128), F32)
        coarse = value.astype(BF16).astype(F32)
        block = jnp.where(at_row == 0, coarse, 0.0) + jnp.where(at_row == 8, value - coarse, 0.0)
        head_sum[slab[chunk // 4], chunk % 4, CHUNK_ROWS:, :] = block.astype(BF16)


def split_rows(total):
    value = total[CHUNK_ROWS : CHUNK_ROWS + 8] + total[CHUNK_ROWS + 8 : CHUNK_ROWS + 16]
    coarse = value.astype(BF16).astype(F32)
    return jnp.concatenate([total[:CHUNK_ROWS], coarse, value - coarse], axis=0).astype(BF16)


def core_sum_kernel(taps, received, kept, send):
    for k in range(2):
        for slab in range(taps.shape[1]):
            kept[k, slab] = taps[k, slab].astype(F32) + received[k, slab].astype(F32)
            send[k, slab] = (
                taps[k + 2, slab].astype(F32) + received[k + 2, slab].astype(F32)
            ).astype(BF16)


def head_sum_kernel(head, received, kept, send):
    for zq in range(4):
        kept[zq] = head[0, zq].astype(F32) + received[0, zq].astype(F32)
        send[zq] = split_rows(head[1, zq].astype(F32) + received[1, zq].astype(F32))


def tap_sum_kernel(before, received, kept, send):
    for slab in range(before.shape[1]):
        kept[slab] = before[0, slab] + received[0, slab].astype(F32)
        send[slab] = (before[1, slab] + received[1, slab].astype(F32)).astype(BF16)


def join_kernel(head, head_in, taps, taps_in, both):
    chunk_rows = head.shape[1]
    for zq in range(4):
        both[zq, :chunk_rows, :] = split_rows(head[zq] + head_in[zq].astype(F32))
        here = slice(zq * 24, (zq + 1) * 24)
        parts = [taps[k, here] + taps_in[k, here].astype(F32) for k in range(taps.shape[0])]
        parts.append(jnp.zeros((8, 128), F32))
        both[zq, chunk_rows:, :] = jnp.concatenate(parts, axis=0).astype(BF16)


def line_sum_kernel(parts, pick, heads, taps):
    total = parts[0].astype(F32)
    for zq in range(1, 4):
        total = total + parts[zq].astype(F32)
    chunk_rows = heads.shape[0]
    heads[...] = split_rows(total[:chunk_rows])
    rest = total[chunk_rows:].astype(BF16)
    half = taps.shape[1]
    for zb in range(2):
        picked = dot(pick[zb * half : (zb + 1) * half, :], rest).astype(BF16)
        for zhi in range(2):
            taps[zb * 2 + zhi] = picked


def far_sum_kernel(sent, received, tap_parts, head, taps):
    total = split_rows(sent[...].astype(F32) + received[...].astype(F32))
    for zq in range(head.shape[0]):
        head[zq] = total
    near = tap_parts[0].astype(F32) + tap_parts[1].astype(F32)
    taps[...] = (near + (tap_parts[2].astype(F32) + tap_parts[3].astype(F32))).astype(BF16)


def line_total_kernel(own, one, two, three, total):
    even = own[...].astype(F32) + two[...].astype(F32)
    total[...] = even + (one[...].astype(F32) + three[...].astype(F32))


def finish_kernel(
    place, own, behind, ahead, low, high, donor_w, accept_w,
    grad_donor, grad_accept, grad_point, gain, loss, held, act_donor, act_accept,
):
    count = held.shape[0]
    for step, part in ((0, own), (3, behind), (1, ahead)):
        held[lax.rem(place[1] + step, count)] = part[...]
    opposite = lax.rem(place[1] + 2, count)
    middle = low.shape[0]
    held[opposite, :middle, :] = low[...]
    held[opposite, middle:, :] = high[...]
    channels = grad_donor.shape[0]
    inner = act_donor.shape[0]
    chunk_rows = CHUNK_ROWS + EXTRA_ROWS
    piece = 0
    for into in (grad_donor, grad_accept, act_donor, act_accept):
        for lane in range(2):
            for k in range(into.shape[0] // PIECE):
                chunk, third = piece // 3, piece % 3
                at = (chunk % 4) * chunk_rows + third * PIECE
                into[k * PIECE : (k + 1) * PIECE, lane * 128 : (lane + 1) * 128] = held[
                    chunk // 4, at : at + PIECE, :
                ]
                piece += 1

    grad_point[...] = (
        dot_t(act_donor[...], donor_w[...]) + dot_t(act_accept[...], accept_w[...])
    ).astype(BF16)

    for chunk in range(channels // 128 + 1):
        at = (chunk % 4) * chunk_rows + CHUNK_ROWS
        block = held[chunk // 4, at : at + EXTRA_ROWS, :].astype(F32)
        value = block[0:1, :] + block[8:9, :]
        if chunk < channels // 128:
            gain[:, chunk * 128 : (chunk + 1) * 128] = value
        else:
            loss[...] = value


def swapped(block, first, between_lines=True):
    count = lax.axis_size(SEQ)
    pairs = [(i, i + 1) for i in range(first, count - 1, 2) if between_lines or i % 8 < 7]
    return lax.ppermute(block, SEQ, pairs + [(j, i) for i, j in pairs])


def swap_parts(parts, axis):
    return lax.all_to_all(parts, axis, 0, 0, tiled=True)


def on_device(
    activations, norm_gain, dilated_tap_weight, point_weight, donor_weight, acceptor_weight,
    pair_sites, pair_count, order, eye, pick,
):
    tokens = activations[0]
    rows, channels = tokens.shape
    tap_count, _, inner = dilated_tap_weight.shape
    heads = donor_weight.shape[1]
    blocks = rows // PANEL
    shape = jax.ShapeDtypeStruct
    here = lax.axis_index(SEQ)
    line = lax.axis_index(("zb", "zq"))
    is_odd = (lax.axis_index("zq") & 1) > 0
    odd = is_odd.astype(jnp.int32)[None]
    start, end = tokens[:STEP], tokens[rows - STEP :]
    even_edge = swapped(jnp.where(is_odd, start, end), 0)
    odd_edge = swapped(jnp.where(is_odd, end, start), 1)
    gain = norm_gain[None]
    sites = pair_sites[0]
    first = here * blocks
    live = (jnp.arange(SLOTS, dtype=jnp.int32) < pair_count[0, 0]).astype(jnp.int32)
    meta = jnp.stack(
        [
            sites[:, 0] // PANEL - first,
            sites[:, 0] % PANEL,
            sites[:, 1] // PANEL - first,
            sites[:, 1] % PANEL,
            live,
        ]
        + [jnp.zeros_like(live)] * 3,
        axis=1,
    )
    meta_rows = jnp.pad(meta.astype(BF16), ((0, 0), (0, heads - meta.shape[1])))

    mine, factor = call(
        own_kernel, [shape((rows, channels), BF16)] * 2, [VM] * 2, 12, 2_000_000_000
    )(tokens, gain)
    (odd_hidden,) = call(edge_kernel, [shape((STEP, channels), BF16)], [VM] * 2, 8, 2_000_000_000)(odd_edge, gain)
    feat = shape((rows + SLOTS, heads), BF16)
    hidden, conv, act, embed, even_feat, odd_feat = call(
        forward_kernel,
        [
            shape((rows + 2 * STEP, channels), BF16),
            shape((rows, inner), F32),
            shape((rows, inner), BF16),
            shape((rows, channels), BF16),
            feat,
            feat,
        ],
        [SM] + [VM] * 10,
        20,
        4_000_000_000,
    )(
        odd, tokens, mine, even_edge, odd_hidden, gain, dilated_tap_weight, point_weight,
        donor_weight, acceptor_weight, meta_rows,
    )

    acc_shapes = [shape((rows, heads), F32), shape((rows, heads), F32), shape((PANEL, PANEL), F32)]
    acc = call(
        lambda *refs: pair_kernel(0, *refs), acc_shapes, [SM] * 2 + [VM] * 2, 12, 2_000_000_000
    )(1 - odd, meta, even_feat, odd_feat)
    edge_factor, slope, hidden_t, act_t, embed_t = call(
        side_kernel,
        [
            shape((2 * STEP, channels), BF16),
            shape((rows, inner), F32),
            shape((channels, rows + 2 * STEP), BF16),
            shape((inner, rows), BF16),
            shape((channels, rows), BF16),
        ],
        [SM] + [VM] * 9,
        20,
        6_000_000_000,
    )(odd, even_edge, odd_edge, gain, hidden, conv, act, embed, order, eye)
    count = lax.axis_size(SEQ)
    starts = range(0, count, 8)
    wide_pairs = [(i + k, i - 4 + k) for i in starts if i > 0 for k in (2, 3)]
    wide_pairs += [(i + k, i + 4 + k) for i in starts if i + 8 < count for k in (4, 5)]
    relay_pairs = [(i + 6, i + 7) for i in starts] + [(i + 1, i) for i in starts]
    wide_feat = jnp.where((line == 2) | (line == 5), even_feat, odd_feat)
    wide = lax.ppermute(wide_feat, SEQ, wide_pairs)
    relay = lax.ppermute(wide, SEQ, relay_pairs)
    at_end = (line == 0) | (line == 7)
    near_end = (line == 1) | (line == 6)
    short_far, long_far = odd_feat, even_feat
    for distance in range(1, SPAN + 1):
        if distance == 1:
            short_far, long_far = swapped(odd_feat, 0), swapped(even_feat, 1)
        else:
            short_far, long_far = swapped(long_far, 0), swapped(short_far, 1, distance <= 2)
        short_use, long_use = short_far, long_far
        if distance == 3:
            long_use = jnp.where(at_end, relay, long_far)
        if distance == 4:
            short_use = jnp.where(near_end, wide, short_far)
            long_use = jnp.where(at_end, wide, long_far)
        far_meta = jnp.where(is_odd, short_use[rows:, :8], long_use[rows:, :8]).astype(jnp.int32)
        acc = call(
            lambda *refs, distance=distance: pair_kernel(distance, *refs),
            acc_shapes,
            [SM] * 3 + [VM] * 7,
            12,
            2_500_000_000,
        )(1 - odd, meta, far_meta, even_feat, odd_feat, long_use, short_use, *acc)

    chunk = CHUNK_ROWS + EXTRA_ROWS
    lanes = inner // 128
    slabs = tap_count * lanes
    y = lax.axis_index("y")
    place = jnp.stack([lax.axis_index("core"), y, lax.axis_index("zb")]).astype(jnp.int32)
    half = shape((4, slabs, PIECE, 128), BF16)
    keep, send, d_conv, d_feat = call(
        tap_grad_kernel,
        [half, half, shape((rows, inner), BF16), shape((rows, 2 * heads), BF16)],
        [SM] + [VM] * 7,
        24,
        4_000_000_000,
    )(place, acc[0], acc[1], point_weight, donor_weight, acceptor_weight, slope, hidden_t)
    received = lax.ppermute(send, "core", [(0, 1), (1, 0)])
    (head_sum,) = call(
        head_grad_kernel, [shape((4, 4, chunk, 128), BF16)], [SM] + [VM] * 8, 20, 4_000_000_000
    )(place, d_conv, d_feat, acc[2], dilated_tap_weight, factor, edge_factor, act_t, embed_t)

    first_pairs = [(0, 1), (1, 0), (2, 3), (3, 2)]
    second_pairs = [(1, 2), (2, 1), (3, 0), (0, 3)]
    quick = 1_000_000
    conv_kept, conv_send = call(
        core_sum_kernel, [shape((2, slabs, PIECE, 128), F32), shape((2, slabs, PIECE, 128), BF16)],
        [VM] * 2, 12, quick,
    )(keep, received)
    other = lax.ppermute(head_sum[2:], "y", first_pairs)
    heads_kept, heads_send = call(
        head_sum_kernel, [shape((4, chunk, 128), F32), shape((4, chunk, 128), BF16)], [VM] * 2, 12, quick
    )(head_sum, other)
    other = lax.ppermute(conv_send, "y", second_pairs)
    conv_kept, conv_send = call(
        tap_sum_kernel, [shape((slabs, PIECE, 128), F32), shape((slabs, PIECE, 128), BF16)],
        [VM] * 2, 12, quick,
    )(conv_kept, other)
    heads_in = lax.ppermute(heads_send, "y", second_pairs)
    conv_in = lax.ppermute(conv_send, "y", first_pairs)

    joint = chunk + 224
    (both,) = call(join_kernel, [shape((4, joint, 128), BF16)], [VM] * 4, 12, quick)(
        heads_kept, heads_in, conv_kept, conv_in
    )
    parts = swap_parts(both, "zq")
    head_line, tap_line = call(
        line_sum_kernel, [shape((chunk, 128), BF16), shape((4, 112, 128), BF16)], [VM] * 2, 8, quick
    )(parts, pick)
    received = lax.ppermute(head_line, "zb", [(0, 1), (1, 0)])
    tap_parts = swap_parts(tap_line, ("zb", "zhi"))
    head_parts, conv_sum = call(
        far_sum_kernel, [shape((4, chunk, 128), BF16), shape((112, 128), BF16)], [VM] * 3, 8, quick
    )(head_line, received, tap_parts)

    head_rows = 4 * chunk
    head_sum = swap_parts(head_parts, "zq").reshape(head_rows, 128)
    line = [
        lax.ppermute(conv_sum, "x", [(i, (i + step) % 4) for i in range(4)]) for step in (1, 2, 3)
    ]
    (conv_sum,) = call(line_total_kernel, [shape((112, 128), F32)], [VM] * 4, 8, quick)(conv_sum, *line)
    head_sum, conv_sum = lax.optimization_barrier((head_sum, conv_sum))
    other = lax.ppermute(conv_sum, "core", [(0, 1), (1, 0)])
    around = [(i, (i + 1) % 4) for i in range(4)]
    back = [(j, i) for i, j in around]
    behind = lax.ppermute(head_sum, "y", around)
    ahead = lax.ppermute(head_sum, "y", back)
    low = lax.ppermute(behind[: head_rows // 2], "y", around)
    high = lax.ppermute(ahead[head_rows // 2 :], "y", back)
    is_first = lax.axis_index("core") == 0
    pieces = jnp.stack([jnp.where(is_first, conv_sum, other), jnp.where(is_first, other, conv_sum)])
    pieces = pieces[:, : slabs * 12].reshape(2, tap_count, lanes, 12, 128)
    grad_conv = pieces.transpose(1, 0, 3, 2, 4).reshape(tap_count, 24, inner)
    head_weight = shape((channels, heads), BF16)
    grad_donor, grad_accept, grad_point, grad_gain, loss = call(
        finish_kernel,
        [head_weight, head_weight, shape((inner, channels), BF16), shape((1, channels), F32), shape((1, 128), F32)],
        [SM] + [VM] * 7,
        20,
        1_000_000_000,
        [
            pltpu.VMEM((4, head_rows, 128), BF16),
            pltpu.VMEM((inner, heads), BF16),
            pltpu.VMEM((inner, heads), BF16),
        ],
    )(place, head_sum, behind, ahead, low, high, donor_weight, acceptor_weight)
    return grad_conv, grad_point[None], grad_donor[None], grad_accept[None], grad_gain, loss[0, :1]


def channel_order():
    core, y, zq, zb, k = np.meshgrid(*[np.arange(n) for n in (2, 4, 4, 2, 12)], indexing="ij")
    channel = (24 * (8 * y + 4 * zb + zq) + 12 * core + k).reshape(-1)
    return np.eye(channel.size, dtype=np.float32)[channel]


def zb_halves():
    pick = np.zeros((224, 224), np.float32)
    for zb in range(2):
        for slab in range(9):
            for k in range(12):
                pick[112 * zb + 12 * slab + k, 24 * slab + 12 * zb + k] = 1.0
    return pick


def solution(mesh):
    fine = Mesh(mesh.devices.reshape(4, 2, 4, 2, 4, 2), SEQ + BATCH)
    placed = jax.shard_map(
        on_device,
        mesh=fine,
        in_specs=(
            P(BATCH, SEQ, None),
            P(),
            P(),
            P(),
            P(),
            P(),
            P(BATCH, SEQ, None),
            P(BATCH, SEQ),
            P(),
            P(),
            P(),
        ),
        out_specs=(
            P(None, SEQ, None),
            P(BATCH, None, None),
            P(BATCH, None, None),
            P(BATCH, None, None),
            P(BATCH, None),
            P(BATCH),
        ),
        check_vma=False,
    )

    def run(*arrays):
        order = jnp.asarray(channel_order(), BF16)
        eye = jnp.eye(order.shape[0], dtype=BF16)
        return placed(*arrays, order, eye, jnp.asarray(zb_halves(), BF16))

    return run
```

```python
import jax
import jax.numpy as jnp
import numpy as np
from jax import lax
from jax.experimental import pallas as pl
from jax.experimental.pallas import tpu as pltpu
from jax.sharding import Mesh
from jax.sharding import PartitionSpec as P

STEP = 128
PANEL = 128
SPAN = 4
SLOTS = 16
EPSILON = 1e-06
LOSS_WEIGHT = 1.0 / 128.0
SEQ = ("y", "zb", "zq")
BATCH = ("zhi", "x", "core")
F32 = jnp.float32
BF16 = jnp.bfloat16
ROOT = 0.7978845608028654
CUBIC = 0.044715
PIECE = 96
CHUNK_ROWS = 288
EXTRA_ROWS = 16


def dot(a, b):
    return lax.dot_general(a, b, (((1,), (0,)), ((), ())), preferred_element_type=F32)


def dot_t(a, b):
    return lax.dot_general(a, b, (((1,), (1,)), ((), ())), preferred_element_type=F32)


def gelu(v):
    return 0.5 * v * (1.0 + jnp.tanh(ROOT * (v + CUBIC * (v * v * v))))


def gelu_both(v):
    square = v * v
    t = jnp.tanh(ROOT * (v + CUBIC * (square * v)))
    half = 0.5 * (1.0 + t)
    return v * half, half + 0.5 * v * (1.0 - t * t) * (ROOT * (1.0 + 3.0 * CUBIC * square))


def rms(v):
    return lax.rsqrt(jnp.mean(v * v, axis=-1, keepdims=True) + EPSILON)


def call(kernel, outs, specs, megabytes, flops, scratch=()):
    return pl.pallas_call(
        kernel,
        out_shape=outs,
        in_specs=specs,
        out_specs=[VM] * len(outs),
        scratch_shapes=list(scratch),
        compiler_params=pltpu.CompilerParams(vmem_limit_bytes=megabytes * 1024 * 1024),
        cost_estimate=pl.CostEstimate(flops=flops, bytes_accessed=1_000_000, transcendentals=0),
    )


VM = pl.BlockSpec(memory_space=pltpu.VMEM)
SM = pl.BlockSpec(memory_space=pltpu.SMEM)


def own_kernel(tok, gain, hidden, factor):
    @pl.loop(0, tok.shape[0] // STEP)
    def _(i):
        here = pl.ds(pl.multiple_of(i * STEP, STEP), STEP)
        v = tok[here, :].astype(F32)
        unit = v * rms(v)
        value, slope = gelu_both(unit * gain[...])
        hidden[here, :] = value.astype(BF16)
        factor[here, :] = (slope * unit).astype(BF16)


def edge_kernel(edge, gain, hidden):
    v = edge[...].astype(F32)
    hidden[...] = gelu(v * rms(v) * gain[...]).astype(BF16)


def forward_kernel(
    odd, tok, mine, even_edge, odd_hidden, gain, taps, point, donor_w, accept_w, meta,
    hidden, conv_out, act_out, embed_out, even_feat, odd_feat,
):
    rows = tok.shape[0]
    is_odd = odd[0] > 0
    v = even_edge[...].astype(F32)
    even_hidden = gelu(v * rms(v) * gain[...]).astype(BF16)
    hidden[pl.ds(0, STEP), :] = jnp.where(is_odd, even_hidden, odd_hidden[...])
    hidden[pl.ds(STEP + rows, STEP), :] = jnp.where(is_odd, odd_hidden[...], even_hidden)
    hidden[pl.ds(STEP, rows), :] = mine[...]

    conv = dot(hidden[:rows, :], taps[0])
    for tap in range(1, taps.shape[0]):
        conv = conv + dot(hidden[tap * STEP : tap * STEP + rows, :], taps[tap])
    conv_out[...] = conv
    act = gelu(conv).astype(BF16)
    act_out[...] = act
    embed = (tok[...].astype(F32) + dot(act, point[...])).astype(BF16)
    embed_out[...] = embed
    donor = dot(embed, donor_w[...]).astype(BF16)
    accept = dot(embed, accept_w[...]).astype(BF16)
    even_feat[:rows, :] = jnp.where(is_odd, donor, accept)
    odd_feat[:rows, :] = jnp.where(is_odd, accept, donor)
    even_feat[pl.ds(rows, SLOTS), :] = meta[...]
    odd_feat[pl.ds(rows, SLOTS), :] = meta[...]


def side_kernel(
    odd, even_edge, odd_edge, gain, hidden, conv, act, embed, order, eye,
    factor, slope, hidden_t, act_t, embed_t,
):
    is_odd = odd[0] > 0
    low = jnp.where(is_odd, even_edge[...], odd_edge[...])
    high = jnp.where(is_odd, odd_edge[...], even_edge[...])
    for edge, at in ((low, 0), (high, STEP)):
        v = edge.astype(F32)
        unit = v * rms(v)
        factor[pl.ds(at, STEP), :] = (gelu_both(unit * gain[...])[1] * unit).astype(BF16)

    @pl.loop(0, conv.shape[0] // STEP)
    def _(i):
        here = pl.ds(pl.multiple_of(i * STEP, STEP), STEP)
        slope[here, :] = gelu_both(conv[here, :])[1]

    hidden_t[...] = dot_t(order[...], hidden[...]).astype(BF16)
    embed_t[...] = dot_t(eye[...], embed[...]).astype(BF16)
    inner = act.shape[1]
    act_t[...] = dot_t(eye[:inner, :inner], act[...]).astype(BF16)


def copy_kernel(source, target):
    target[...] = source[...]


def pair_kernel(distance, *refs):
    if distance == 0:
        odd, own, even0, odd0, d_donor, d_accept, loss = refs
        d_donor[...] = jnp.zeros_like(d_donor)
        d_accept[...] = jnp.zeros_like(d_accept)
        loss[...] = jnp.zeros_like(loss)
    else:
        odd, own, far, even0, odd0, even1, odd1, dd_in, da_in, loss_in, d_donor, d_accept, loss = refs
        d_donor[...] = dd_in[...]
        d_accept[...] = da_in[...]
        loss[...] = loss_in[...]
    is_odd = odd[0] > 0
    scale = even0.shape[1] ** (-0.5)
    per_device = d_donor.shape[0] // PANEL
    row = lax.broadcasted_iota(jnp.int32, (PANEL, PANEL), 0)
    col = lax.broadcasted_iota(jnp.int32, (PANEL, PANEL), 1)

    def place(block):
        return pl.ds(pl.multiple_of(block * PANEL, PANEL), PANEL)

    def own_donor(block):
        return jnp.where(is_odd, odd0[place(block), :], even0[place(block), :])

    def own_accept(block):
        return jnp.where(is_odd, even0[place(block), :], odd0[place(block), :])

    if distance == 0:
        far_accept, far_donor = own_accept, None
    else:

        def far_accept(block):
            return jnp.where(is_odd, odd1[place(block), :], even1[place(block), :])

        def far_donor(block):
            return jnp.where(is_odd, even1[place(block), :], odd1[place(block), :])

    def visit(meta, j, donors, acceptors, is_owner):
        accept_block = meta[j, 2] - distance * per_device
        here = (meta[j, 4] > 0) & (accept_block >= 0) & (accept_block < per_device)

        @pl.when(here)
        def _():
            donor_block = meta[j, 0]
            dpan = donors(donor_block)
            apan = acceptors(accept_block)
            scores = dot_t(dpan, apan) * scale
            target = ((row == meta[j, 1]) & (col == meta[j, 3])).astype(F32)
            small = jnp.exp(-jnp.abs(scores))
            inverse = 1.0 / (1.0 + small)
            sigmoid = jnp.where(scores >= 0, inverse, small * inverse)
            dscore = ((sigmoid - target) * LOSS_WEIGHT).astype(BF16)
            if is_owner:
                loss[...] += (jnp.maximum(scores, 0.0) + jnp.log1p(small)) - target * scores
                d_donor[place(donor_block), :] += dot(dscore, apan) * scale
            if distance == 0 or not is_owner:
                d_accept[place(accept_block), :] += scale * lax.dot_general(
                    dscore, dpan, (((0,), (0,)), ((), ())), preferred_element_type=F32
                )

    @pl.loop(0, SLOTS)
    def _(j):
        visit(own, j, own_donor, far_accept, True)
        if distance > 0:
            visit(far, j, far_donor, own_accept, False)


def relative(target, y, first):
    code = (target ^ (target >> 1)) ^ (y ^ (y >> 1))
    low, high = code & 1, code >> 1
    return low * 2 + high if first == 0 else high * 2 + low


def tap_grad_kernel(
    place, d_donor, d_accept, point, donor_w, accept_w, slope, hidden_t,
    keep, send, d_conv, d_feat,
):
    rows, heads = d_donor.shape
    channels = hidden_t.shape[0]

    dd = d_donor[...].astype(BF16)
    da = d_accept[...].astype(BF16)
    d_feat[:, :heads] = dd
    d_feat[:, heads:] = da
    d_embed = (dot_t(dd, donor_w[...]) + dot_t(da, accept_w[...])).astype(BF16)
    d_conv[...] = (dot_t(d_embed, point[...]) * slope[...]).astype(BF16)

    lanes = d_conv.shape[1] // 128
    half_rows = channels // 2
    slab = [relative(target, place[1], 1) for target in range(4)]
    for tap in range(3):
        for half in range(2):
            part = dot(
                hidden_t[half * half_rows : (half + 1) * half_rows, tap * STEP : tap * STEP + rows],
                d_conv[...],
            ).astype(BF16)

            def store(into, part=part, tap=tap):
                for k in range(4):
                    for lane in range(lanes):
                        into[slab[k], tap * lanes + lane] = part[
                            k * PIECE : (k + 1) * PIECE, lane * 128 : (lane + 1) * 128
                        ]

            pl.when(place[0] == half)(lambda: store(keep))
            pl.when(place[0] != half)(lambda: store(send))


def head_grad_kernel(
    place, d_conv, d_feat, loss, taps, factor, edge_factor, act_t, embed_t, head_sum,
):
    rows = d_conv.shape[0]
    channels = embed_t.shape[0]
    inner = act_t.shape[0]
    slab = [relative(target, place[1], 0) for target in range(4)]

    def put(part, base, group_rows, first):
        for lane in range(4):
            for k in range(part.shape[0] // PIECE):
                piece = first + lane * (group_rows // PIECE) + k + base
                chunk, third = piece // 3, piece % 3
                head_sum[slab[chunk // 4], chunk % 4, third * PIECE : (third + 1) * PIECE, :] = part[
                    k * PIECE : (k + 1) * PIECE, lane * 128 : (lane + 1) * 128
                ]

    for i in range(2):
        part = dot(embed_t[i * 4 * PIECE : (i + 1) * 4 * PIECE, :], d_feat[...]).astype(BF16)
        put(part, 4 * i, channels, 0)
    put(dot(act_t[...], d_feat[...]).astype(BF16), 0, inner, 4 * channels // PIECE)

    total = jnp.zeros((8, channels), F32)
    edge = edge_factor.shape[0] // 2
    for tap in range(taps.shape[0]):
        product = dot_t(d_conv[...], taps[tap])
        if tap == 0:
            weights = jnp.concatenate([edge_factor[:edge, :], factor[: rows - edge, :]], axis=0)
        elif tap == 1:
            weights = factor[...]
        else:
            weights = jnp.concatenate([factor[edge:, :], edge_factor[edge:, :]], axis=0)
        product = product * weights.astype(F32)
        total = total + jnp.sum(product.reshape(rows // 8, 8, channels), axis=0)
    gain = jnp.sum(total, axis=0, keepdims=True)
    loss_row = jnp.sum(loss[...], axis=0, keepdims=True) * LOSS_WEIGHT
    loss_all = jnp.broadcast_to(jnp.sum(loss_row, axis=1, keepdims=True), (1, 128))
    at_row = lax.broadcasted_iota(jnp.int32, (EXTRA_ROWS, 128), 0)
    for chunk in range(16):
        if chunk < channels // 128:
            value = gain[:, chunk * 128 : (chunk + 1) * 128]
        elif chunk == channels // 128:
            value = loss_all
        else:
            value = jnp.zeros((1, 128), F32)
        coarse = value.astype(BF16).astype(F32)
        block = jnp.where(at_row == 0, coarse, 0.0) + jnp.where(at_row == 8, value - coarse, 0.0)
        head_sum[slab[chunk // 4], chunk % 4, CHUNK_ROWS:, :] = block.astype(BF16)


def split_rows(total):
    value = total[CHUNK_ROWS : CHUNK_ROWS + 8] + total[CHUNK_ROWS + 8 : CHUNK_ROWS + 16]
    coarse = value.astype(BF16).astype(F32)
    return jnp.concatenate([total[:CHUNK_ROWS], coarse, value - coarse], axis=0).astype(BF16)


def core_sum_kernel(taps, received, kept, send):
    for k in range(2):
        for slab in range(taps.shape[1]):
            kept[k, slab] = taps[k, slab].astype(F32) + received[k, slab].astype(F32)
            send[k, slab] = (
                taps[k + 2, slab].astype(F32) + received[k + 2, slab].astype(F32)
            ).astype(BF16)


def head_sum_kernel(head, received, kept, send):
    for zq in range(4):
        kept[zq] = head[0, zq].astype(F32) + received[0, zq].astype(F32)
        send[zq] = split_rows(head[1, zq].astype(F32) + received[1, zq].astype(F32))


def tap_sum_kernel(before, received, kept, send):
    for slab in range(before.shape[1]):
        kept[slab] = before[0, slab] + received[0, slab].astype(F32)
        send[slab] = (before[1, slab] + received[1, slab].astype(F32)).astype(BF16)


def join_kernel(head, head_in, taps, taps_in, both):
    chunk_rows = head.shape[1]
    for zq in range(4):
        both[zq, :chunk_rows, :] = split_rows(head[zq] + head_in[zq].astype(F32))
        here = slice(zq * 24, (zq + 1) * 24)
        parts = [taps[k, here] + taps_in[k, here].astype(F32) for k in range(taps.shape[0])]
        parts.append(jnp.zeros((8, 128), F32))
        both[zq, chunk_rows:, :] = jnp.concatenate(parts, axis=0).astype(BF16)


def line_sum_kernel(place, parts, pick, send, mine):
    total = parts[0].astype(F32)
    for zq in range(1, 4):
        total = total + parts[zq].astype(F32)
    chunk_rows = CHUNK_ROWS + EXTRA_ROWS
    send[:chunk_rows, :] = split_rows(total[:chunk_rows])
    taps = total[chunk_rows:].astype(BF16)
    half = mine.shape[0]
    zb = place[2]

    def picked(which):
        return dot(pick[pl.ds(pl.multiple_of(which * half, half), half), :], taps).astype(BF16)

    send[chunk_rows:, :] = picked(1 - zb)
    mine[...] = picked(zb)


def far_sum_kernel(sent, received, mine, one, two, head, taps):
    chunk_rows = head.shape[1]
    total = split_rows(sent[:chunk_rows, :].astype(F32) + received[:chunk_rows, :].astype(F32))
    for zq in range(head.shape[0]):
        head[zq] = total
    near = mine[...].astype(F32) + received[chunk_rows:, :].astype(F32)
    taps[...] = (near + (one[...].astype(F32) + two[...].astype(F32))).astype(BF16)


def line_total_kernel(own, one, two, three, total):
    even = own[...].astype(F32) + two[...].astype(F32)
    total[...] = even + (one[...].astype(F32) + three[...].astype(F32))


def finish_kernel(
    place, own, behind, ahead, low, high, donor_w, accept_w,
    grad_donor, grad_accept, grad_point, gain, loss, held, act_donor, act_accept,
):
    count = held.shape[0]
    for step, part in ((0, own), (3, behind), (1, ahead)):
        held[lax.rem(place[1] + step, count)] = part[...]
    opposite = lax.rem(place[1] + 2, count)
    middle = low.shape[0]
    held[opposite, :middle, :] = low[...]
    held[opposite, middle:, :] = high[...]
    channels = grad_donor.shape[0]
    inner = act_donor.shape[0]
    chunk_rows = CHUNK_ROWS + EXTRA_ROWS
    piece = 0
    for into in (grad_donor, grad_accept, act_donor, act_accept):
        for lane in range(2):
            for k in range(into.shape[0] // PIECE):
                chunk, third = piece // 3, piece % 3
                at = (chunk % 4) * chunk_rows + third * PIECE
                into[k * PIECE : (k + 1) * PIECE, lane * 128 : (lane + 1) * 128] = held[
                    chunk // 4, at : at + PIECE, :
                ]
                piece += 1

    grad_point[...] = (
        dot_t(act_donor[...], donor_w[...]) + dot_t(act_accept[...], accept_w[...])
    ).astype(BF16)

    for chunk in range(channels // 128 + 1):
        at = (chunk % 4) * chunk_rows + CHUNK_ROWS
        block = held[chunk // 4, at : at + EXTRA_ROWS, :].astype(F32)
        value = block[0:1, :] + block[8:9, :]
        if chunk < channels // 128:
            gain[:, chunk * 128 : (chunk + 1) * 128] = value
        else:
            loss[...] = value


def swapped(block, first, between_lines=True):
    count = lax.axis_size(SEQ)
    pairs = [(i, i + 1) for i in range(first, count - 1, 2) if between_lines or i % 8 < 7]
    return lax.ppermute(block, SEQ, pairs + [(j, i) for i, j in pairs])


def swap_parts(parts, axis):
    return lax.all_to_all(parts, axis, 0, 0, tiled=True)


def on_device(
    activations, norm_gain, dilated_tap_weight, point_weight, donor_weight, acceptor_weight,
    pair_sites, pair_count, order, eye, pick,
):
    tokens = activations[0]
    rows, channels = tokens.shape
    tap_count, _, inner = dilated_tap_weight.shape
    heads = donor_weight.shape[1]
    blocks = rows // PANEL
    shape = jax.ShapeDtypeStruct
    here = lax.axis_index(SEQ)
    line = lax.axis_index(("zb", "zq"))
    is_odd = (lax.axis_index("zq") & 1) > 0
    odd = is_odd.astype(jnp.int32)[None]
    start, end = tokens[:STEP], tokens[rows - STEP :]
    even_edge = swapped(jnp.where(is_odd, start, end), 0)
    odd_edge = swapped(jnp.where(is_odd, end, start), 1)
    gain = norm_gain[None]
    sites = pair_sites[0]
    first = here * blocks
    live = (jnp.arange(SLOTS, dtype=jnp.int32) < pair_count[0, 0]).astype(jnp.int32)
    meta = jnp.stack(
        [
            sites[:, 0] // PANEL - first,
            sites[:, 0] % PANEL,
            sites[:, 1] // PANEL - first,
            sites[:, 1] % PANEL,
            live,
        ]
        + [jnp.zeros_like(live)] * 3,
        axis=1,
    )
    meta_rows = jnp.pad(meta.astype(BF16), ((0, 0), (0, heads - meta.shape[1])))

    mine, factor = call(
        own_kernel, [shape((rows, channels), BF16)] * 2, [VM] * 2, 12, 2_000_000_000
    )(tokens, gain)
    (odd_hidden,) = call(edge_kernel, [shape((STEP, channels), BF16)], [VM] * 2, 8, 2_000_000_000)(odd_edge, gain)
    feat = shape((rows + SLOTS, heads), BF16)
    hidden, conv, act, embed, even_feat, odd_feat = call(
        forward_kernel,
        [
            shape((rows + 2 * STEP, channels), BF16),
            shape((rows, inner), F32),
            shape((rows, inner), BF16),
            shape((rows, channels), BF16),
            feat,
            feat,
        ],
        [SM] + [VM] * 10,
        20,
        4_000_000_000,
    )(
        odd, tokens, mine, even_edge, odd_hidden, gain, dilated_tap_weight, point_weight,
        donor_weight, acceptor_weight, meta_rows,
    )

    acc_shapes = [shape((rows, heads), F32), shape((rows, heads), F32), shape((PANEL, PANEL), F32)]
    acc = call(
        lambda *refs: pair_kernel(0, *refs), acc_shapes, [SM] * 2 + [VM] * 2, 12, 2_000_000_000
    )(1 - odd, meta, even_feat, odd_feat)
    edge_factor, slope, hidden_t, act_t, embed_t = call(
        side_kernel,
        [
            shape((2 * STEP, channels), BF16),
            shape((rows, inner), F32),
            shape((channels, rows + 2 * STEP), BF16),
            shape((inner, rows), BF16),
            shape((channels, rows), BF16),
        ],
        [SM] + [VM] * 9,
        20,
        6_000_000_000,
    )(odd, even_edge, odd_edge, gain, hidden, conv, act, embed, order, eye)
    count = lax.axis_size(SEQ)
    starts = range(0, count, 8)
    wide_pairs = [(i + k, i - 4 + k) for i in starts if i > 0 for k in (2, 3)]
    wide_pairs += [(i + k, i + 4 + k) for i in starts if i + 8 < count for k in (4, 5)]
    relay_pairs = [(i + 6, i + 7) for i in starts] + [(i + 1, i) for i in starts]
    wide_feat = jnp.where((line == 2) | (line == 5), even_feat, odd_feat)
    wide = lax.ppermute(wide_feat, SEQ, wide_pairs)
    relay = lax.ppermute(wide, SEQ, relay_pairs)
    at_end = (line == 0) | (line == 7)
    near_end = (line == 1) | (line == 6)
    short_far, long_far = odd_feat, even_feat
    for distance in range(1, SPAN + 1):
        if distance == 1:
            short_far, long_far = swapped(odd_feat, 0), swapped(even_feat, 1)
            (short_far,) = call(copy_kernel, [feat], [VM], 4, 2000000000)(short_far)
        else:
            short_far, long_far = swapped(long_far, 0), swapped(short_far, 1, distance <= 2)
        short_use, long_use = short_far, long_far
        if distance == 3:
            long_use = jnp.where(at_end, relay, long_far)
        if distance == 4:
            short_use = jnp.where(near_end, wide, short_far)
            long_use = jnp.where(at_end, wide, long_far)
        far_meta = jnp.where(is_odd, short_use[rows:, :8], long_use[rows:, :8]).astype(jnp.int32)
        acc = call(
            lambda *refs, distance=distance: pair_kernel(distance, *refs),
            acc_shapes,
            [SM] * 3 + [VM] * 7,
            12,
            2_500_000_000,
        )(1 - odd, meta, far_meta, even_feat, odd_feat, long_use, short_use, *acc)

    chunk = CHUNK_ROWS + EXTRA_ROWS
    lanes = inner // 128
    slabs = tap_count * lanes
    y = lax.axis_index("y")
    place = jnp.stack([lax.axis_index("core"), y, lax.axis_index("zb")]).astype(jnp.int32)
    half = shape((4, slabs, PIECE, 128), BF16)
    keep, send, d_conv, d_feat = call(
        tap_grad_kernel,
        [half, half, shape((rows, inner), BF16), shape((rows, 2 * heads), BF16)],
        [SM] + [VM] * 7,
        24,
        4_000_000_000,
    )(place, acc[0], acc[1], point_weight, donor_weight, acceptor_weight, slope, hidden_t)
    received = lax.ppermute(send, "core", [(0, 1), (1, 0)])
    (head_sum,) = call(
        head_grad_kernel, [shape((4, 4, chunk, 128), BF16)], [SM] + [VM] * 8, 20, 4_000_000_000
    )(place, d_conv, d_feat, acc[2], dilated_tap_weight, factor, edge_factor, act_t, embed_t)

    first_pairs = [(0, 1), (1, 0), (2, 3), (3, 2)]
    second_pairs = [(1, 2), (2, 1), (3, 0), (0, 3)]
    quick = 1_000_000
    conv_kept, conv_send = call(
        core_sum_kernel, [shape((2, slabs, PIECE, 128), F32), shape((2, slabs, PIECE, 128), BF16)],
        [VM] * 2, 12, quick,
    )(keep, received)
    other = lax.ppermute(head_sum[2:], "y", first_pairs)
    heads_kept, heads_send = call(
        head_sum_kernel, [shape((4, chunk, 128), F32), shape((4, chunk, 128), BF16)], [VM] * 2, 12, quick
    )(head_sum, other)
    other = lax.ppermute(conv_send, "y", second_pairs)
    conv_kept, conv_send = call(
        tap_sum_kernel, [shape((slabs, PIECE, 128), F32), shape((slabs, PIECE, 128), BF16)],
        [VM] * 2, 12, quick,
    )(conv_kept, other)
    heads_in = lax.ppermute(heads_send, "y", second_pairs)
    conv_in = lax.ppermute(conv_send, "y", first_pairs)

    joint = chunk + 224
    (both,) = call(join_kernel, [shape((4, joint, 128), BF16)], [VM] * 4, 12, quick)(
        heads_kept, heads_in, conv_kept, conv_in
    )
    parts = swap_parts(both, "zq")
    sent, mine = call(
        line_sum_kernel, [shape((chunk + 112, 128), BF16), shape((112, 128), BF16)],
        [SM] + [VM] * 2, 8, quick,
    )(place, parts, pick)
    received = lax.ppermute(sent, "zb", [(0, 1), (1, 0)])
    across = lax.ppermute(mine, "zhi", [(0, 1), (1, 0)])
    corner = lax.ppermute(
        sent[chunk:], ("zb", "zhi"), [(0, 3), (3, 0), (1, 2), (2, 1)]
    )
    head_parts, conv_sum = call(
        far_sum_kernel, [shape((4, chunk, 128), BF16), shape((112, 128), BF16)], [VM] * 5, 8, quick
    )(sent, received, mine, across, corner)

    head_rows = 4 * chunk
    head_sum = swap_parts(head_parts, "zq").reshape(head_rows, 128)
    line = [
        lax.ppermute(conv_sum, "x", [(i, (i + step) % 4) for i in range(4)]) for step in (1, 2, 3)
    ]
    (conv_sum,) = call(line_total_kernel, [shape((112, 128), F32)], [VM] * 4, 8, quick)(conv_sum, *line)
    head_sum, conv_sum = lax.optimization_barrier((head_sum, conv_sum))
    other = lax.ppermute(conv_sum, "core", [(0, 1), (1, 0)])
    around = [(i, (i + 1) % 4) for i in range(4)]
    back = [(j, i) for i, j in around]
    behind = lax.ppermute(head_sum, "y", around)
    ahead = lax.ppermute(head_sum, "y", back)
    low = lax.ppermute(behind[: head_rows // 2], "y", around)
    high = lax.ppermute(ahead[head_rows // 2 :], "y", back)
    is_first = lax.axis_index("core") == 0
    pieces = jnp.stack([jnp.where(is_first, conv_sum, other), jnp.where(is_first, other, conv_sum)])
    pieces = pieces[:, : slabs * 12].reshape(2, tap_count, lanes, 12, 128)
    grad_conv = pieces.transpose(1, 0, 3, 2, 4).reshape(tap_count, 24, inner)
    head_weight = shape((channels, heads), BF16)
    grad_donor, grad_accept, grad_point, grad_gain, loss = call(
        finish_kernel,
        [head_weight, head_weight, shape((inner, channels), BF16), shape((1, channels), F32), shape((1, 128), F32)],
        [SM] + [VM] * 7,
        20,
        1_000_000_000,
        [
            pltpu.VMEM((4, head_rows, 128), BF16),
            pltpu.VMEM((inner, heads), BF16),
            pltpu.VMEM((inner, heads), BF16),
        ],
    )(place, head_sum, behind, ahead, low, high, donor_weight, acceptor_weight)
    return grad_conv, grad_point[None], grad_donor[None], grad_accept[None], grad_gain, loss[0, :1]


def channel_order():
    core, y, zq, zb, k = np.meshgrid(*[np.arange(n) for n in (2, 4, 4, 2, 12)], indexing="ij")
    channel = (24 * (8 * y + 4 * zb + zq) + 12 * core + k).reshape(-1)
    return np.eye(channel.size, dtype=np.float32)[channel]


def zb_halves():
    pick = np.zeros((224, 224), np.float32)
    for zb in range(2):
        for slab in range(9):
            for k in range(12):
                pick[112 * zb + 12 * slab + k, 24 * slab + 12 * zb + k] = 1.0
    return pick


def solution(mesh):
    fine = Mesh(mesh.devices.reshape(4, 2, 4, 2, 4, 2), SEQ + BATCH)
    placed = jax.shard_map(
        on_device,
        mesh=fine,
        in_specs=(
            P(BATCH, SEQ, None),
            P(),
            P(),
            P(),
            P(),
            P(),
            P(BATCH, SEQ, None),
            P(BATCH, SEQ),
            P(),
            P(),
            P(),
        ),
        out_specs=(
            P(None, SEQ, None),
            P(BATCH, None, None),
            P(BATCH, None, None),
            P(BATCH, None, None),
            P(BATCH, None),
            P(BATCH),
        ),
        check_vma=False,
    )

    def run(*arrays):
        order = jnp.asarray(channel_order(), BF16)
        eye = jnp.eye(order.shape[0], dtype=BF16)
        return placed(*arrays, order, eye, jnp.asarray(zb_halves(), BF16))

    return run
```

```python
import jax
import jax.numpy as jnp
import numpy as np
from jax import lax
from jax.experimental import pallas as pl
from jax.experimental.pallas import tpu as pltpu
from jax.sharding import Mesh
from jax.sharding import PartitionSpec as P

STEP = 128
PANEL = 128
SPAN = 4
SLOTS = 16
EPSILON = 1e-06
LOSS_WEIGHT = 1.0 / 128.0
SEQ = ("y", "zb", "zq")
BATCH = ("zhi", "x", "core")
F32 = jnp.float32
BF16 = jnp.bfloat16
ROOT = 0.7978845608028654
CUBIC = 0.044715
PIECE = 96
CHUNK_ROWS = 288
EXTRA_ROWS = 16


def dot(a, b):
    return lax.dot_general(a, b, (((1,), (0,)), ((), ())), preferred_element_type=F32)


def dot_t(a, b):
    return lax.dot_general(a, b, (((1,), (1,)), ((), ())), preferred_element_type=F32)


def gelu(v):
    return 0.5 * v * (1.0 + jnp.tanh(ROOT * (v + CUBIC * (v * v * v))))


def gelu_both(v):
    square = v * v
    t = jnp.tanh(ROOT * (v + CUBIC * (square * v)))
    half = 0.5 * (1.0 + t)
    return v * half, half + 0.5 * v * (1.0 - t * t) * (ROOT * (1.0 + 3.0 * CUBIC * square))


def rms(v):
    return lax.rsqrt(jnp.mean(v * v, axis=-1, keepdims=True) + EPSILON)


def call(kernel, outs, specs, megabytes, flops, scratch=()):
    return pl.pallas_call(
        kernel,
        out_shape=outs,
        in_specs=specs,
        out_specs=[VM] * len(outs),
        scratch_shapes=list(scratch),
        compiler_params=pltpu.CompilerParams(vmem_limit_bytes=megabytes * 1024 * 1024),
        cost_estimate=pl.CostEstimate(flops=flops, bytes_accessed=1_000_000, transcendentals=0),
    )


VM = pl.BlockSpec(memory_space=pltpu.VMEM)
SM = pl.BlockSpec(memory_space=pltpu.SMEM)


def own_kernel(tok, gain, hidden, factor):
    @pl.loop(0, tok.shape[0] // STEP)
    def _(i):
        here = pl.ds(pl.multiple_of(i * STEP, STEP), STEP)
        v = tok[here, :].astype(F32)
        unit = v * rms(v)
        value, slope = gelu_both(unit * gain[...])
        hidden[here, :] = value.astype(BF16)
        factor[here, :] = (slope * unit).astype(BF16)


def edge_kernel(edge, gain, hidden):
    v = edge[...].astype(F32)
    hidden[...] = gelu(v * rms(v) * gain[...]).astype(BF16)


def forward_kernel(
    odd, tok, mine, even_edge, odd_hidden, gain, taps, point, donor_w, accept_w, meta,
    hidden, conv_out, act_out, embed_out, even_feat, odd_feat,
):
    rows = tok.shape[0]
    is_odd = odd[0] > 0
    v = even_edge[...].astype(F32)
    even_hidden = gelu(v * rms(v) * gain[...]).astype(BF16)
    hidden[pl.ds(0, STEP), :] = jnp.where(is_odd, even_hidden, odd_hidden[...])
    hidden[pl.ds(STEP + rows, STEP), :] = jnp.where(is_odd, odd_hidden[...], even_hidden)
    hidden[pl.ds(STEP, rows), :] = mine[...]

    conv = dot(hidden[:rows, :], taps[0])
    for tap in range(1, taps.shape[0]):
        conv = conv + dot(hidden[tap * STEP : tap * STEP + rows, :], taps[tap])
    conv_out[...] = conv
    act = gelu(conv).astype(BF16)
    act_out[...] = act
    embed = (tok[...].astype(F32) + dot(act, point[...])).astype(BF16)
    embed_out[...] = embed
    donor = dot(embed, donor_w[...]).astype(BF16)
    accept = dot(embed, accept_w[...]).astype(BF16)
    even_feat[:rows, :] = jnp.where(is_odd, donor, accept)
    odd_feat[:rows, :] = jnp.where(is_odd, accept, donor)
    even_feat[pl.ds(rows, SLOTS), :] = meta[...]
    odd_feat[pl.ds(rows, SLOTS), :] = meta[...]


def side_kernel(
    odd, even_edge, odd_edge, gain, hidden, conv, act, embed, order, eye,
    factor, slope, hidden_t, act_t, embed_t,
):
    is_odd = odd[0] > 0
    low = jnp.where(is_odd, even_edge[...], odd_edge[...])
    high = jnp.where(is_odd, odd_edge[...], even_edge[...])
    for edge, at in ((low, 0), (high, STEP)):
        v = edge.astype(F32)
        unit = v * rms(v)
        factor[pl.ds(at, STEP), :] = (gelu_both(unit * gain[...])[1] * unit).astype(BF16)

    @pl.loop(0, conv.shape[0] // STEP)
    def _(i):
        here = pl.ds(pl.multiple_of(i * STEP, STEP), STEP)
        slope[here, :] = gelu_both(conv[here, :])[1]

    hidden_t[...] = dot_t(order[...], hidden[...]).astype(BF16)
    embed_t[...] = dot_t(eye[...], embed[...]).astype(BF16)
    inner = act.shape[1]
    act_t[...] = dot_t(eye[:inner, :inner], act[...]).astype(BF16)


def copy_kernel(source, target):
    target[...] = source[...]


def pair_kernel(distance, *refs):
    if distance == 0:
        odd, own, even0, odd0, d_donor, d_accept, loss = refs
        d_donor[...] = jnp.zeros_like(d_donor)
        d_accept[...] = jnp.zeros_like(d_accept)
        loss[...] = jnp.zeros_like(loss)
    else:
        odd, own, far, even0, odd0, even1, odd1, dd_in, da_in, loss_in, d_donor, d_accept, loss = refs
        d_donor[...] = dd_in[...]
        d_accept[...] = da_in[...]
        loss[...] = loss_in[...]
    is_odd = odd[0] > 0
    scale = even0.shape[1] ** (-0.5)
    per_device = d_donor.shape[0] // PANEL
    row = lax.broadcasted_iota(jnp.int32, (PANEL, PANEL), 0)
    col = lax.broadcasted_iota(jnp.int32, (PANEL, PANEL), 1)

    def place(block):
        return pl.ds(pl.multiple_of(block * PANEL, PANEL), PANEL)

    def own_donor(block):
        return jnp.where(is_odd, odd0[place(block), :], even0[place(block), :])

    def own_accept(block):
        return jnp.where(is_odd, even0[place(block), :], odd0[place(block), :])

    if distance == 0:
        far_accept, far_donor = own_accept, None
    else:

        def far_accept(block):
            return jnp.where(is_odd, odd1[place(block), :], even1[place(block), :])

        def far_donor(block):
            return jnp.where(is_odd, even1[place(block), :], odd1[place(block), :])

    def visit(meta, j, donors, acceptors, is_owner):
        accept_block = meta[j, 2] - distance * per_device
        here = (meta[j, 4] > 0) & (accept_block >= 0) & (accept_block < per_device)

        @pl.when(here)
        def _():
            donor_block = meta[j, 0]
            dpan = donors(donor_block)
            apan = acceptors(accept_block)
            scores = dot_t(dpan, apan) * scale
            target = ((row == meta[j, 1]) & (col == meta[j, 3])).astype(F32)
            small = jnp.exp(-jnp.abs(scores))
            inverse = 1.0 / (1.0 + small)
            sigmoid = jnp.where(scores >= 0, inverse, small * inverse)
            dscore = ((sigmoid - target) * LOSS_WEIGHT).astype(BF16)
            if is_owner:
                loss[...] += (jnp.maximum(scores, 0.0) + jnp.log1p(small)) - target * scores
                d_donor[place(donor_block), :] += dot(dscore, apan) * scale
            if distance == 0 or not is_owner:
                d_accept[place(accept_block), :] += scale * lax.dot_general(
                    dscore, dpan, (((0,), (0,)), ((), ())), preferred_element_type=F32
                )

    @pl.loop(0, SLOTS)
    def _(j):
        visit(own, j, own_donor, far_accept, True)
        if distance > 0:
            visit(far, j, far_donor, own_accept, False)


def relative(target, y, first):
    code = (target ^ (target >> 1)) ^ (y ^ (y >> 1))
    low, high = code & 1, code >> 1
    return low * 2 + high if first == 0 else high * 2 + low


def tap_grad_kernel(
    place, d_donor, d_accept, point, donor_w, accept_w, slope, hidden_t,
    keep, send, d_conv, d_feat,
):
    rows, heads = d_donor.shape
    channels = hidden_t.shape[0]

    dd = d_donor[...].astype(BF16)
    da = d_accept[...].astype(BF16)
    d_feat[:, :heads] = dd
    d_feat[:, heads:] = da
    d_embed = (dot_t(dd, donor_w[...]) + dot_t(da, accept_w[...])).astype(BF16)
    d_conv[...] = (dot_t(d_embed, point[...]) * slope[...]).astype(BF16)

    lanes = d_conv.shape[1] // 128
    half_rows = channels // 2
    slab = [relative(target, place[1], 1) for target in range(4)]
    for tap in range(3):
        for half in range(2):
            part = dot(
                hidden_t[half * half_rows : (half + 1) * half_rows, tap * STEP : tap * STEP + rows],
                d_conv[...],
            ).astype(BF16)

            def store(into, part=part, tap=tap):
                for k in range(4):
                    for lane in range(lanes):
                        into[slab[k], tap * lanes + lane] = part[
                            k * PIECE : (k + 1) * PIECE, lane * 128 : (lane + 1) * 128
                        ]

            pl.when(place[0] == half)(lambda: store(keep))
            pl.when(place[0] != half)(lambda: store(send))


def head_grad_kernel(
    place, d_conv, d_feat, loss, taps, factor, edge_factor, act_t, embed_t, head_sum,
):
    rows = d_conv.shape[0]
    channels = embed_t.shape[0]
    inner = act_t.shape[0]
    slab = [relative(target, place[1], 0) for target in range(4)]

    def put(part, base, group_rows, first):
        for lane in range(4):
            for k in range(part.shape[0] // PIECE):
                piece = first + lane * (group_rows // PIECE) + k + base
                chunk, third = piece // 3, piece % 3
                head_sum[slab[chunk // 4], chunk % 4, third * PIECE : (third + 1) * PIECE, :] = part[
                    k * PIECE : (k + 1) * PIECE, lane * 128 : (lane + 1) * 128
                ]

    for i in range(2):
        part = dot(embed_t[i * 4 * PIECE : (i + 1) * 4 * PIECE, :], d_feat[...]).astype(BF16)
        put(part, 4 * i, channels, 0)
    put(dot(act_t[...], d_feat[...]).astype(BF16), 0, inner, 4 * channels // PIECE)

    total = jnp.zeros((8, channels), F32)
    edge = edge_factor.shape[0] // 2
    for tap in range(taps.shape[0]):
        product = dot_t(d_conv[...], taps[tap])
        if tap == 0:
            weights = jnp.concatenate([edge_factor[:edge, :], factor[: rows - edge, :]], axis=0)
        elif tap == 1:
            weights = factor[...]
        else:
            weights = jnp.concatenate([factor[edge:, :], edge_factor[edge:, :]], axis=0)
        product = product * weights.astype(F32)
        total = total + jnp.sum(product.reshape(rows // 8, 8, channels), axis=0)
    gain = jnp.sum(total, axis=0, keepdims=True)
    loss_row = jnp.sum(loss[...], axis=0, keepdims=True) * LOSS_WEIGHT
    loss_all = jnp.broadcast_to(jnp.sum(loss_row, axis=1, keepdims=True), (1, 128))
    at_row = lax.broadcasted_iota(jnp.int32, (EXTRA_ROWS, 128), 0)
    for chunk in range(16):
        if chunk < channels // 128:
            value = gain[:, chunk * 128 : (chunk + 1) * 128]
        elif chunk == channels // 128:
            value = loss_all
        else:
            value = jnp.zeros((1, 128), F32)
        coarse = value.astype(BF16).astype(F32)
        block = jnp.where(at_row == 0, coarse, 0.0) + jnp.where(at_row == 8, value - coarse, 0.0)
        head_sum[slab[chunk // 4], chunk % 4, CHUNK_ROWS:, :] = block.astype(BF16)


def split_rows(total):
    value = total[CHUNK_ROWS : CHUNK_ROWS + 8] + total[CHUNK_ROWS + 8 : CHUNK_ROWS + 16]
    coarse = value.astype(BF16).astype(F32)
    return jnp.concatenate([total[:CHUNK_ROWS], coarse, value - coarse], axis=0).astype(BF16)


def core_sum_kernel(taps, received, kept, send):
    for k in range(2):
        for slab in range(taps.shape[1]):
            kept[k, slab] = taps[k, slab].astype(F32) + received[k, slab].astype(F32)
            send[k, slab] = (
                taps[k + 2, slab].astype(F32) + received[k + 2, slab].astype(F32)
            ).astype(BF16)


def head_sum_kernel(head, received, kept, send):
    for zq in range(4):
        kept[zq] = head[0, zq].astype(F32) + received[0, zq].astype(F32)
        send[zq] = split_rows(head[1, zq].astype(F32) + received[1, zq].astype(F32))


def tap_sum_kernel(before, received, kept, send):
    for slab in range(before.shape[1]):
        kept[slab] = before[0, slab] + received[0, slab].astype(F32)
        send[slab] = (before[1, slab] + received[1, slab].astype(F32)).astype(BF16)


def join_kernel(head, head_in, taps, taps_in, both):
    chunk_rows = head.shape[1]
    for zq in range(4):
        both[zq, :chunk_rows, :] = split_rows(head[zq] + head_in[zq].astype(F32))
        here = slice(zq * 24, (zq + 1) * 24)
        parts = [taps[k, here] + taps_in[k, here].astype(F32) for k in range(taps.shape[0])]
        parts.append(jnp.zeros((8, 128), F32))
        both[zq, chunk_rows:, :] = jnp.concatenate(parts, axis=0).astype(BF16)


def line_sum_kernel(place, parts, pick, send, mine):
    total = parts[0].astype(F32)
    for zq in range(1, 4):
        total = total + parts[zq].astype(F32)
    chunk_rows = CHUNK_ROWS + EXTRA_ROWS
    send[:chunk_rows, :] = split_rows(total[:chunk_rows])
    taps = total[chunk_rows:].astype(BF16)
    half = mine.shape[0]
    zb = place[2]

    def picked(which):
        return dot(pick[pl.ds(pl.multiple_of(which * half, half), half), :], taps).astype(BF16)

    send[chunk_rows:, :] = picked(1 - zb)
    mine[...] = picked(zb)


def far_sum_kernel(sent, received, mine, one, two, head, taps):
    chunk_rows = head.shape[1]
    total = split_rows(sent[:chunk_rows, :].astype(F32) + received[:chunk_rows, :].astype(F32))
    for zq in range(head.shape[0]):
        head[zq] = total
    near = mine[...].astype(F32) + received[chunk_rows:, :].astype(F32)
    taps[...] = (near + (one[...].astype(F32) + two[...].astype(F32))).astype(BF16)


def line_total_kernel(own, one, two, three, total):
    even = own[...].astype(F32) + two[...].astype(F32)
    total[...] = even + (one[...].astype(F32) + three[...].astype(F32))


def finish_kernel(
    place, own, behind, ahead, low, high, donor_w, accept_w,
    grad_donor, grad_accept, grad_point, gain, loss, held, act_donor, act_accept,
):
    count = held.shape[0]
    for step, part in ((0, own), (3, behind), (1, ahead)):
        held[lax.rem(place[1] + step, count)] = part[...]
    opposite = lax.rem(place[1] + 2, count)
    middle = low.shape[0]
    held[opposite, :middle, :] = low[...]
    held[opposite, middle:, :] = high[...]
    channels = grad_donor.shape[0]
    inner = act_donor.shape[0]
    chunk_rows = CHUNK_ROWS + EXTRA_ROWS
    piece = 0
    for into in (grad_donor, grad_accept, act_donor, act_accept):
        for lane in range(2):
            for k in range(into.shape[0] // PIECE):
                chunk, third = piece // 3, piece % 3
                at = (chunk % 4) * chunk_rows + third * PIECE
                into[k * PIECE : (k + 1) * PIECE, lane * 128 : (lane + 1) * 128] = held[
                    chunk // 4, at : at + PIECE, :
                ]
                piece += 1

    grad_point[...] = (
        dot_t(act_donor[...], donor_w[...]) + dot_t(act_accept[...], accept_w[...])
    ).astype(BF16)

    for chunk in range(channels // 128 + 1):
        at = (chunk % 4) * chunk_rows + CHUNK_ROWS
        block = held[chunk // 4, at : at + EXTRA_ROWS, :].astype(F32)
        value = block[0:1, :] + block[8:9, :]
        if chunk < channels // 128:
            gain[:, chunk * 128 : (chunk + 1) * 128] = value
        else:
            loss[...] = value


def swapped(block, first, between_lines=True):
    count = lax.axis_size(SEQ)
    pairs = [(i, i + 1) for i in range(first, count - 1, 2) if between_lines or i % 8 < 7]
    return lax.ppermute(block, SEQ, pairs + [(j, i) for i, j in pairs])


def swap_parts(parts, axis):
    return lax.all_to_all(parts, axis, 0, 0, tiled=True)


def on_device(
    activations, norm_gain, dilated_tap_weight, point_weight, donor_weight, acceptor_weight,
    pair_sites, pair_count, order, eye, pick,
):
    tokens = activations[0]
    rows, channels = tokens.shape
    tap_count, _, inner = dilated_tap_weight.shape
    heads = donor_weight.shape[1]
    blocks = rows // PANEL
    shape = jax.ShapeDtypeStruct
    here = lax.axis_index(SEQ)
    line = lax.axis_index(("zb", "zq"))
    is_odd = (lax.axis_index("zq") & 1) > 0
    odd = is_odd.astype(jnp.int32)[None]
    start, end = tokens[:STEP], tokens[rows - STEP :]
    even_edge = swapped(jnp.where(is_odd, start, end), 0)
    odd_edge = swapped(jnp.where(is_odd, end, start), 1)
    gain = norm_gain[None]
    sites = pair_sites[0]
    first = here * blocks
    live = (jnp.arange(SLOTS, dtype=jnp.int32) < pair_count[0, 0]).astype(jnp.int32)
    meta = jnp.stack(
        [
            sites[:, 0] // PANEL - first,
            sites[:, 0] % PANEL,
            sites[:, 1] // PANEL - first,
            sites[:, 1] % PANEL,
            live,
        ]
        + [jnp.zeros_like(live)] * 3,
        axis=1,
    )
    meta_rows = jnp.pad(meta.astype(BF16), ((0, 0), (0, heads - meta.shape[1])))

    mine, factor = call(
        own_kernel, [shape((rows, channels), BF16)] * 2, [VM] * 2, 12, 2_000_000_000
    )(tokens, gain)
    (odd_hidden,) = call(edge_kernel, [shape((STEP, channels), BF16)], [VM] * 2, 8, 2_000_000_000)(odd_edge, gain)
    feat = shape((rows + SLOTS, heads), BF16)
    hidden, conv, act, embed, even_feat, odd_feat = call(
        forward_kernel,
        [
            shape((rows + 2 * STEP, channels), BF16),
            shape((rows, inner), F32),
            shape((rows, inner), BF16),
            shape((rows, channels), BF16),
            feat,
            feat,
        ],
        [SM] + [VM] * 10,
        20,
        4_000_000_000,
    )(
        odd, tokens, mine, even_edge, odd_hidden, gain, dilated_tap_weight, point_weight,
        donor_weight, acceptor_weight, meta_rows,
    )

    acc_shapes = [shape((rows, heads), F32), shape((rows, heads), F32), shape((PANEL, PANEL), F32)]
    acc = call(
        lambda *refs: pair_kernel(0, *refs), acc_shapes, [SM] * 2 + [VM] * 2, 12, 2_000_000_000
    )(1 - odd, meta, even_feat, odd_feat)
    edge_factor, slope, hidden_t, act_t, embed_t = call(
        side_kernel,
        [
            shape((2 * STEP, channels), BF16),
            shape((rows, inner), F32),
            shape((channels, rows + 2 * STEP), BF16),
            shape((inner, rows), BF16),
            shape((channels, rows), BF16),
        ],
        [SM] + [VM] * 9,
        20,
        6_000_000_000,
    )(odd, even_edge, odd_edge, gain, hidden, conv, act, embed, order, eye)
    count = lax.axis_size(SEQ)
    starts = range(0, count, 8)
    wide_pairs = [(i + k, i - 4 + k) for i in starts if i > 0 for k in (2, 3)]
    wide_pairs += [(i + k, i + 4 + k) for i in starts if i + 8 < count for k in (4, 5)]
    relay_pairs = [(i + 6, i + 7) for i in starts] + [(i + 1, i) for i in starts]
    wide_feat = jnp.where((line == 2) | (line == 5), even_feat, odd_feat)
    wide = lax.ppermute(wide_feat, SEQ, wide_pairs)
    at_end = (line == 0) | (line == 7)
    near_end = (line == 1) | (line == 6)
    short_far, long_far = odd_feat, even_feat
    for distance in range(1, SPAN + 1):
        if distance == 1:
            short_far, long_far = swapped(odd_feat, 0), swapped(even_feat, 1)
            (short_far,) = call(copy_kernel, [feat], [VM], 4, 1000000)(short_far)
        else:
            short_far, long_far = swapped(long_far, 0), swapped(short_far, 1, distance <= 2)
        short_use, long_use = short_far, long_far
        if distance == 2:
            ready, _ = lax.optimization_barrier((wide, long_far))
            relay = lax.ppermute(ready, SEQ, relay_pairs)
        if distance == 3:
            long_use = jnp.where(at_end, relay, long_far)
        if distance == 4:
            short_use = jnp.where(near_end, wide, short_far)
            long_use = jnp.where(at_end, wide, long_far)
        far_meta = jnp.where(is_odd, short_use[rows:, :8], long_use[rows:, :8]).astype(jnp.int32)
        acc = call(
            lambda *refs, distance=distance: pair_kernel(distance, *refs),
            acc_shapes,
            [SM] * 3 + [VM] * 7,
            12,
            2_500_000_000,
        )(1 - odd, meta, far_meta, even_feat, odd_feat, long_use, short_use, *acc)

    chunk = CHUNK_ROWS + EXTRA_ROWS
    lanes = inner // 128
    slabs = tap_count * lanes
    y = lax.axis_index("y")
    place = jnp.stack([lax.axis_index("core"), y, lax.axis_index("zb")]).astype(jnp.int32)
    half = shape((4, slabs, PIECE, 128), BF16)
    keep, send, d_conv, d_feat = call(
        tap_grad_kernel,
        [half, half, shape((rows, inner), BF16), shape((rows, 2 * heads), BF16)],
        [SM] + [VM] * 7,
        24,
        4_000_000_000,
    )(place, acc[0], acc[1], point_weight, donor_weight, acceptor_weight, slope, hidden_t)
    received = lax.ppermute(send, "core", [(0, 1), (1, 0)])
    (head_sum,) = call(
        head_grad_kernel, [shape((4, 4, chunk, 128), BF16)], [SM] + [VM] * 8, 20, 4_000_000_000
    )(place, d_conv, d_feat, acc[2], dilated_tap_weight, factor, edge_factor, act_t, embed_t)

    first_pairs = [(0, 1), (1, 0), (2, 3), (3, 2)]
    second_pairs = [(1, 2), (2, 1), (3, 0), (0, 3)]
    quick = 1_000_000
    conv_kept, conv_send = call(
        core_sum_kernel, [shape((2, slabs, PIECE, 128), F32), shape((2, slabs, PIECE, 128), BF16)],
        [VM] * 2, 12, quick,
    )(keep, received)
    other = lax.ppermute(head_sum[2:], "y", first_pairs)
    heads_kept, heads_send = call(
        head_sum_kernel, [shape((4, chunk, 128), F32), shape((4, chunk, 128), BF16)], [VM] * 2, 12, quick
    )(head_sum, other)
    other = lax.ppermute(conv_send, "y", second_pairs)
    conv_kept, conv_send = call(
        tap_sum_kernel, [shape((slabs, PIECE, 128), F32), shape((slabs, PIECE, 128), BF16)],
        [VM] * 2, 12, quick,
    )(conv_kept, other)
    heads_in = lax.ppermute(heads_send, "y", second_pairs)
    conv_in = lax.ppermute(conv_send, "y", first_pairs)

    joint = chunk + 224
    (both,) = call(join_kernel, [shape((4, joint, 128), BF16)], [VM] * 4, 12, quick)(
        heads_kept, heads_in, conv_kept, conv_in
    )
    parts = swap_parts(both, "zq")
    sent, mine = call(
        line_sum_kernel, [shape((chunk + 112, 128), BF16), shape((112, 128), BF16)],
        [SM] + [VM] * 2, 8, quick,
    )(place, parts, pick)
    received = lax.ppermute(sent, "zb", [(0, 1), (1, 0)])
    across = lax.ppermute(mine, "zhi", [(0, 1), (1, 0)])
    corner = lax.ppermute(
        sent[chunk:], ("zb", "zhi"), [(0, 3), (3, 0), (1, 2), (2, 1)]
    )
    head_parts, conv_sum = call(
        far_sum_kernel, [shape((4, chunk, 128), BF16), shape((112, 128), BF16)], [VM] * 5, 8, quick
    )(sent, received, mine, across, corner)

    head_rows = 4 * chunk
    head_sum = swap_parts(head_parts, "zq").reshape(head_rows, 128)
    line = [
        lax.ppermute(conv_sum, "x", [(i, (i + step) % 4) for i in range(4)]) for step in (1, 2, 3)
    ]
    (conv_sum,) = call(line_total_kernel, [shape((112, 128), F32)], [VM] * 4, 8, quick)(conv_sum, *line)
    head_sum, conv_sum = lax.optimization_barrier((head_sum, conv_sum))
    other = lax.ppermute(conv_sum, "core", [(0, 1), (1, 0)])
    around = [(i, (i + 1) % 4) for i in range(4)]
    back = [(j, i) for i, j in around]
    behind = lax.ppermute(head_sum, "y", around)
    ahead = lax.ppermute(head_sum, "y", back)
    low = lax.ppermute(behind[: head_rows // 2], "y", around)
    high = lax.ppermute(ahead[head_rows // 2 :], "y", back)
    is_first = lax.axis_index("core") == 0
    pieces = jnp.stack([jnp.where(is_first, conv_sum, other), jnp.where(is_first, other, conv_sum)])
    pieces = pieces[:, : slabs * 12].reshape(2, tap_count, lanes, 12, 128)
    grad_conv = pieces.transpose(1, 0, 3, 2, 4).reshape(tap_count, 24, inner)
    head_weight = shape((channels, heads), BF16)
    grad_donor, grad_accept, grad_point, grad_gain, loss = call(
        finish_kernel,
        [head_weight, head_weight, shape((inner, channels), BF16), shape((1, channels), F32), shape((1, 128), F32)],
        [SM] + [VM] * 7,
        20,
        1_000_000_000,
        [
            pltpu.VMEM((4, head_rows, 128), BF16),
            pltpu.VMEM((inner, heads), BF16),
            pltpu.VMEM((inner, heads), BF16),
        ],
    )(place, head_sum, behind, ahead, low, high, donor_weight, acceptor_weight)
    return grad_conv, grad_point[None], grad_donor[None], grad_accept[None], grad_gain, loss[0, :1]


def channel_order():
    core, y, zq, zb, k = np.meshgrid(*[np.arange(n) for n in (2, 4, 4, 2, 12)], indexing="ij")
    channel = (24 * (8 * y + 4 * zb + zq) + 12 * core + k).reshape(-1)
    return np.eye(channel.size, dtype=np.float32)[channel]


def zb_halves():
    pick = np.zeros((224, 224), np.float32)
    for zb in range(2):
        for slab in range(9):
            for k in range(12):
                pick[112 * zb + 12 * slab + k, 24 * slab + 12 * zb + k] = 1.0
    return pick


def solution(mesh):
    fine = Mesh(mesh.devices.reshape(4, 2, 4, 2, 4, 2), SEQ + BATCH)
    placed = jax.shard_map(
        on_device,
        mesh=fine,
        in_specs=(
            P(BATCH, SEQ, None),
            P(),
            P(),
            P(),
            P(),
            P(),
            P(BATCH, SEQ, None),
            P(BATCH, SEQ),
            P(),
            P(),
            P(),
        ),
        out_specs=(
            P(None, SEQ, None),
            P(BATCH, None, None),
            P(BATCH, None, None),
            P(BATCH, None, None),
            P(BATCH, None),
            P(BATCH),
        ),
        check_vma=False,
    )

    def run(*arrays):
        order = jnp.asarray(channel_order(), BF16)
        eye = jnp.eye(order.shape[0], dtype=BF16)
        return placed(*arrays, order, eye, jnp.asarray(zb_halves(), BF16))

    return run
```

```python
import jax
import jax.numpy as jnp
import numpy as np
from jax import lax
from jax.experimental import pallas as pl
from jax.experimental.pallas import tpu as pltpu
from jax.sharding import Mesh
from jax.sharding import PartitionSpec as P

STEP = 128
PANEL = 128
SPAN = 4
SLOTS = 16
EPSILON = 1e-06
LOSS_WEIGHT = 1.0 / 128.0
SEQ = ("y", "zb", "zq")
BATCH = ("zhi", "x", "core")
F32 = jnp.float32
BF16 = jnp.bfloat16
ROOT = 0.7978845608028654
CUBIC = 0.044715
PIECE = 96
CHUNK_ROWS = 288
EXTRA_ROWS = 16


def dot(a, b):
    return lax.dot_general(a, b, (((1,), (0,)), ((), ())), preferred_element_type=F32)


def dot_t(a, b):
    return lax.dot_general(a, b, (((1,), (1,)), ((), ())), preferred_element_type=F32)


def gelu(v):
    return 0.5 * v * (1.0 + jnp.tanh(ROOT * (v + CUBIC * (v * v * v))))


def gelu_both(v):
    square = v * v
    t = jnp.tanh(ROOT * (v + CUBIC * (square * v)))
    half = 0.5 * (1.0 + t)
    return v * half, half + 0.5 * v * (1.0 - t * t) * (ROOT * (1.0 + 3.0 * CUBIC * square))


def rms(v):
    return lax.rsqrt(jnp.mean(v * v, axis=-1, keepdims=True) + EPSILON)


def call(kernel, outs, specs, megabytes, flops, scratch=()):
    return pl.pallas_call(
        kernel,
        out_shape=outs,
        in_specs=specs,
        out_specs=[VM] * len(outs),
        scratch_shapes=list(scratch),
        compiler_params=pltpu.CompilerParams(vmem_limit_bytes=megabytes * 1024 * 1024),
        cost_estimate=pl.CostEstimate(flops=flops, bytes_accessed=1_000_000, transcendentals=0),
    )


VM = pl.BlockSpec(memory_space=pltpu.VMEM)
SM = pl.BlockSpec(memory_space=pltpu.SMEM)


def own_kernel(tok, gain, hidden, factor):
    @pl.loop(0, tok.shape[0] // STEP)
    def _(i):
        here = pl.ds(pl.multiple_of(i * STEP, STEP), STEP)
        v = tok[here, :].astype(F32)
        unit = v * rms(v)
        value, slope = gelu_both(unit * gain[...])
        hidden[here, :] = value.astype(BF16)
        factor[here, :] = (slope * unit).astype(BF16)


def edge_kernel(edge, gain, hidden):
    v = edge[...].astype(F32)
    hidden[...] = gelu(v * rms(v) * gain[...]).astype(BF16)


def forward_kernel(
    odd, tok, mine, even_edge, odd_hidden, gain, taps, point, donor_w, accept_w, meta,
    hidden, conv_out, act_out, embed_out, even_feat, odd_feat,
):
    rows = tok.shape[0]
    is_odd = odd[0] > 0
    v = even_edge[...].astype(F32)
    even_hidden = gelu(v * rms(v) * gain[...]).astype(BF16)
    hidden[pl.ds(0, STEP), :] = jnp.where(is_odd, even_hidden, odd_hidden[...])
    hidden[pl.ds(STEP + rows, STEP), :] = jnp.where(is_odd, odd_hidden[...], even_hidden)
    hidden[pl.ds(STEP, rows), :] = mine[...]

    conv = dot(hidden[:rows, :], taps[0])
    for tap in range(1, taps.shape[0]):
        conv = conv + dot(hidden[tap * STEP : tap * STEP + rows, :], taps[tap])
    conv_out[...] = conv
    act = gelu(conv).astype(BF16)
    act_out[...] = act
    embed = (tok[...].astype(F32) + dot(act, point[...])).astype(BF16)
    embed_out[...] = embed
    donor = dot(embed, donor_w[...]).astype(BF16)
    accept = dot(embed, accept_w[...]).astype(BF16)
    even_feat[:rows, :] = jnp.where(is_odd, donor, accept)
    odd_feat[:rows, :] = jnp.where(is_odd, accept, donor)
    even_feat[pl.ds(rows, SLOTS), :] = meta[...]
    odd_feat[pl.ds(rows, SLOTS), :] = meta[...]


def side_kernel(
    odd, even_edge, odd_edge, gain, hidden, conv, act, embed, order, eye,
    factor, slope, hidden_t, act_t, embed_t,
):
    is_odd = odd[0] > 0
    low = jnp.where(is_odd, even_edge[...], odd_edge[...])
    high = jnp.where(is_odd, odd_edge[...], even_edge[...])
    for edge, at in ((low, 0), (high, STEP)):
        v = edge.astype(F32)
        unit = v * rms(v)
        factor[pl.ds(at, STEP), :] = (gelu_both(unit * gain[...])[1] * unit).astype(BF16)

    @pl.loop(0, conv.shape[0] // STEP)
    def _(i):
        here = pl.ds(pl.multiple_of(i * STEP, STEP), STEP)
        slope[here, :] = gelu_both(conv[here, :])[1]

    hidden_t[...] = dot_t(order[...], hidden[...]).astype(BF16)
    embed_t[...] = dot_t(eye[...], embed[...]).astype(BF16)
    inner = act.shape[1]
    act_t[...] = dot_t(eye[:inner, :inner], act[...]).astype(BF16)


def copy_kernel(source, target):
    target[...] = source[...]


def pair_kernel(distance, *refs):
    if distance == 0:
        odd, own, even0, odd0, d_donor, d_accept, loss = refs
        d_donor[...] = jnp.zeros_like(d_donor)
        d_accept[...] = jnp.zeros_like(d_accept)
        loss[...] = jnp.zeros_like(loss)
    else:
        odd, own, far, even0, odd0, even1, odd1, dd_in, da_in, loss_in, d_donor, d_accept, loss = refs
        d_donor[...] = dd_in[...]
        d_accept[...] = da_in[...]
        loss[...] = loss_in[...]
    is_odd = odd[0] > 0
    scale = even0.shape[1] ** (-0.5)
    per_device = d_donor.shape[0] // PANEL
    row = lax.broadcasted_iota(jnp.int32, (PANEL, PANEL), 0)
    col = lax.broadcasted_iota(jnp.int32, (PANEL, PANEL), 1)

    def place(block):
        return pl.ds(pl.multiple_of(block * PANEL, PANEL), PANEL)

    def own_donor(block):
        return jnp.where(is_odd, odd0[place(block), :], even0[place(block), :])

    def own_accept(block):
        return jnp.where(is_odd, even0[place(block), :], odd0[place(block), :])

    if distance == 0:
        far_accept, far_donor = own_accept, None
    else:

        def far_accept(block):
            return jnp.where(is_odd, odd1[place(block), :], even1[place(block), :])

        def far_donor(block):
            return jnp.where(is_odd, even1[place(block), :], odd1[place(block), :])

    def visit(meta, j, donors, acceptors, is_owner):
        accept_block = meta[j, 2] - distance * per_device
        here = (meta[j, 4] > 0) & (accept_block >= 0) & (accept_block < per_device)

        @pl.when(here)
        def _():
            donor_block = meta[j, 0]
            dpan = donors(donor_block)
            apan = acceptors(accept_block)
            scores = dot_t(dpan, apan) * scale
            target = ((row == meta[j, 1]) & (col == meta[j, 3])).astype(F32)
            small = jnp.exp(-jnp.abs(scores))
            inverse = 1.0 / (1.0 + small)
            sigmoid = jnp.where(scores >= 0, inverse, small * inverse)
            dscore = ((sigmoid - target) * LOSS_WEIGHT).astype(BF16)
            if is_owner:
                loss[...] += (jnp.maximum(scores, 0.0) + jnp.log1p(small)) - target * scores
                d_donor[place(donor_block), :] += dot(dscore, apan) * scale
            if distance == 0 or not is_owner:
                d_accept[place(accept_block), :] += scale * lax.dot_general(
                    dscore, dpan, (((0,), (0,)), ((), ())), preferred_element_type=F32
                )

    @pl.loop(0, SLOTS)
    def _(j):
        visit(own, j, own_donor, far_accept, True)
        if distance > 0:
            visit(far, j, far_donor, own_accept, False)


def relative(target, y, first):
    code = (target ^ (target >> 1)) ^ (y ^ (y >> 1))
    low, high = code & 1, code >> 1
    return low * 2 + high if first == 0 else high * 2 + low


def tap_grad_kernel(
    place, d_donor, d_accept, point, donor_w, accept_w, slope, hidden_t,
    keep, send, d_conv, d_feat,
):
    rows, heads = d_donor.shape
    channels = hidden_t.shape[0]

    dd = d_donor[...].astype(BF16)
    da = d_accept[...].astype(BF16)
    d_feat[:, :heads] = dd
    d_feat[:, heads:] = da
    d_embed = (dot_t(dd, donor_w[...]) + dot_t(da, accept_w[...])).astype(BF16)
    d_conv[...] = (dot_t(d_embed, point[...]) * slope[...]).astype(BF16)

    lanes = d_conv.shape[1] // 128
    half_rows = channels // 2
    slab = [relative(target, place[1], 1) for target in range(4)]
    for tap in range(3):
        for half in range(2):
            part = dot(
                hidden_t[half * half_rows : (half + 1) * half_rows, tap * STEP : tap * STEP + rows],
                d_conv[...],
            ).astype(BF16)

            def store(into, part=part, tap=tap):
                for k in range(4):
                    for lane in range(lanes):
                        into[slab[k], tap * lanes + lane] = part[
                            k * PIECE : (k + 1) * PIECE, lane * 128 : (lane + 1) * 128
                        ]

            pl.when(place[0] == half)(lambda: store(keep))
            pl.when(place[0] != half)(lambda: store(send))


def head_grad_kernel(
    place, d_conv, d_feat, loss, taps, factor, edge_factor, act_t, embed_t, head_sum,
):
    rows = d_conv.shape[0]
    channels = embed_t.shape[0]
    inner = act_t.shape[0]
    slab = [relative(target, place[1], 0) for target in range(4)]

    def put(part, base, group_rows, first):
        for lane in range(4):
            for k in range(part.shape[0] // PIECE):
                piece = first + lane * (group_rows // PIECE) + k + base
                chunk, third = piece // 3, piece % 3
                head_sum[slab[chunk // 4], chunk % 4, third * PIECE : (third + 1) * PIECE, :] = part[
                    k * PIECE : (k + 1) * PIECE, lane * 128 : (lane + 1) * 128
                ]

    for i in range(2):
        part = dot(embed_t[i * 4 * PIECE : (i + 1) * 4 * PIECE, :], d_feat[...]).astype(BF16)
        put(part, 4 * i, channels, 0)
    put(dot(act_t[...], d_feat[...]).astype(BF16), 0, inner, 4 * channels // PIECE)

    total = jnp.zeros((8, channels), F32)
    edge = edge_factor.shape[0] // 2
    for tap in range(taps.shape[0]):
        product = dot_t(d_conv[...], taps[tap])
        if tap == 0:
            weights = jnp.concatenate([edge_factor[:edge, :], factor[: rows - edge, :]], axis=0)
        elif tap == 1:
            weights = factor[...]
        else:
            weights = jnp.concatenate([factor[edge:, :], edge_factor[edge:, :]], axis=0)
        product = product * weights.astype(F32)
        total = total + jnp.sum(product.reshape(rows // 8, 8, channels), axis=0)
    gain = jnp.sum(total, axis=0, keepdims=True)
    loss_row = jnp.sum(loss[...], axis=0, keepdims=True) * LOSS_WEIGHT
    loss_all = jnp.broadcast_to(jnp.sum(loss_row, axis=1, keepdims=True), (1, 128))
    at_row = lax.broadcasted_iota(jnp.int32, (EXTRA_ROWS, 128), 0)
    for chunk in range(16):
        if chunk < channels // 128:
            value = gain[:, chunk * 128 : (chunk + 1) * 128]
        elif chunk == channels // 128:
            value = loss_all
        else:
            value = jnp.zeros((1, 128), F32)
        coarse = value.astype(BF16).astype(F32)
        block = jnp.where(at_row == 0, coarse, 0.0) + jnp.where(at_row == 8, value - coarse, 0.0)
        head_sum[slab[chunk // 4], chunk % 4, CHUNK_ROWS:, :] = block.astype(BF16)


def split_rows(total):
    value = total[CHUNK_ROWS : CHUNK_ROWS + 8] + total[CHUNK_ROWS + 8 : CHUNK_ROWS + 16]
    coarse = value.astype(BF16).astype(F32)
    return jnp.concatenate([total[:CHUNK_ROWS], coarse, value - coarse], axis=0).astype(BF16)


def core_sum_kernel(taps, received, kept, send):
    for k in range(2):
        for slab in range(taps.shape[1]):
            kept[k, slab] = taps[k, slab].astype(F32) + received[k, slab].astype(F32)
            send[k, slab] = (
                taps[k + 2, slab].astype(F32) + received[k + 2, slab].astype(F32)
            ).astype(BF16)


def head_sum_kernel(head, received, kept, send):
    for zq in range(4):
        kept[zq] = head[0, zq].astype(F32) + received[0, zq].astype(F32)
        send[zq] = split_rows(head[1, zq].astype(F32) + received[1, zq].astype(F32))


def tap_sum_kernel(before, received, kept, send):
    for slab in range(before.shape[1]):
        kept[slab] = before[0, slab] + received[0, slab].astype(F32)
        send[slab] = (before[1, slab] + received[1, slab].astype(F32)).astype(BF16)


def join_kernel(head, head_in, taps, taps_in, both):
    chunk_rows = head.shape[1]
    for zq in range(4):
        both[zq, :chunk_rows, :] = split_rows(head[zq] + head_in[zq].astype(F32))
        here = slice(zq * 24, (zq + 1) * 24)
        parts = [taps[k, here] + taps_in[k, here].astype(F32) for k in range(taps.shape[0])]
        parts.append(jnp.zeros((8, 128), F32))
        both[zq, chunk_rows:, :] = jnp.concatenate(parts, axis=0).astype(BF16)


def line_sum_kernel(place, parts, pick, send, mine):
    total = parts[0].astype(F32)
    for zq in range(1, 4):
        total = total + parts[zq].astype(F32)
    chunk_rows = CHUNK_ROWS + EXTRA_ROWS
    send[:chunk_rows, :] = split_rows(total[:chunk_rows])
    taps = total[chunk_rows:].astype(BF16)
    half = mine.shape[0]
    zb = place[2]

    def picked(which):
        return dot(pick[pl.ds(pl.multiple_of(which * half, half), half), :], taps).astype(BF16)

    send[chunk_rows:, :] = picked(1 - zb)
    mine[...] = picked(zb)


def far_sum_kernel(sent, received, mine, one, two, head, taps):
    chunk_rows = head.shape[1]
    total = split_rows(sent[:chunk_rows, :].astype(F32) + received[:chunk_rows, :].astype(F32))
    for zq in range(head.shape[0]):
        head[zq] = total
    near = mine[...].astype(F32) + received[chunk_rows:, :].astype(F32)
    taps[...] = (near + (one[...].astype(F32) + two[...].astype(F32))).astype(BF16)


def line_total_kernel(own, one, two, three, total):
    even = own[...].astype(F32) + two[...].astype(F32)
    total[...] = even + (one[...].astype(F32) + three[...].astype(F32))


def finish_kernel(
    place, own, behind, ahead, low, high, donor_w, accept_w,
    grad_donor, grad_accept, grad_point, gain, loss, held, act_donor, act_accept,
):
    count = held.shape[0]
    for step, part in ((0, own), (3, behind), (1, ahead)):
        held[lax.rem(place[1] + step, count)] = part[...]
    opposite = lax.rem(place[1] + 2, count)
    middle = low.shape[0]
    held[opposite, :middle, :] = low[...]
    held[opposite, middle:, :] = high[...]
    channels = grad_donor.shape[0]
    inner = act_donor.shape[0]
    chunk_rows = CHUNK_ROWS + EXTRA_ROWS
    piece = 0
    for into in (grad_donor, grad_accept, act_donor, act_accept):
        for lane in range(2):
            for k in range(into.shape[0] // PIECE):
                chunk, third = piece // 3, piece % 3
                at = (chunk % 4) * chunk_rows + third * PIECE
                into[k * PIECE : (k + 1) * PIECE, lane * 128 : (lane + 1) * 128] = held[
                    chunk // 4, at : at + PIECE, :
                ]
                piece += 1

    grad_point[...] = (
        dot_t(act_donor[...], donor_w[...]) + dot_t(act_accept[...], accept_w[...])
    ).astype(BF16)

    for chunk in range(channels // 128 + 1):
        at = (chunk % 4) * chunk_rows + CHUNK_ROWS
        block = held[chunk // 4, at : at + EXTRA_ROWS, :].astype(F32)
        value = block[0:1, :] + block[8:9, :]
        if chunk < channels // 128:
            gain[:, chunk * 128 : (chunk + 1) * 128] = value
        else:
            loss[...] = value


def swapped(block, first, between_lines=True):
    count = lax.axis_size(SEQ)
    pairs = [(i, i + 1) for i in range(first, count - 1, 2) if between_lines or i % 8 < 7]
    return lax.ppermute(block, SEQ, pairs + [(j, i) for i, j in pairs])


def swap_parts(parts, axis):
    return lax.all_to_all(parts, axis, 0, 0, tiled=True)


def on_device(
    activations, norm_gain, dilated_tap_weight, point_weight, donor_weight, acceptor_weight,
    pair_sites, pair_count, order, eye, pick,
):
    tokens = activations[0]
    rows, channels = tokens.shape
    tap_count, _, inner = dilated_tap_weight.shape
    heads = donor_weight.shape[1]
    blocks = rows // PANEL
    shape = jax.ShapeDtypeStruct
    here = lax.axis_index(SEQ)
    line = lax.axis_index(("zb", "zq"))
    is_odd = (lax.axis_index("zq") & 1) > 0
    odd = is_odd.astype(jnp.int32)[None]
    start, end = tokens[:STEP], tokens[rows - STEP :]
    even_edge = swapped(jnp.where(is_odd, start, end), 0)
    odd_edge = swapped(jnp.where(is_odd, end, start), 1)
    gain = norm_gain[None]
    sites = pair_sites[0]
    first = here * blocks
    live = (jnp.arange(SLOTS, dtype=jnp.int32) < pair_count[0, 0]).astype(jnp.int32)
    meta = jnp.stack(
        [
            sites[:, 0] // PANEL - first,
            sites[:, 0] % PANEL,
            sites[:, 1] // PANEL - first,
            sites[:, 1] % PANEL,
            live,
        ]
        + [jnp.zeros_like(live)] * 3,
        axis=1,
    )
    meta_rows = jnp.pad(meta.astype(BF16), ((0, 0), (0, heads - meta.shape[1])))

    mine, factor = call(
        own_kernel, [shape((rows, channels), BF16)] * 2, [VM] * 2, 12, 2_000_000_000
    )(tokens, gain)
    (odd_hidden,) = call(edge_kernel, [shape((STEP, channels), BF16)], [VM] * 2, 8, 2_000_000_000)(odd_edge, gain)
    feat = shape((rows + SLOTS, heads), BF16)
    hidden, conv, act, embed, even_feat, odd_feat = call(
        forward_kernel,
        [
            shape((rows + 2 * STEP, channels), BF16),
            shape((rows, inner), F32),
            shape((rows, inner), BF16),
            shape((rows, channels), BF16),
            feat,
            feat,
        ],
        [SM] + [VM] * 10,
        20,
        4_000_000_000,
    )(
        odd, tokens, mine, even_edge, odd_hidden, gain, dilated_tap_weight, point_weight,
        donor_weight, acceptor_weight, meta_rows,
    )

    acc_shapes = [shape((rows, heads), F32), shape((rows, heads), F32), shape((PANEL, PANEL), F32)]
    acc = call(
        lambda *refs: pair_kernel(0, *refs), acc_shapes, [SM] * 2 + [VM] * 2, 12, 2_000_000_000
    )(1 - odd, meta, even_feat, odd_feat)
    edge_factor, slope, hidden_t, act_t, embed_t = call(
        side_kernel,
        [
            shape((2 * STEP, channels), BF16),
            shape((rows, inner), F32),
            shape((channels, rows + 2 * STEP), BF16),
            shape((inner, rows), BF16),
            shape((channels, rows), BF16),
        ],
        [SM] + [VM] * 9,
        20,
        6_000_000_000,
    )(odd, even_edge, odd_edge, gain, hidden, conv, act, embed, order, eye)
    count = lax.axis_size(SEQ)
    starts = range(0, count, 8)
    wide_pairs = [(i + k, i - 4 + k) for i in starts if i > 0 for k in (2, 3)]
    wide_pairs += [(i + k, i + 4 + k) for i in starts if i + 8 < count for k in (4, 5)]
    wider_pairs = [(i + 2, i - 1) for i in starts if i > 0]
    wider_pairs += [(i + 5, i + 8) for i in starts if i + 8 < count]
    wide_feat = jnp.where((line == 2) | (line == 5), even_feat, odd_feat)
    wide = lax.ppermute(wide_feat, SEQ, wide_pairs)
    wider = lax.ppermute(wide_feat, SEQ, wider_pairs)
    at_end = (line == 0) | (line == 7)
    near_end = (line == 1) | (line == 6)
    short_far, long_far = odd_feat, even_feat
    for distance in range(1, SPAN + 1):
        if distance == 1:
            short_far, long_far = swapped(odd_feat, 0), swapped(even_feat, 1)
            (short_far,) = call(copy_kernel, [feat], [VM], 4, 1000000)(short_far)
        else:
            short_far, long_far = swapped(long_far, 0), swapped(short_far, 1, distance <= 2)
        short_use, long_use = short_far, long_far
        if distance == 3:
            long_use = jnp.where(at_end, wider, long_far)
        if distance == 4:
            short_use = jnp.where(near_end, wide, short_far)
            long_use = jnp.where(at_end, wide, long_far)
        far_meta = jnp.where(is_odd, short_use[rows:, :8], long_use[rows:, :8]).astype(jnp.int32)
        acc = call(
            lambda *refs, distance=distance: pair_kernel(distance, *refs),
            acc_shapes,
            [SM] * 3 + [VM] * 7,
            12,
            2_500_000_000,
        )(1 - odd, meta, far_meta, even_feat, odd_feat, long_use, short_use, *acc)

    chunk = CHUNK_ROWS + EXTRA_ROWS
    lanes = inner // 128
    slabs = tap_count * lanes
    y = lax.axis_index("y")
    place = jnp.stack([lax.axis_index("core"), y, lax.axis_index("zb")]).astype(jnp.int32)
    half = shape((4, slabs, PIECE, 128), BF16)
    keep, send, d_conv, d_feat = call(
        tap_grad_kernel,
        [half, half, shape((rows, inner), BF16), shape((rows, 2 * heads), BF16)],
        [SM] + [VM] * 7,
        24,
        4_000_000_000,
    )(place, acc[0], acc[1], point_weight, donor_weight, acceptor_weight, slope, hidden_t)
    received = lax.ppermute(send, "core", [(0, 1), (1, 0)])
    (head_sum,) = call(
        head_grad_kernel, [shape((4, 4, chunk, 128), BF16)], [SM] + [VM] * 8, 20, 4_000_000_000
    )(place, d_conv, d_feat, acc[2], dilated_tap_weight, factor, edge_factor, act_t, embed_t)

    first_pairs = [(0, 1), (1, 0), (2, 3), (3, 2)]
    second_pairs = [(1, 2), (2, 1), (3, 0), (0, 3)]
    quick = 1_000_000
    conv_kept, conv_send = call(
        core_sum_kernel, [shape((2, slabs, PIECE, 128), F32), shape((2, slabs, PIECE, 128), BF16)],
        [VM] * 2, 12, quick,
    )(keep, received)
    other = lax.ppermute(head_sum[2:], "y", first_pairs)
    heads_kept, heads_send = call(
        head_sum_kernel, [shape((4, chunk, 128), F32), shape((4, chunk, 128), BF16)], [VM] * 2, 12, quick
    )(head_sum, other)
    other = lax.ppermute(conv_send, "y", second_pairs)
    conv_kept, conv_send = call(
        tap_sum_kernel, [shape((slabs, PIECE, 128), F32), shape((slabs, PIECE, 128), BF16)],
        [VM] * 2, 12, quick,
    )(conv_kept, other)
    heads_in = lax.ppermute(heads_send, "y", second_pairs)
    conv_in = lax.ppermute(conv_send, "y", first_pairs)

    joint = chunk + 224
    (both,) = call(join_kernel, [shape((4, joint, 128), BF16)], [VM] * 4, 12, quick)(
        heads_kept, heads_in, conv_kept, conv_in
    )
    parts = swap_parts(both, "zq")
    sent, mine = call(
        line_sum_kernel, [shape((chunk + 112, 128), BF16), shape((112, 128), BF16)],
        [SM] + [VM] * 2, 8, quick,
    )(place, parts, pick)
    received = lax.ppermute(sent, "zb", [(0, 1), (1, 0)])
    across = lax.ppermute(mine, "zhi", [(0, 1), (1, 0)])
    corner = lax.ppermute(
        sent[chunk:], ("zb", "zhi"), [(0, 3), (3, 0), (1, 2), (2, 1)]
    )
    head_parts, conv_sum = call(
        far_sum_kernel, [shape((4, chunk, 128), BF16), shape((112, 128), BF16)], [VM] * 5, 8, quick
    )(sent, received, mine, across, corner)

    head_rows = 4 * chunk
    head_sum = swap_parts(head_parts, "zq").reshape(head_rows, 128)
    line = [
        lax.ppermute(conv_sum, "x", [(i, (i + step) % 4) for i in range(4)]) for step in (1, 2, 3)
    ]
    (conv_sum,) = call(line_total_kernel, [shape((112, 128), F32)], [VM] * 4, 8, quick)(conv_sum, *line)
    head_sum, conv_sum = lax.optimization_barrier((head_sum, conv_sum))
    other = lax.ppermute(conv_sum, "core", [(0, 1), (1, 0)])
    around = [(i, (i + 1) % 4) for i in range(4)]
    back = [(j, i) for i, j in around]
    behind = lax.ppermute(head_sum, "y", around)
    ahead = lax.ppermute(head_sum, "y", back)
    low = lax.ppermute(behind[: head_rows // 2], "y", around)
    high = lax.ppermute(ahead[head_rows // 2 :], "y", back)
    is_first = lax.axis_index("core") == 0
    pieces = jnp.stack([jnp.where(is_first, conv_sum, other), jnp.where(is_first, other, conv_sum)])
    pieces = pieces[:, : slabs * 12].reshape(2, tap_count, lanes, 12, 128)
    grad_conv = pieces.transpose(1, 0, 3, 2, 4).reshape(tap_count, 24, inner)
    head_weight = shape((channels, heads), BF16)
    grad_donor, grad_accept, grad_point, grad_gain, loss = call(
        finish_kernel,
        [head_weight, head_weight, shape((inner, channels), BF16), shape((1, channels), F32), shape((1, 128), F32)],
        [SM] + [VM] * 7,
        20,
        1_000_000_000,
        [
            pltpu.VMEM((4, head_rows, 128), BF16),
            pltpu.VMEM((inner, heads), BF16),
            pltpu.VMEM((inner, heads), BF16),
        ],
    )(place, head_sum, behind, ahead, low, high, donor_weight, acceptor_weight)
    return grad_conv, grad_point[None], grad_donor[None], grad_accept[None], grad_gain, loss[0, :1]


def channel_order():
    core, y, zq, zb, k = np.meshgrid(*[np.arange(n) for n in (2, 4, 4, 2, 12)], indexing="ij")
    channel = (24 * (8 * y + 4 * zb + zq) + 12 * core + k).reshape(-1)
    return np.eye(channel.size, dtype=np.float32)[channel]


def zb_halves():
    pick = np.zeros((224, 224), np.float32)
    for zb in range(2):
        for slab in range(9):
            for k in range(12):
                pick[112 * zb + 12 * slab + k, 24 * slab + 12 * zb + k] = 1.0
    return pick


def solution(mesh):
    fine = Mesh(mesh.devices.reshape(4, 2, 4, 2, 4, 2), SEQ + BATCH)
    placed = jax.shard_map(
        on_device,
        mesh=fine,
        in_specs=(
            P(BATCH, SEQ, None),
            P(),
            P(),
            P(),
            P(),
            P(),
            P(BATCH, SEQ, None),
            P(BATCH, SEQ),
            P(),
            P(),
            P(),
        ),
        out_specs=(
            P(None, SEQ, None),
            P(BATCH, None, None),
            P(BATCH, None, None),
            P(BATCH, None, None),
            P(BATCH, None),
            P(BATCH),
        ),
        check_vma=False,
    )

    def run(*arrays):
        order = jnp.asarray(channel_order(), BF16)
        eye = jnp.eye(order.shape[0], dtype=BF16)
        return placed(*arrays, order, eye, jnp.asarray(zb_halves(), BF16))

    return run
```

```python
import jax
import jax.numpy as jnp
import numpy as np
from jax import lax
from jax.experimental import pallas as pl
from jax.experimental.pallas import tpu as pltpu
from jax.sharding import Mesh
from jax.sharding import PartitionSpec as P

STEP = 128
PANEL = 128
SPAN = 4
SLOTS = 16
EPSILON = 1e-06
LOSS_WEIGHT = 1.0 / 128.0
SEQ = ("y", "zb", "zq")
BATCH = ("zhi", "x", "core")
F32 = jnp.float32
BF16 = jnp.bfloat16
ROOT = 0.7978845608028654
CUBIC = 0.044715
PIECE = 96
CHUNK_ROWS = 288
EXTRA_ROWS = 16


def dot(a, b):
    return lax.dot_general(a, b, (((1,), (0,)), ((), ())), preferred_element_type=F32)


def dot_t(a, b):
    return lax.dot_general(a, b, (((1,), (1,)), ((), ())), preferred_element_type=F32)


def gelu(v):
    return 0.5 * v * (1.0 + jnp.tanh(ROOT * (v + CUBIC * (v * v * v))))


def gelu_both(v):
    square = v * v
    t = jnp.tanh(ROOT * (v + CUBIC * (square * v)))
    half = 0.5 * (1.0 + t)
    return v * half, half + 0.5 * v * (1.0 - t * t) * (ROOT * (1.0 + 3.0 * CUBIC * square))


def rms(v):
    return lax.rsqrt(jnp.mean(v * v, axis=-1, keepdims=True) + EPSILON)


def call(kernel, outs, specs, megabytes, flops, scratch=()):
    return pl.pallas_call(
        kernel,
        out_shape=outs,
        in_specs=specs,
        out_specs=[VM] * len(outs),
        scratch_shapes=list(scratch),
        compiler_params=pltpu.CompilerParams(vmem_limit_bytes=megabytes * 1024 * 1024),
        cost_estimate=pl.CostEstimate(flops=flops, bytes_accessed=1_000_000, transcendentals=0),
    )


VM = pl.BlockSpec(memory_space=pltpu.VMEM)
SM = pl.BlockSpec(memory_space=pltpu.SMEM)


def own_kernel(tok, gain, hidden, factor):
    @pl.loop(0, tok.shape[0] // STEP)
    def _(i):
        here = pl.ds(pl.multiple_of(i * STEP, STEP), STEP)
        v = tok[here, :].astype(F32)
        unit = v * rms(v)
        value, slope = gelu_both(unit * gain[...])
        hidden[here, :] = value.astype(BF16)
        factor[here, :] = (slope * unit).astype(BF16)


def edge_kernel(edge, gain, hidden):
    v = edge[...].astype(F32)
    hidden[...] = gelu(v * rms(v) * gain[...]).astype(BF16)


def forward_kernel(
    odd, tok, mine, even_edge, odd_hidden, gain, taps, point, donor_w, accept_w, meta,
    hidden, conv_out, act_out, embed_out, even_feat, odd_feat,
):
    rows = tok.shape[0]
    is_odd = odd[0] > 0
    v = even_edge[...].astype(F32)
    even_hidden = gelu(v * rms(v) * gain[...]).astype(BF16)
    hidden[pl.ds(0, STEP), :] = jnp.where(is_odd, even_hidden, odd_hidden[...])
    hidden[pl.ds(STEP + rows, STEP), :] = jnp.where(is_odd, odd_hidden[...], even_hidden)
    hidden[pl.ds(STEP, rows), :] = mine[...]

    conv = dot(hidden[:rows, :], taps[0])
    for tap in range(1, taps.shape[0]):
        conv = conv + dot(hidden[tap * STEP : tap * STEP + rows, :], taps[tap])
    conv_out[...] = conv
    act = gelu(conv).astype(BF16)
    act_out[...] = act
    embed = (tok[...].astype(F32) + dot(act, point[...])).astype(BF16)
    embed_out[...] = embed
    donor = dot(embed, donor_w[...]).astype(BF16)
    accept = dot(embed, accept_w[...]).astype(BF16)
    even_feat[:rows, :] = jnp.where(is_odd, donor, accept)
    odd_feat[:rows, :] = jnp.where(is_odd, accept, donor)
    even_feat[pl.ds(rows, SLOTS), :] = meta[...]
    odd_feat[pl.ds(rows, SLOTS), :] = meta[...]


def side_kernel(
    odd, even_edge, odd_edge, gain, hidden, conv, act, embed, order, eye,
    factor, slope, hidden_t, act_t, embed_t,
):
    is_odd = odd[0] > 0
    low = jnp.where(is_odd, even_edge[...], odd_edge[...])
    high = jnp.where(is_odd, odd_edge[...], even_edge[...])
    for edge, at in ((low, 0), (high, STEP)):
        v = edge.astype(F32)
        unit = v * rms(v)
        factor[pl.ds(at, STEP), :] = (gelu_both(unit * gain[...])[1] * unit).astype(BF16)

    @pl.loop(0, conv.shape[0] // STEP)
    def _(i):
        here = pl.ds(pl.multiple_of(i * STEP, STEP), STEP)
        slope[here, :] = gelu_both(conv[here, :])[1]

    hidden_t[...] = dot_t(order[...], hidden[...]).astype(BF16)
    embed_t[...] = dot_t(eye[...], embed[...]).astype(BF16)
    inner = act.shape[1]
    act_t[...] = dot_t(eye[:inner, :inner], act[...]).astype(BF16)


def pair_kernel(distance, *refs):
    if distance == 0:
        odd, own, even0, odd0, d_donor, d_accept, loss = refs
        d_donor[...] = jnp.zeros_like(d_donor)
        d_accept[...] = jnp.zeros_like(d_accept)
        loss[...] = jnp.zeros_like(loss)
    else:
        odd, own, far, even0, odd0, even1, odd1, dd_in, da_in, loss_in, d_donor, d_accept, loss = refs
        d_donor[...] = dd_in[...]
        d_accept[...] = da_in[...]
        loss[...] = loss_in[...]
    is_odd = odd[0] > 0
    scale = even0.shape[1] ** (-0.5)
    per_device = d_donor.shape[0] // PANEL
    row = lax.broadcasted_iota(jnp.int32, (PANEL, PANEL), 0)
    col = lax.broadcasted_iota(jnp.int32, (PANEL, PANEL), 1)

    def place(block):
        return pl.ds(pl.multiple_of(block * PANEL, PANEL), PANEL)

    def own_donor(block):
        return jnp.where(is_odd, odd0[place(block), :], even0[place(block), :])

    def own_accept(block):
        return jnp.where(is_odd, even0[place(block), :], odd0[place(block), :])

    if distance == 0:
        far_accept, far_donor = own_accept, None
    else:

        def far_accept(block):
            return jnp.where(is_odd, odd1[place(block), :], even1[place(block), :])

        def far_donor(block):
            return jnp.where(is_odd, even1[place(block), :], odd1[place(block), :])

    def visit(meta, j, donors, acceptors, is_owner):
        accept_block = meta[j, 2] - distance * per_device
        here = (meta[j, 4] > 0) & (accept_block >= 0) & (accept_block < per_device)

        @pl.when(here)
        def _():
            donor_block = meta[j, 0]
            dpan = donors(donor_block)
            apan = acceptors(accept_block)
            scores = dot_t(dpan, apan) * scale
            target = ((row == meta[j, 1]) & (col == meta[j, 3])).astype(F32)
            small = jnp.exp(-jnp.abs(scores))
            inverse = 1.0 / (1.0 + small)
            sigmoid = jnp.where(scores >= 0, inverse, small * inverse)
            dscore = ((sigmoid - target) * LOSS_WEIGHT).astype(BF16)
            if is_owner:
                loss[...] += (jnp.maximum(scores, 0.0) + jnp.log1p(small)) - target * scores
                d_donor[place(donor_block), :] += dot(dscore, apan) * scale
            if distance == 0 or not is_owner:
                d_accept[place(accept_block), :] += scale * lax.dot_general(
                    dscore, dpan, (((0,), (0,)), ((), ())), preferred_element_type=F32
                )

    @pl.loop(0, SLOTS)
    def _(j):
        visit(own, j, own_donor, far_accept, True)
        if distance > 0:
            visit(far, j, far_donor, own_accept, False)


def relative(target, y, first):
    code = (target ^ (target >> 1)) ^ (y ^ (y >> 1))
    low, high = code & 1, code >> 1
    return low * 2 + high if first == 0 else high * 2 + low


def tap_grad_kernel(
    place, d_donor, d_accept, point, donor_w, accept_w, slope, hidden_t,
    keep, send, d_conv, d_feat,
):
    rows, heads = d_donor.shape
    channels = hidden_t.shape[0]

    dd = d_donor[...].astype(BF16)
    da = d_accept[...].astype(BF16)
    d_feat[:, :heads] = dd
    d_feat[:, heads:] = da
    d_embed = (dot_t(dd, donor_w[...]) + dot_t(da, accept_w[...])).astype(BF16)
    d_conv[...] = (dot_t(d_embed, point[...]) * slope[...]).astype(BF16)

    lanes = d_conv.shape[1] // 128
    half_rows = channels // 2
    slab = [relative(target, place[1], 1) for target in range(4)]
    for tap in range(3):
        for half in range(2):
            part = dot(
                hidden_t[half * half_rows : (half + 1) * half_rows, tap * STEP : tap * STEP + rows],
                d_conv[...],
            ).astype(BF16)

            def store(into, part=part, tap=tap):
                for k in range(4):
                    for lane in range(lanes):
                        into[slab[k], tap * lanes + lane] = part[
                            k * PIECE : (k + 1) * PIECE, lane * 128 : (lane + 1) * 128
                        ]

            pl.when(place[0] == half)(lambda: store(keep))
            pl.when(place[0] != half)(lambda: store(send))


def head_grad_kernel(
    place, d_conv, d_feat, loss, taps, factor, edge_factor, act_t, embed_t, head_sum,
):
    rows = d_conv.shape[0]
    channels = embed_t.shape[0]
    inner = act_t.shape[0]
    slab = [relative(target, place[1], 0) for target in range(4)]

    def put(part, base, group_rows, first):
        for lane in range(4):
            for k in range(part.shape[0] // PIECE):
                piece = first + lane * (group_rows // PIECE) + k + base
                chunk, third = piece // 3, piece % 3
                head_sum[slab[chunk // 4], chunk % 4, third * PIECE : (third + 1) * PIECE, :] = part[
                    k * PIECE : (k + 1) * PIECE, lane * 128 : (lane + 1) * 128
                ]

    for i in range(2):
        part = dot(embed_t[i * 4 * PIECE : (i + 1) * 4 * PIECE, :], d_feat[...]).astype(BF16)
        put(part, 4 * i, channels, 0)
    put(dot(act_t[...], d_feat[...]).astype(BF16), 0, inner, 4 * channels // PIECE)

    total = jnp.zeros((8, channels), F32)
    edge = edge_factor.shape[0] // 2
    for tap in range(taps.shape[0]):
        product = dot_t(d_conv[...], taps[tap])
        if tap == 0:
            weights = jnp.concatenate([edge_factor[:edge, :], factor[: rows - edge, :]], axis=0)
        elif tap == 1:
            weights = factor[...]
        else:
            weights = jnp.concatenate([factor[edge:, :], edge_factor[edge:, :]], axis=0)
        product = product * weights.astype(F32)
        total = total + jnp.sum(product.reshape(rows // 8, 8, channels), axis=0)
    gain = jnp.sum(total, axis=0, keepdims=True)
    loss_row = jnp.sum(loss[...], axis=0, keepdims=True) * LOSS_WEIGHT
    loss_all = jnp.broadcast_to(jnp.sum(loss_row, axis=1, keepdims=True), (1, 128))
    at_row = lax.broadcasted_iota(jnp.int32, (EXTRA_ROWS, 128), 0)
    for chunk in range(16):
        if chunk < channels // 128:
            value = gain[:, chunk * 128 : (chunk + 1) * 128]
        elif chunk == channels // 128:
            value = loss_all
        else:
            value = jnp.zeros((1, 128), F32)
        coarse = value.astype(BF16).astype(F32)
        block = jnp.where(at_row == 0, coarse, 0.0) + jnp.where(at_row == 8, value - coarse, 0.0)
        head_sum[slab[chunk // 4], chunk % 4, CHUNK_ROWS:, :] = block.astype(BF16)


def split_rows(total):
    value = total[CHUNK_ROWS : CHUNK_ROWS + 8] + total[CHUNK_ROWS + 8 : CHUNK_ROWS + 16]
    coarse = value.astype(BF16).astype(F32)
    return jnp.concatenate([total[:CHUNK_ROWS], coarse, value - coarse], axis=0).astype(BF16)


def core_sum_kernel(taps, received, kept, send):
    for k in range(2):
        for slab in range(taps.shape[1]):
            kept[k, slab] = taps[k, slab].astype(F32) + received[k, slab].astype(F32)
            send[k, slab] = (
                taps[k + 2, slab].astype(F32) + received[k + 2, slab].astype(F32)
            ).astype(BF16)


def head_sum_kernel(head, received, kept, send):
    for zq in range(4):
        kept[zq] = head[0, zq].astype(F32) + received[0, zq].astype(F32)
        send[zq] = split_rows(head[1, zq].astype(F32) + received[1, zq].astype(F32))


def tap_sum_kernel(before, received, kept, send):
    for slab in range(before.shape[1]):
        kept[slab] = before[0, slab] + received[0, slab].astype(F32)
        send[slab] = (before[1, slab] + received[1, slab].astype(F32)).astype(BF16)


def join_kernel(head, head_in, taps, taps_in, both):
    chunk_rows = head.shape[1]
    for zq in range(4):
        both[zq, :chunk_rows, :] = split_rows(head[zq] + head_in[zq].astype(F32))
        here = slice(zq * 24, (zq + 1) * 24)
        parts = [taps[k, here] + taps_in[k, here].astype(F32) for k in range(taps.shape[0])]
        parts.append(jnp.zeros((8, 128), F32))
        both[zq, chunk_rows:, :] = jnp.concatenate(parts, axis=0).astype(BF16)


def line_sum_kernel(place, parts, pick, send, mine):
    total = parts[0].astype(F32)
    for zq in range(1, 4):
        total = total + parts[zq].astype(F32)
    chunk_rows = CHUNK_ROWS + EXTRA_ROWS
    send[:chunk_rows, :] = split_rows(total[:chunk_rows])
    taps = total[chunk_rows:].astype(BF16)
    half = mine.shape[0]
    zb = place[2]

    def picked(which):
        return dot(pick[pl.ds(pl.multiple_of(which * half, half), half), :], taps).astype(BF16)

    send[chunk_rows:, :] = picked(1 - zb)
    mine[...] = picked(zb)


def far_sum_kernel(sent, received, mine, one, two, head, taps):
    chunk_rows = head.shape[1]
    total = split_rows(sent[:chunk_rows, :].astype(F32) + received[:chunk_rows, :].astype(F32))
    for zq in range(head.shape[0]):
        head[zq] = total
    near = mine[...].astype(F32) + received[chunk_rows:, :].astype(F32)
    taps[...] = (near + (one[...].astype(F32) + two[...].astype(F32))).astype(BF16)


def line_total_kernel(own, one, two, three, total):
    even = own[...].astype(F32) + two[...].astype(F32)
    total[...] = even + (one[...].astype(F32) + three[...].astype(F32))


def finish_kernel(
    place, own, behind, ahead, low, high, donor_w, accept_w,
    grad_donor, grad_accept, grad_point, gain, loss, held, act_donor, act_accept,
):
    count = held.shape[0]
    for step, part in ((0, own), (3, behind), (1, ahead)):
        held[lax.rem(place[1] + step, count)] = part[...]
    opposite = lax.rem(place[1] + 2, count)
    middle = low.shape[0]
    held[opposite, :middle, :] = low[...]
    held[opposite, middle:, :] = high[...]
    channels = grad_donor.shape[0]
    inner = act_donor.shape[0]
    chunk_rows = CHUNK_ROWS + EXTRA_ROWS
    piece = 0
    for into in (grad_donor, grad_accept, act_donor, act_accept):
        for lane in range(2):
            for k in range(into.shape[0] // PIECE):
                chunk, third = piece // 3, piece % 3
                at = (chunk % 4) * chunk_rows + third * PIECE
                into[k * PIECE : (k + 1) * PIECE, lane * 128 : (lane + 1) * 128] = held[
                    chunk // 4, at : at + PIECE, :
                ]
                piece += 1

    grad_point[...] = (
        dot_t(act_donor[...], donor_w[...]) + dot_t(act_accept[...], accept_w[...])
    ).astype(BF16)

    for chunk in range(channels // 128 + 1):
        at = (chunk % 4) * chunk_rows + CHUNK_ROWS
        block = held[chunk // 4, at : at + EXTRA_ROWS, :].astype(F32)
        value = block[0:1, :] + block[8:9, :]
        if chunk < channels // 128:
            gain[:, chunk * 128 : (chunk + 1) * 128] = value
        else:
            loss[...] = value


def swapped(block, first, between_lines=True):
    count = lax.axis_size(SEQ)
    pairs = [(i, i + 1) for i in range(first, count - 1, 2) if between_lines or i % 8 < 7]
    return lax.ppermute(block, SEQ, pairs + [(j, i) for i, j in pairs])


def swap_parts(parts, axis):
    return lax.all_to_all(parts, axis, 0, 0, tiled=True)


def on_device(
    activations, norm_gain, dilated_tap_weight, point_weight, donor_weight, acceptor_weight,
    pair_sites, pair_count, order, eye, pick,
):
    tokens = activations[0]
    rows, channels = tokens.shape
    tap_count, _, inner = dilated_tap_weight.shape
    heads = donor_weight.shape[1]
    blocks = rows // PANEL
    shape = jax.ShapeDtypeStruct
    here = lax.axis_index(SEQ)
    line = lax.axis_index(("zb", "zq"))
    is_odd = (lax.axis_index("zq") & 1) > 0
    odd = is_odd.astype(jnp.int32)[None]
    start, end = tokens[:STEP], tokens[rows - STEP :]
    even_edge = swapped(jnp.where(is_odd, start, end), 0)
    odd_edge = swapped(jnp.where(is_odd, end, start), 1)
    gain = norm_gain[None]
    sites = pair_sites[0]
    first = here * blocks
    live = (jnp.arange(SLOTS, dtype=jnp.int32) < pair_count[0, 0]).astype(jnp.int32)
    meta = jnp.stack(
        [
            sites[:, 0] // PANEL - first,
            sites[:, 0] % PANEL,
            sites[:, 1] // PANEL - first,
            sites[:, 1] % PANEL,
            live,
        ]
        + [jnp.zeros_like(live)] * 3,
        axis=1,
    )
    meta_rows = jnp.pad(meta.astype(BF16), ((0, 0), (0, heads - meta.shape[1])))

    mine, factor = call(
        own_kernel, [shape((rows, channels), BF16)] * 2, [VM] * 2, 12, 2_000_000_000
    )(tokens, gain)
    (odd_hidden,) = call(edge_kernel, [shape((STEP, channels), BF16)], [VM] * 2, 8, 2_000_000_000)(odd_edge, gain)
    feat = shape((rows + SLOTS, heads), BF16)
    hidden, conv, act, embed, even_feat, odd_feat = call(
        forward_kernel,
        [
            shape((rows + 2 * STEP, channels), BF16),
            shape((rows, inner), F32),
            shape((rows, inner), BF16),
            shape((rows, channels), BF16),
            feat,
            feat,
        ],
        [SM] + [VM] * 10,
        20,
        4_000_000_000,
    )(
        odd, tokens, mine, even_edge, odd_hidden, gain, dilated_tap_weight, point_weight,
        donor_weight, acceptor_weight, meta_rows,
    )

    acc_shapes = [shape((rows, heads), F32), shape((rows, heads), F32), shape((PANEL, PANEL), F32)]
    acc = call(
        lambda *refs: pair_kernel(0, *refs), acc_shapes, [SM] * 2 + [VM] * 2, 12, 2_000_000_000
    )(1 - odd, meta, even_feat, odd_feat)
    edge_factor, slope, hidden_t, act_t, embed_t = call(
        side_kernel,
        [
            shape((2 * STEP, channels), BF16),
            shape((rows, inner), F32),
            shape((channels, rows + 2 * STEP), BF16),
            shape((inner, rows), BF16),
            shape((channels, rows), BF16),
        ],
        [SM] + [VM] * 9,
        20,
        6_000_000_000,
    )(odd, even_edge, odd_edge, gain, hidden, conv, act, embed, order, eye)
    count = lax.axis_size(SEQ)
    starts = range(0, count, 8)
    wide_pairs = [(i + k, i - 4 + k) for i in starts if i > 0 for k in (2, 3)]
    wide_pairs += [(i + k, i + 4 + k) for i in starts if i + 8 < count for k in (4, 5)]
    relay_pairs = [(i + 6, i + 7) for i in starts] + [(i + 1, i) for i in starts]
    wide_feat = jnp.where((line == 2) | (line == 5), even_feat, odd_feat)
    wide = lax.ppermute(wide_feat, SEQ, wide_pairs)
    relay = lax.ppermute(wide, SEQ, relay_pairs)
    at_end = (line == 0) | (line == 7)
    near_end = (line == 1) | (line == 6)
    short_far, long_far = odd_feat, even_feat
    for distance in range(1, SPAN + 1):
        if distance == 1:
            short_far, long_far = swapped(odd_feat, 0), swapped(even_feat, 1)
        else:
            short_far, long_far = swapped(long_far, 0), swapped(short_far, 1, distance <= 2)
        short_use, long_use = short_far, long_far
        if distance == 3:
            long_use = jnp.where(at_end, relay, long_far)
        if distance == 4:
            short_use = jnp.where(near_end, wide, short_far)
            long_use = jnp.where(at_end, wide, long_far)
        far_meta = jnp.where(is_odd, short_use[rows:, :8], long_use[rows:, :8]).astype(jnp.int32)
        acc = call(
            lambda *refs, distance=distance: pair_kernel(distance, *refs),
            acc_shapes,
            [SM] * 3 + [VM] * 7,
            12,
            2_500_000_000,
        )(1 - odd, meta, far_meta, even_feat, odd_feat, long_use, short_use, *acc)

    chunk = CHUNK_ROWS + EXTRA_ROWS
    lanes = inner // 128
    slabs = tap_count * lanes
    y = lax.axis_index("y")
    place = jnp.stack([lax.axis_index("core"), y, lax.axis_index("zb")]).astype(jnp.int32)
    half = shape((4, slabs, PIECE, 128), BF16)
    keep, send, d_conv, d_feat = call(
        tap_grad_kernel,
        [half, half, shape((rows, inner), BF16), shape((rows, 2 * heads), BF16)],
        [SM] + [VM] * 7,
        24,
        4_000_000_000,
    )(place, acc[0], acc[1], point_weight, donor_weight, acceptor_weight, slope, hidden_t)
    received = lax.ppermute(send, "core", [(0, 1), (1, 0)])
    (head_sum,) = call(
        head_grad_kernel, [shape((4, 4, chunk, 128), BF16)], [SM] + [VM] * 8, 20, 4_000_000_000
    )(place, d_conv, d_feat, acc[2], dilated_tap_weight, factor, edge_factor, act_t, embed_t)

    first_pairs = [(0, 1), (1, 0), (2, 3), (3, 2)]
    second_pairs = [(1, 2), (2, 1), (3, 0), (0, 3)]
    quick = 1_000_000
    conv_kept, conv_send = call(
        core_sum_kernel, [shape((2, slabs, PIECE, 128), F32), shape((2, slabs, PIECE, 128), BF16)],
        [VM] * 2, 12, quick,
    )(keep, received)
    other = lax.ppermute(head_sum[2:], "y", first_pairs)
    heads_kept, heads_send = call(
        head_sum_kernel, [shape((4, chunk, 128), F32), shape((4, chunk, 128), BF16)], [VM] * 2, 12, quick
    )(head_sum, other)
    other = lax.ppermute(conv_send, "y", second_pairs)
    conv_kept, conv_send = call(
        tap_sum_kernel, [shape((slabs, PIECE, 128), F32), shape((slabs, PIECE, 128), BF16)],
        [VM] * 2, 12, quick,
    )(conv_kept, other)
    heads_in = lax.ppermute(heads_send, "y", second_pairs)
    conv_in = lax.ppermute(conv_send, "y", first_pairs)

    joint = chunk + 224
    (both,) = call(join_kernel, [shape((4, joint, 128), BF16)], [VM] * 4, 12, quick)(
        heads_kept, heads_in, conv_kept, conv_in
    )
    parts = swap_parts(both, "zq")
    sent, mine = call(
        line_sum_kernel, [shape((chunk + 112, 128), BF16), shape((112, 128), BF16)],
        [SM] + [VM] * 2, 8, quick,
    )(place, parts, pick)
    received = lax.ppermute(sent, "zb", [(0, 1), (1, 0)])
    across = lax.ppermute(mine, "zhi", [(0, 1), (1, 0)])
    corner = lax.ppermute(
        sent[chunk:], ("zb", "zhi"), [(0, 3), (3, 0), (1, 2), (2, 1)]
    )
    head_parts, conv_sum = call(
        far_sum_kernel, [shape((4, chunk, 128), BF16), shape((112, 128), BF16)], [VM] * 5, 8, quick
    )(sent, received, mine, across, corner)

    head_rows = 4 * chunk
    head_sum = swap_parts(head_parts, "zq").reshape(head_rows, 128)
    line = [
        lax.ppermute(conv_sum, "x", [(i, (i + step) % 4) for i in range(4)]) for step in (1, 2, 3)
    ]
    (conv_sum,) = call(line_total_kernel, [shape((112, 128), F32)], [VM] * 4, 8, quick)(conv_sum, *line)
    head_sum, conv_sum = lax.optimization_barrier((head_sum, conv_sum))
    other = lax.ppermute(conv_sum, "core", [(0, 1), (1, 0)])
    around = [(i, (i + 1) % 4) for i in range(4)]
    back = [(j, i) for i, j in around]
    behind = lax.ppermute(head_sum, "y", around)
    ahead = lax.ppermute(head_sum, "y", back)
    low = lax.ppermute(behind[: head_rows // 2], "y", around)
    high = lax.ppermute(ahead[head_rows // 2 :], "y", back)
    is_first = lax.axis_index("core") == 0
    pieces = jnp.stack([jnp.where(is_first, conv_sum, other), jnp.where(is_first, other, conv_sum)])
    pieces = pieces[:, : slabs * 12].reshape(2, tap_count, lanes, 12, 128)
    grad_conv = pieces.transpose(1, 0, 3, 2, 4).reshape(tap_count, 24, inner)
    head_weight = shape((channels, heads), BF16)
    grad_donor, grad_accept, grad_point, grad_gain, loss = call(
        finish_kernel,
        [head_weight, head_weight, shape((inner, channels), BF16), shape((1, channels), F32), shape((1, 128), F32)],
        [SM] + [VM] * 7,
        20,
        1_000_000_000,
        [
            pltpu.VMEM((4, head_rows, 128), BF16),
            pltpu.VMEM((inner, heads), BF16),
            pltpu.VMEM((inner, heads), BF16),
        ],
    )(place, head_sum, behind, ahead, low, high, donor_weight, acceptor_weight)
    return grad_conv, grad_point[None], grad_donor[None], grad_accept[None], grad_gain, loss[0, :1]


def channel_order():
    core, y, zq, zb, k = np.meshgrid(*[np.arange(n) for n in (2, 4, 4, 2, 12)], indexing="ij")
    channel = (24 * (8 * y + 4 * zb + zq) + 12 * core + k).reshape(-1)
    return np.eye(channel.size, dtype=np.float32)[channel]


def zb_halves():
    pick = np.zeros((224, 224), np.float32)
    for zb in range(2):
        for slab in range(9):
            for k in range(12):
                pick[112 * zb + 12 * slab + k, 24 * slab + 12 * zb + k] = 1.0
    return pick


def solution(mesh):
    fine = Mesh(mesh.devices.reshape(4, 2, 4, 2, 4, 2), SEQ + BATCH)
    placed = jax.shard_map(
        on_device,
        mesh=fine,
        in_specs=(
            P(BATCH, SEQ, None),
            P(),
            P(),
            P(),
            P(),
            P(),
            P(BATCH, SEQ, None),
            P(BATCH, SEQ),
            P(),
            P(),
            P(),
        ),
        out_specs=(
            P(None, SEQ, None),
            P(BATCH, None, None),
            P(BATCH, None, None),
            P(BATCH, None, None),
            P(BATCH, None),
            P(BATCH),
        ),
        check_vma=False,
    )

    def run(*arrays):
        order = jnp.asarray(channel_order(), BF16)
        eye = jnp.eye(order.shape[0], dtype=BF16)
        return placed(*arrays, order, eye, jnp.asarray(zb_halves(), BF16))

    return run
```

```python
import jax
import jax.numpy as jnp
import numpy as np
from jax import lax
from jax.experimental import pallas as pl
from jax.experimental.pallas import tpu as pltpu
from jax.sharding import Mesh
from jax.sharding import PartitionSpec as P

STEP = 128
PANEL = 128
SPAN = 4
SLOTS = 16
EPSILON = 1e-06
LOSS_WEIGHT = 1.0 / 128.0
SEQ = ("y", "zb", "zq")
BATCH = ("zhi", "x", "core")
F32 = jnp.float32
BF16 = jnp.bfloat16
ROOT = 0.7978845608028654
CUBIC = 0.044715
PIECE = 96
CHUNK_ROWS = 288
EXTRA_ROWS = 16


def dot(a, b):
    return lax.dot_general(a, b, (((1,), (0,)), ((), ())), preferred_element_type=F32)


def dot_t(a, b):
    return lax.dot_general(a, b, (((1,), (1,)), ((), ())), preferred_element_type=F32)


def gelu(v):
    return 0.5 * v * (1.0 + jnp.tanh(ROOT * (v + CUBIC * (v * v * v))))


def gelu_both(v):
    square = v * v
    t = jnp.tanh(ROOT * (v + CUBIC * (square * v)))
    half = 0.5 * (1.0 + t)
    return v * half, half + 0.5 * v * (1.0 - t * t) * (ROOT * (1.0 + 3.0 * CUBIC * square))


def rms(v):
    return lax.rsqrt(jnp.mean(v * v, axis=-1, keepdims=True) + EPSILON)


def call(kernel, outs, specs, megabytes, flops, scratch=()):
    return pl.pallas_call(
        kernel,
        out_shape=outs,
        in_specs=specs,
        out_specs=[VM] * len(outs),
        scratch_shapes=list(scratch),
        compiler_params=pltpu.CompilerParams(vmem_limit_bytes=megabytes * 1024 * 1024),
        cost_estimate=pl.CostEstimate(flops=flops, bytes_accessed=1_000_000, transcendentals=0),
    )


VM = pl.BlockSpec(memory_space=pltpu.VMEM)
SM = pl.BlockSpec(memory_space=pltpu.SMEM)


def own_kernel(tok, gain, hidden, factor):
    @pl.loop(0, tok.shape[0] // STEP)
    def _(i):
        here = pl.ds(pl.multiple_of(i * STEP, STEP), STEP)
        v = tok[here, :].astype(F32)
        unit = v * rms(v)
        value, slope = gelu_both(unit * gain[...])
        hidden[here, :] = value.astype(BF16)
        factor[here, :] = (slope * unit).astype(BF16)


def forward_kernel(
    odd, tok, mine, even_edge, odd_edge, gain, taps, point, donor_w, accept_w, meta,
    hidden, conv_out, act_out, embed_out, even_feat, odd_feat, wide_feat,
):
    rows = tok.shape[0]
    is_odd = odd[0] > 0
    low = jnp.where(is_odd, even_edge[...], odd_edge[...])
    high = jnp.where(is_odd, odd_edge[...], even_edge[...])
    for edge, at in ((low, 0), (high, STEP + rows)):
        v = edge.astype(F32)
        hidden[pl.ds(at, STEP), :] = gelu(v * rms(v) * gain[...]).astype(BF16)
    hidden[pl.ds(STEP, rows), :] = mine[...]

    conv = dot(hidden[:rows, :], taps[0])
    for tap in range(1, taps.shape[0]):
        conv = conv + dot(hidden[tap * STEP : tap * STEP + rows, :], taps[tap])
    conv_out[...] = conv
    act = gelu(conv).astype(BF16)
    act_out[...] = act
    embed = (tok[...].astype(F32) + dot(act, point[...])).astype(BF16)
    embed_out[...] = embed
    donor = dot(embed, donor_w[...]).astype(BF16)
    accept = dot(embed, accept_w[...]).astype(BF16)
    even_feat[:rows, :] = jnp.where(is_odd, donor, accept)
    odd_feat[:rows, :] = jnp.where(is_odd, accept, donor)
    wide_feat[:rows, :] = jnp.where(odd[1] < 4, accept, donor)
    even_feat[pl.ds(rows, SLOTS), :] = meta[...]
    odd_feat[pl.ds(rows, SLOTS), :] = meta[...]
    wide_feat[pl.ds(rows, SLOTS), :] = meta[...]


def side_kernel(
    odd, even_edge, odd_edge, gain, hidden, conv, act, embed, order, eye,
    factor, slope, hidden_t, act_t, embed_t,
):
    is_odd = odd[0] > 0
    low = jnp.where(is_odd, even_edge[...], odd_edge[...])
    high = jnp.where(is_odd, odd_edge[...], even_edge[...])
    for edge, at in ((low, 0), (high, STEP)):
        v = edge.astype(F32)
        unit = v * rms(v)
        factor[pl.ds(at, STEP), :] = (gelu_both(unit * gain[...])[1] * unit).astype(BF16)

    @pl.loop(0, conv.shape[0] // STEP)
    def _(i):
        here = pl.ds(pl.multiple_of(i * STEP, STEP), STEP)
        slope[here, :] = gelu_both(conv[here, :])[1]

    hidden_t[...] = dot_t(order[...], hidden[...]).astype(BF16)
    embed_t[...] = dot_t(eye[...], embed[...]).astype(BF16)
    inner = act.shape[1]
    act_t[...] = dot_t(eye[:inner, :inner], act[...]).astype(BF16)


def pair_kernel(distance, *refs):
    if distance == 0:
        odd, own, even0, odd0, d_donor, d_accept, loss = refs
        d_donor[...] = jnp.zeros_like(d_donor)
        d_accept[...] = jnp.zeros_like(d_accept)
        loss[...] = jnp.zeros_like(loss)
    else:
        odd, own, far, even0, odd0, even1, odd1, dd_in, da_in, loss_in, d_donor, d_accept, loss = refs
        d_donor[...] = dd_in[...]
        d_accept[...] = da_in[...]
        loss[...] = loss_in[...]
    is_odd = odd[0] > 0
    scale = even0.shape[1] ** (-0.5)
    per_device = d_donor.shape[0] // PANEL
    row = lax.broadcasted_iota(jnp.int32, (PANEL, PANEL), 0)
    col = lax.broadcasted_iota(jnp.int32, (PANEL, PANEL), 1)

    def place(block):
        return pl.ds(pl.multiple_of(block * PANEL, PANEL), PANEL)

    def own_donor(block):
        return jnp.where(is_odd, odd0[place(block), :], even0[place(block), :])

    def own_accept(block):
        return jnp.where(is_odd, even0[place(block), :], odd0[place(block), :])

    if distance == 0:
        far_accept, far_donor = own_accept, None
    else:

        def far_accept(block):
            return jnp.where(is_odd, odd1[place(block), :], even1[place(block), :])

        def far_donor(block):
            return jnp.where(is_odd, even1[place(block), :], odd1[place(block), :])

    def visit(meta, j, donors, acceptors, is_owner):
        accept_block = meta[j, 2] - distance * per_device
        here = (meta[j, 4] > 0) & (accept_block >= 0) & (accept_block < per_device)

        @pl.when(here)
        def _():
            donor_block = meta[j, 0]
            dpan = donors(donor_block)
            apan = acceptors(accept_block)
            scores = dot_t(dpan, apan) * scale
            target = ((row == meta[j, 1]) & (col == meta[j, 3])).astype(F32)
            small = jnp.exp(-jnp.abs(scores))
            inverse = 1.0 / (1.0 + small)
            sigmoid = jnp.where(scores >= 0, inverse, small * inverse)
            dscore = ((sigmoid - target) * LOSS_WEIGHT).astype(BF16)
            if is_owner:
                loss[...] += (jnp.maximum(scores, 0.0) + jnp.log1p(small)) - target * scores
                d_donor[place(donor_block), :] += dot(dscore, apan) * scale
            if distance == 0 or not is_owner:
                d_accept[place(accept_block), :] += scale * lax.dot_general(
                    dscore, dpan, (((0,), (0,)), ((), ())), preferred_element_type=F32
                )

    @pl.loop(0, SLOTS)
    def _(j):
        visit(own, j, own_donor, far_accept, True)
        if distance > 0:
            visit(far, j, far_donor, own_accept, False)


def relative(target, y, first):
    code = (target ^ (target >> 1)) ^ (y ^ (y >> 1))
    low, high = code & 1, code >> 1
    return low * 2 + high if first == 0 else high * 2 + low


def tap_grad_kernel(
    place, d_donor, d_accept, point, donor_w, accept_w, slope, hidden_t,
    keep, send, d_conv, d_feat,
):
    rows, heads = d_donor.shape
    channels = hidden_t.shape[0]

    dd = d_donor[...].astype(BF16)
    da = d_accept[...].astype(BF16)
    d_feat[:, :heads] = dd
    d_feat[:, heads:] = da
    d_embed = (dot_t(dd, donor_w[...]) + dot_t(da, accept_w[...])).astype(BF16)
    d_conv[...] = (dot_t(d_embed, point[...]) * slope[...]).astype(BF16)

    lanes = d_conv.shape[1] // 128
    half_rows = channels // 2
    slab = [relative(target, place[1], 1) for target in range(4)]
    for tap in range(3):
        for half in range(2):
            part = dot(
                hidden_t[half * half_rows : (half + 1) * half_rows, tap * STEP : tap * STEP + rows],
                d_conv[...],
            ).astype(BF16)

            def store(into, part=part, tap=tap):
                for k in range(4):
                    for lane in range(lanes):
                        into[slab[k], tap * lanes + lane] = part[
                            k * PIECE : (k + 1) * PIECE, lane * 128 : (lane + 1) * 128
                        ]

            pl.when(place[0] == half)(lambda: store(keep))
            pl.when(place[0] != half)(lambda: store(send))


def head_grad_kernel(
    place, d_conv, d_feat, loss, taps, factor, edge_factor, act_t, embed_t, head_sum,
):
    rows = d_conv.shape[0]
    channels = embed_t.shape[0]
    inner = act_t.shape[0]
    slab = [relative(target, place[1], 0) for target in range(4)]

    def put(part, base, group_rows, first):
        for lane in range(4):
            for k in range(part.shape[0] // PIECE):
                piece = first + lane * (group_rows // PIECE) + k + base
                chunk, third = piece // 3, piece % 3
                head_sum[slab[chunk // 4], chunk % 4, third * PIECE : (third + 1) * PIECE, :] = part[
                    k * PIECE : (k + 1) * PIECE, lane * 128 : (lane + 1) * 128
                ]

    for i in range(2):
        part = dot(embed_t[i * 4 * PIECE : (i + 1) * 4 * PIECE, :], d_feat[...]).astype(BF16)
        put(part, 4 * i, channels, 0)
    put(dot(act_t[...], d_feat[...]).astype(BF16), 0, inner, 4 * channels // PIECE)

    total = jnp.zeros((8, channels), F32)
    edge = edge_factor.shape[0] // 2
    for tap in range(taps.shape[0]):
        product = dot_t(d_conv[...], taps[tap])
        if tap == 0:
            weights = jnp.concatenate([edge_factor[:edge, :], factor[: rows - edge, :]], axis=0)
        elif tap == 1:
            weights = factor[...]
        else:
            weights = jnp.concatenate([factor[edge:, :], edge_factor[edge:, :]], axis=0)
        product = product * weights.astype(F32)
        total = total + jnp.sum(product.reshape(rows // 8, 8, channels), axis=0)
    gain = jnp.sum(total, axis=0, keepdims=True)
    loss_row = jnp.sum(loss[...], axis=0, keepdims=True) * LOSS_WEIGHT
    loss_all = jnp.broadcast_to(jnp.sum(loss_row, axis=1, keepdims=True), (1, 128))
    at_row = lax.broadcasted_iota(jnp.int32, (EXTRA_ROWS, 128), 0)
    for chunk in range(16):
        if chunk < channels // 128:
            value = gain[:, chunk * 128 : (chunk + 1) * 128]
        elif chunk == channels // 128:
            value = loss_all
        else:
            value = jnp.zeros((1, 128), F32)
        coarse = value.astype(BF16).astype(F32)
        block = jnp.where(at_row == 0, coarse, 0.0) + jnp.where(at_row == 8, value - coarse, 0.0)
        head_sum[slab[chunk // 4], chunk % 4, CHUNK_ROWS:, :] = block.astype(BF16)


def split_rows(total):
    value = total[CHUNK_ROWS : CHUNK_ROWS + 8] + total[CHUNK_ROWS + 8 : CHUNK_ROWS + 16]
    coarse = value.astype(BF16).astype(F32)
    return jnp.concatenate([total[:CHUNK_ROWS], coarse, value - coarse], axis=0).astype(BF16)


def core_sum_kernel(taps, received, kept, send):
    for k in range(2):
        for slab in range(taps.shape[1]):
            kept[k, slab] = taps[k, slab].astype(F32) + received[k, slab].astype(F32)
            send[k, slab] = (
                taps[k + 2, slab].astype(F32) + received[k + 2, slab].astype(F32)
            ).astype(BF16)


def head_sum_kernel(head, received, kept, send):
    for zq in range(4):
        kept[zq] = head[0, zq].astype(F32) + received[0, zq].astype(F32)
        send[zq] = split_rows(head[1, zq].astype(F32) + received[1, zq].astype(F32))


def tap_sum_kernel(before, received, kept, send):
    for slab in range(before.shape[1]):
        kept[slab] = before[0, slab] + received[0, slab].astype(F32)
        send[slab] = (before[1, slab] + received[1, slab].astype(F32)).astype(BF16)


def join_kernel(head, head_in, taps, taps_in, both):
    chunk_rows = head.shape[1]
    for zq in range(4):
        both[zq, :chunk_rows, :] = split_rows(head[zq] + head_in[zq].astype(F32))
        here = slice(zq * 24, (zq + 1) * 24)
        parts = [taps[k, here] + taps_in[k, here].astype(F32) for k in range(taps.shape[0])]
        parts.append(jnp.zeros((8, 128), F32))
        both[zq, chunk_rows:, :] = jnp.concatenate(parts, axis=0).astype(BF16)


def line_sum_kernel(place, parts, pick, send, mine):
    total = parts[0].astype(F32)
    for zq in range(1, 4):
        total = total + parts[zq].astype(F32)
    chunk_rows = CHUNK_ROWS + EXTRA_ROWS
    send[:chunk_rows, :] = split_rows(total[:chunk_rows])
    taps = total[chunk_rows:].astype(BF16)
    half = mine.shape[0]
    zb = place[2]

    def picked(which):
        return dot(pick[pl.ds(pl.multiple_of(which * half, half), half), :], taps).astype(BF16)

    send[chunk_rows:, :] = picked(1 - zb)
    mine[...] = picked(zb)


def far_sum_kernel(sent, received, mine, one, two, head, taps):
    chunk_rows = head.shape[1]
    total = split_rows(sent[:chunk_rows, :].astype(F32) + received[:chunk_rows, :].astype(F32))
    for zq in range(head.shape[0]):
        head[zq] = total
    near = mine[...].astype(F32) + received[chunk_rows:, :].astype(F32)
    taps[...] = (near + (one[...].astype(F32) + two[...].astype(F32))).astype(BF16)


def add_kernel(one, two, total):
    total[...] = (one[...].astype(F32) + two[...].astype(F32)).astype(total.dtype)


def finish_kernel(
    place, own, behind, ahead, low, high, donor_w, accept_w,
    grad_donor, grad_accept, grad_point, gain, loss, held, act_donor, act_accept,
):
    count = held.shape[0]
    for step, part in ((0, own), (3, behind), (1, ahead)):
        held[lax.rem(place[1] + step, count)] = part[...]
    opposite = lax.rem(place[1] + 2, count)
    middle = low.shape[0]
    held[opposite, :middle, :] = low[...]
    held[opposite, middle:, :] = high[...]
    channels = grad_donor.shape[0]
    inner = act_donor.shape[0]
    chunk_rows = CHUNK_ROWS + EXTRA_ROWS
    piece = 0
    for into in (grad_donor, grad_accept, act_donor, act_accept):
        for lane in range(2):
            for k in range(into.shape[0] // PIECE):
                chunk, third = piece // 3, piece % 3
                at = (chunk % 4) * chunk_rows + third * PIECE
                into[k * PIECE : (k + 1) * PIECE, lane * 128 : (lane + 1) * 128] = held[
                    chunk // 4, at : at + PIECE, :
                ]
                piece += 1

    grad_point[...] = (
        dot_t(act_donor[...], donor_w[...]) + dot_t(act_accept[...], accept_w[...])
    ).astype(BF16)

    for chunk in range(channels // 128 + 1):
        at = (chunk % 4) * chunk_rows + CHUNK_ROWS
        block = held[chunk // 4, at : at + EXTRA_ROWS, :].astype(F32)
        value = block[0:1, :] + block[8:9, :]
        if chunk < channels // 128:
            gain[:, chunk * 128 : (chunk + 1) * 128] = value
        else:
            loss[...] = value


def swapped(block, first, between_lines=True):
    count = lax.axis_size(SEQ)
    pairs = [(i, i + 1) for i in range(first, count - 1, 2) if between_lines or i % 8 < 7]
    return lax.ppermute(block, SEQ, pairs + [(j, i) for i, j in pairs])


def swap_parts(parts, axis):
    return lax.all_to_all(parts, axis, 0, 0, tiled=True)


def on_device(
    activations, norm_gain, dilated_tap_weight, point_weight, donor_weight, acceptor_weight,
    pair_sites, pair_count, order, eye, pick,
):
    tokens = activations[0]
    rows, channels = tokens.shape
    tap_count, _, inner = dilated_tap_weight.shape
    heads = donor_weight.shape[1]
    blocks = rows // PANEL
    shape = jax.ShapeDtypeStruct
    here = lax.axis_index(SEQ)
    line = here % 8
    odd = jnp.stack([here % 2, line]).astype(jnp.int32)
    is_odd = odd[0] > 0
    start, end = tokens[:STEP], tokens[rows - STEP :]
    even_edge = swapped(jnp.where(is_odd, start, end), 0)
    odd_edge = swapped(jnp.where(is_odd, end, start), 1)
    gain = norm_gain[None]
    sites = pair_sites[0]
    first = here * blocks
    live = (jnp.arange(SLOTS, dtype=jnp.int32) < pair_count[0, 0]).astype(jnp.int32)
    meta = jnp.stack(
        [
            sites[:, 0] // PANEL - first,
            sites[:, 0] % PANEL,
            sites[:, 1] // PANEL - first,
            sites[:, 1] % PANEL,
            live,
        ]
        + [jnp.zeros_like(live)] * 3,
        axis=1,
    )
    meta_rows = jnp.pad(meta.astype(BF16), ((0, 0), (0, heads - meta.shape[1])))

    mine, factor = call(
        own_kernel, [shape((rows, channels), BF16)] * 2, [VM] * 2, 12, 2_000_000_000
    )(tokens, gain)
    feat = shape((rows + SLOTS, heads), BF16)
    hidden, conv, act, embed, even_feat, odd_feat, wide_feat = call(
        forward_kernel,
        [
            shape((rows + 2 * STEP, channels), BF16),
            shape((rows, inner), F32),
            shape((rows, inner), BF16),
            shape((rows, channels), BF16),
            feat,
            feat,
            feat,
        ],
        [SM] + [VM] * 10,
        20,
        4_000_000_000,
    )(
        odd, tokens, mine, even_edge, odd_edge, gain, dilated_tap_weight, point_weight,
        donor_weight, acceptor_weight, meta_rows,
    )

    acc_shapes = [shape((rows, heads), F32), shape((rows, heads), F32), shape((PANEL, PANEL), F32)]
    acc = call(
        lambda *refs: pair_kernel(0, *refs), acc_shapes, [SM] * 2 + [VM] * 2, 12, 2_000_000_000
    )(1 - odd[:1], meta, even_feat, odd_feat)
    edge_factor, slope, hidden_t, act_t, embed_t = call(
        side_kernel,
        [
            shape((2 * STEP, channels), BF16),
            shape((rows, inner), F32),
            shape((channels, rows + 2 * STEP), BF16),
            shape((inner, rows), BF16),
            shape((channels, rows), BF16),
        ],
        [SM] + [VM] * 9,
        20,
        6_000_000_000,
    )(odd, even_edge, odd_edge, gain, hidden, conv, act, embed, order, eye)
    count = lax.axis_size(SEQ)
    starts = range(0, count, 8)
    wide_pairs = [(i + k, i - 4 + k) for i in starts if i > 0 for k in (2, 3)]
    wide_pairs += [(i + k, i + 4 + k) for i in starts if i + 8 < count for k in (4, 5)]
    relay_pairs = [(i + 6, i + 7) for i in starts] + [(i + 1, i) for i in starts]
    wide = lax.ppermute(wide_feat, SEQ, wide_pairs)
    relay = lax.ppermute(wide, SEQ, relay_pairs)
    at_end = (line == 0) | (line == 7)
    near_end = (line == 1) | (line == 6)
    short_far, long_far = odd_feat, even_feat
    for distance in range(1, SPAN + 1):
        if distance == 1:
            short_far, long_far = swapped(odd_feat, 0), swapped(even_feat, 1)
        else:
            short_far, long_far = swapped(long_far, 0), swapped(short_far, 1, distance <= 2)
        short_use, long_use = short_far, long_far
        if distance == 3:
            long_use = jnp.where(at_end, relay, long_far)
        if distance == 4:
            short_use = jnp.where(near_end, wide, short_far)
            long_use = jnp.where(at_end, wide, long_far)
        far_meta = jnp.where(odd[0] > 0, short_use[rows:, :8], long_use[rows:, :8]).astype(jnp.int32)
        acc = call(
            lambda *refs, distance=distance: pair_kernel(distance, *refs),
            acc_shapes,
            [SM] * 3 + [VM] * 7,
            12,
            2_500_000_000,
        )(1 - odd[:1], meta, far_meta, even_feat, odd_feat, long_use, short_use, *acc)

    chunk = CHUNK_ROWS + EXTRA_ROWS
    lanes = inner // 128
    slabs = tap_count * lanes
    y = lax.axis_index("y")
    place = jnp.stack([lax.axis_index("core"), y, lax.axis_index("zb")]).astype(jnp.int32)
    half = shape((4, slabs, PIECE, 128), BF16)
    keep, send, d_conv, d_feat = call(
        tap_grad_kernel,
        [half, half, shape((rows, inner), BF16), shape((rows, 2 * heads), BF16)],
        [SM] + [VM] * 7,
        24,
        4_000_000_000,
    )(place, acc[0], acc[1], point_weight, donor_weight, acceptor_weight, slope, hidden_t)
    received = lax.ppermute(send, "core", [(0, 1), (1, 0)])
    (head_sum,) = call(
        head_grad_kernel, [shape((4, 4, chunk, 128), BF16)], [SM] + [VM] * 8, 20, 4_000_000_000
    )(place, d_conv, d_feat, acc[2], dilated_tap_weight, factor, edge_factor, act_t, embed_t)

    first_pairs = [(0, 1), (1, 0), (2, 3), (3, 2)]
    second_pairs = [(1, 2), (2, 1), (3, 0), (0, 3)]
    quick = 1_000_000
    conv_kept, conv_send = call(
        core_sum_kernel, [shape((2, slabs, PIECE, 128), F32), shape((2, slabs, PIECE, 128), BF16)],
        [VM] * 2, 12, quick,
    )(keep, received)
    other = lax.ppermute(head_sum[2:], "y", first_pairs)
    heads_kept, heads_send = call(
        head_sum_kernel, [shape((4, chunk, 128), F32), shape((4, chunk, 128), BF16)], [VM] * 2, 12, quick
    )(head_sum, other)
    other = lax.ppermute(conv_send, "y", second_pairs)
    conv_kept, conv_send = call(
        tap_sum_kernel, [shape((slabs, PIECE, 128), F32), shape((slabs, PIECE, 128), BF16)],
        [VM] * 2, 12, quick,
    )(conv_kept, other)
    heads_in = lax.ppermute(heads_send, "y", second_pairs)
    conv_in = lax.ppermute(conv_send, "y", first_pairs)

    joint = chunk + 224
    (both,) = call(join_kernel, [shape((4, joint, 128), BF16)], [VM] * 4, 12, quick)(
        heads_kept, heads_in, conv_kept, conv_in
    )
    parts = swap_parts(both, "zq")
    sent, mine = call(
        line_sum_kernel, [shape((chunk + 112, 128), BF16), shape((112, 128), BF16)],
        [SM] + [VM] * 2, 8, quick,
    )(place, parts, pick)
    received = lax.ppermute(sent, "zb", [(0, 1), (1, 0)])
    across = lax.ppermute(mine, "zhi", [(0, 1), (1, 0)])
    corner = lax.ppermute(
        sent[chunk:], ("zb", "zhi"), [(0, 3), (3, 0), (1, 2), (2, 1)]
    )
    head_parts, conv_sum = call(
        far_sum_kernel, [shape((4, chunk, 128), BF16), shape((112, 128), BF16)], [VM] * 5, 8, quick
    )(sent, received, mine, across, corner)

    head_rows = 4 * chunk
    head_sum = swap_parts(head_parts, "zq").reshape(head_rows, 128)
    other = lax.ppermute(conv_sum, "x", first_pairs)
    (conv_sum,) = call(add_kernel, [shape((112, 128), BF16)], [VM] * 2, 8, quick)(conv_sum, other)
    other = lax.ppermute(conv_sum, "x", second_pairs)
    (conv_sum,) = call(add_kernel, [shape((112, 128), F32)], [VM] * 2, 8, quick)(conv_sum, other)
    head_sum, conv_sum = lax.optimization_barrier((head_sum, conv_sum))
    other = lax.ppermute(conv_sum, "core", [(0, 1), (1, 0)])
    around = [(i, (i + 1) % 4) for i in range(4)]
    back = [(j, i) for i, j in around]
    behind = lax.ppermute(head_sum, "y", around)
    ahead = lax.ppermute(head_sum, "y", back)
    low = lax.ppermute(behind[: head_rows // 2], "y", around)
    high = lax.ppermute(ahead[head_rows // 2 :], "y", back)
    is_first = lax.axis_index("core") == 0
    pieces = jnp.stack([jnp.where(is_first, conv_sum, other), jnp.where(is_first, other, conv_sum)])
    pieces = pieces[:, : slabs * 12].reshape(2, tap_count, lanes, 12, 128)
    grad_conv = pieces.transpose(1, 0, 3, 2, 4).reshape(tap_count, 24, inner)
    head_weight = shape((channels, heads), BF16)
    grad_donor, grad_accept, grad_point, grad_gain, loss = call(
        finish_kernel,
        [head_weight, head_weight, shape((inner, channels), BF16), shape((1, channels), F32), shape((1, 128), F32)],
        [SM] + [VM] * 7,
        20,
        1_000_000_000,
        [
            pltpu.VMEM((4, head_rows, 128), BF16),
            pltpu.VMEM((inner, heads), BF16),
            pltpu.VMEM((inner, heads), BF16),
        ],
    )(place, head_sum, behind, ahead, low, high, donor_weight, acceptor_weight)
    return grad_conv, grad_point[None], grad_donor[None], grad_accept[None], grad_gain, loss[0, :1]


def channel_order():
    core, y, zq, zb, k = np.meshgrid(*[np.arange(n) for n in (2, 4, 4, 2, 12)], indexing="ij")
    channel = (24 * (8 * y + 4 * zb + zq) + 12 * core + k).reshape(-1)
    return np.eye(channel.size, dtype=np.float32)[channel]


def zb_halves():
    pick = np.zeros((224, 224), np.float32)
    for zb in range(2):
        for slab in range(9):
            for k in range(12):
                pick[112 * zb + 12 * slab + k, 24 * slab + 12 * zb + k] = 1.0
    return pick


def solution(mesh):
    fine = Mesh(mesh.devices.reshape(4, 2, 4, 2, 4, 2), SEQ + BATCH)
    placed = jax.shard_map(
        on_device,
        mesh=fine,
        in_specs=(
            P(BATCH, SEQ, None),
            P(),
            P(),
            P(),
            P(),
            P(),
            P(BATCH, SEQ, None),
            P(BATCH, SEQ),
            P(),
            P(),
            P(),
        ),
        out_specs=(
            P(None, SEQ, None),
            P(BATCH, None, None),
            P(BATCH, None, None),
            P(BATCH, None, None),
            P(BATCH, None),
            P(BATCH),
        ),
        check_vma=False,
    )

    def run(*arrays):
        order = jnp.asarray(channel_order(), BF16)
        eye = jnp.eye(order.shape[0], dtype=BF16)
        return placed(*arrays, order, eye, jnp.asarray(zb_halves(), BF16))

    return run
```

```python
import jax
import jax.numpy as jnp
import numpy as np
from jax import lax
from jax.experimental import pallas as pl
from jax.experimental.pallas import tpu as pltpu
from jax.sharding import Mesh
from jax.sharding import PartitionSpec as P

STEP = 128
PANEL = 128
SPAN = 4
SLOTS = 16
EPSILON = 1e-06
LOSS_WEIGHT = 1.0 / 128.0
SEQ = ("y", "zb", "zq")
BATCH = ("zhi", "x", "core")
F32 = jnp.float32
BF16 = jnp.bfloat16
ROOT = 0.7978845608028654
CUBIC = 0.044715
PIECE = 96
CHUNK_ROWS = 288
EXTRA_ROWS = 16


def dot(a, b):
    return lax.dot_general(a, b, (((1,), (0,)), ((), ())), preferred_element_type=F32)


def dot_t(a, b):
    return lax.dot_general(a, b, (((1,), (1,)), ((), ())), preferred_element_type=F32)


def gelu(v):
    return 0.5 * v * (1.0 + jnp.tanh(ROOT * (v + CUBIC * (v * v * v))))


def gelu_both(v):
    square = v * v
    t = jnp.tanh(ROOT * (v + CUBIC * (square * v)))
    half = 0.5 * (1.0 + t)
    return v * half, half + 0.5 * v * (1.0 - t * t) * (ROOT * (1.0 + 3.0 * CUBIC * square))


def rms(v):
    return lax.rsqrt(jnp.mean(v * v, axis=-1, keepdims=True) + EPSILON)


def call(kernel, outs, specs, megabytes, flops, scratch=()):
    return pl.pallas_call(
        kernel,
        out_shape=outs,
        in_specs=specs,
        out_specs=[VM] * len(outs),
        scratch_shapes=list(scratch),
        compiler_params=pltpu.CompilerParams(vmem_limit_bytes=megabytes * 1024 * 1024),
        cost_estimate=pl.CostEstimate(flops=flops, bytes_accessed=1_000_000, transcendentals=0),
    )


VM = pl.BlockSpec(memory_space=pltpu.VMEM)
SM = pl.BlockSpec(memory_space=pltpu.SMEM)


def own_kernel(tok, gain, hidden, factor):
    @pl.loop(0, tok.shape[0] // STEP)
    def _(i):
        here = pl.ds(pl.multiple_of(i * STEP, STEP), STEP)
        v = tok[here, :].astype(F32)
        unit = v * rms(v)
        value, slope = gelu_both(unit * gain[...])
        hidden[here, :] = value.astype(BF16)
        factor[here, :] = (slope * unit).astype(BF16)


def edge_kernel(edge, gain, hidden):
    v = edge[...].astype(F32)
    hidden[...] = gelu(v * rms(v) * gain[...]).astype(BF16)


def forward_kernel(
    odd, tok, mine, even_edge, odd_hidden, gain, taps, point, donor_w, accept_w, meta,
    hidden, conv_out, act_out, embed_out, even_feat, odd_feat,
):
    rows = tok.shape[0]
    is_odd = odd[0] > 0
    v = even_edge[...].astype(F32)
    even_hidden = gelu(v * rms(v) * gain[...]).astype(BF16)
    hidden[pl.ds(0, STEP), :] = jnp.where(is_odd, even_hidden, odd_hidden[...])
    hidden[pl.ds(STEP + rows, STEP), :] = jnp.where(is_odd, odd_hidden[...], even_hidden)
    hidden[pl.ds(STEP, rows), :] = mine[...]

    conv = dot(hidden[:rows, :], taps[0])
    for tap in range(1, taps.shape[0]):
        conv = conv + dot(hidden[tap * STEP : tap * STEP + rows, :], taps[tap])
    conv_out[...] = conv
    act = gelu(conv).astype(BF16)
    act_out[...] = act
    embed = (tok[...].astype(F32) + dot(act, point[...])).astype(BF16)
    embed_out[...] = embed
    donor = dot(embed, donor_w[...]).astype(BF16)
    accept = dot(embed, accept_w[...]).astype(BF16)
    even_feat[:rows, :] = jnp.where(is_odd, donor, accept)
    odd_feat[:rows, :] = jnp.where(is_odd, accept, donor)
    even_feat[pl.ds(rows, SLOTS), :] = meta[...]
    odd_feat[pl.ds(rows, SLOTS), :] = meta[...]


def side_kernel(
    odd, even_edge, odd_edge, gain, hidden, conv, act, embed, order, eye,
    factor, slope, hidden_t, act_t, embed_t,
):
    is_odd = odd[0] > 0
    low = jnp.where(is_odd, even_edge[...], odd_edge[...])
    high = jnp.where(is_odd, odd_edge[...], even_edge[...])
    for edge, at in ((low, 0), (high, STEP)):
        v = edge.astype(F32)
        unit = v * rms(v)
        factor[pl.ds(at, STEP), :] = (gelu_both(unit * gain[...])[1] * unit).astype(BF16)

    @pl.loop(0, conv.shape[0] // STEP)
    def _(i):
        here = pl.ds(pl.multiple_of(i * STEP, STEP), STEP)
        slope[here, :] = gelu_both(conv[here, :])[1]

    hidden_t[...] = dot_t(order[...], hidden[...]).astype(BF16)
    embed_t[...] = dot_t(eye[...], embed[...]).astype(BF16)
    inner = act.shape[1]
    act_t[...] = dot_t(eye[:inner, :inner], act[...]).astype(BF16)


def pair_kernel(distance, *refs):
    if distance == 0:
        odd, own, even0, odd0, d_donor, d_accept, loss = refs
        d_donor[...] = jnp.zeros_like(d_donor)
        d_accept[...] = jnp.zeros_like(d_accept)
        loss[...] = jnp.zeros_like(loss)
    else:
        odd, own, far, even0, odd0, even1, odd1, dd_in, da_in, loss_in, d_donor, d_accept, loss = refs
        d_donor[...] = dd_in[...]
        d_accept[...] = da_in[...]
        loss[...] = loss_in[...]
    is_odd = odd[0] > 0
    scale = even0.shape[1] ** (-0.5)
    per_device = d_donor.shape[0] // PANEL
    row = lax.broadcasted_iota(jnp.int32, (PANEL, PANEL), 0)
    col = lax.broadcasted_iota(jnp.int32, (PANEL, PANEL), 1)

    def place(block):
        return pl.ds(pl.multiple_of(block * PANEL, PANEL), PANEL)

    def own_donor(block):
        return jnp.where(is_odd, odd0[place(block), :], even0[place(block), :])

    def own_accept(block):
        return jnp.where(is_odd, even0[place(block), :], odd0[place(block), :])

    if distance == 0:
        far_accept, far_donor = own_accept, None
    else:

        def far_accept(block):
            return jnp.where(is_odd, odd1[place(block), :], even1[place(block), :])

        def far_donor(block):
            return jnp.where(is_odd, even1[place(block), :], odd1[place(block), :])

    def visit(meta, j, donors, acceptors, is_owner):
        accept_block = meta[j, 2] - distance * per_device
        here = (meta[j, 4] > 0) & (accept_block >= 0) & (accept_block < per_device)

        @pl.when(here)
        def _():
            donor_block = meta[j, 0]
            dpan = donors(donor_block)
            apan = acceptors(accept_block)
            scores = dot_t(dpan, apan) * scale
            target = ((row == meta[j, 1]) & (col == meta[j, 3])).astype(F32)
            small = jnp.exp(-jnp.abs(scores))
            inverse = 1.0 / (1.0 + small)
            sigmoid = jnp.where(scores >= 0, inverse, small * inverse)
            dscore = ((sigmoid - target) * LOSS_WEIGHT).astype(BF16)
            if is_owner:
                loss[...] += (jnp.maximum(scores, 0.0) + jnp.log1p(small)) - target * scores
                d_donor[place(donor_block), :] += dot(dscore, apan) * scale
            if distance == 0 or not is_owner:
                d_accept[place(accept_block), :] += scale * lax.dot_general(
                    dscore, dpan, (((0,), (0,)), ((), ())), preferred_element_type=F32
                )

    @pl.loop(0, SLOTS)
    def _(j):
        visit(own, j, own_donor, far_accept, True)
        if distance > 0:
            visit(far, j, far_donor, own_accept, False)


def relative(target, y, first):
    code = (target ^ (target >> 1)) ^ (y ^ (y >> 1))
    low, high = code & 1, code >> 1
    return low * 2 + high if first == 0 else high * 2 + low


def tap_grad_kernel(
    place, d_donor, d_accept, point, donor_w, accept_w, slope, hidden_t,
    keep, send, d_conv, d_feat,
):
    rows, heads = d_donor.shape
    channels = hidden_t.shape[0]

    dd = d_donor[...].astype(BF16)
    da = d_accept[...].astype(BF16)
    d_feat[:, :heads] = dd
    d_feat[:, heads:] = da
    d_embed = (dot_t(dd, donor_w[...]) + dot_t(da, accept_w[...])).astype(BF16)
    d_conv[...] = (dot_t(d_embed, point[...]) * slope[...]).astype(BF16)

    lanes = d_conv.shape[1] // 128
    half_rows = channels // 2
    slab = [relative(target, place[1], 1) for target in range(4)]
    for tap in range(3):
        for half in range(2):
            part = dot(
                hidden_t[half * half_rows : (half + 1) * half_rows, tap * STEP : tap * STEP + rows],
                d_conv[...],
            ).astype(BF16)

            def store(into, part=part, tap=tap):
                for k in range(4):
                    for lane in range(lanes):
                        into[slab[k], tap * lanes + lane] = part[
                            k * PIECE : (k + 1) * PIECE, lane * 128 : (lane + 1) * 128
                        ]

            pl.when(place[0] == half)(lambda: store(keep))
            pl.when(place[0] != half)(lambda: store(send))


def head_grad_kernel(
    place, d_conv, d_feat, loss, taps, factor, edge_factor, act_t, embed_t, head_sum,
):
    rows = d_conv.shape[0]
    channels = embed_t.shape[0]
    inner = act_t.shape[0]
    slab = [relative(target, place[1], 0) for target in range(4)]

    def put(part, base, group_rows, first):
        for lane in range(4):
            for k in range(part.shape[0] // PIECE):
                piece = first + lane * (group_rows // PIECE) + k + base
                chunk, third = piece // 3, piece % 3
                head_sum[slab[chunk // 4], chunk % 4, third * PIECE : (third + 1) * PIECE, :] = part[
                    k * PIECE : (k + 1) * PIECE, lane * 128 : (lane + 1) * 128
                ]

    for i in range(2):
        part = dot(embed_t[i * 4 * PIECE : (i + 1) * 4 * PIECE, :], d_feat[...]).astype(BF16)
        put(part, 4 * i, channels, 0)
    put(dot(act_t[...], d_feat[...]).astype(BF16), 0, inner, 4 * channels // PIECE)

    total = jnp.zeros((8, channels), F32)
    edge = edge_factor.shape[0] // 2
    for tap in range(taps.shape[0]):
        product = dot_t(d_conv[...], taps[tap])
        if tap == 0:
            weights = jnp.concatenate([edge_factor[:edge, :], factor[: rows - edge, :]], axis=0)
        elif tap == 1:
            weights = factor[...]
        else:
            weights = jnp.concatenate([factor[edge:, :], edge_factor[edge:, :]], axis=0)
        product = product * weights.astype(F32)
        total = total + jnp.sum(product.reshape(rows // 8, 8, channels), axis=0)
    gain = jnp.sum(total, axis=0, keepdims=True)
    loss_row = jnp.sum(loss[...], axis=0, keepdims=True) * LOSS_WEIGHT
    loss_all = jnp.broadcast_to(jnp.sum(loss_row, axis=1, keepdims=True), (1, 128))
    at_row = lax.broadcasted_iota(jnp.int32, (EXTRA_ROWS, 128), 0)
    for chunk in range(16):
        if chunk < channels // 128:
            value = gain[:, chunk * 128 : (chunk + 1) * 128]
        elif chunk == channels // 128:
            value = loss_all
        else:
            value = jnp.zeros((1, 128), F32)
        coarse = value.astype(BF16).astype(F32)
        block = jnp.where(at_row == 0, coarse, 0.0) + jnp.where(at_row == 8, value - coarse, 0.0)
        head_sum[slab[chunk // 4], chunk % 4, CHUNK_ROWS:, :] = block.astype(BF16)


def split_rows(total):
    value = total[CHUNK_ROWS : CHUNK_ROWS + 8] + total[CHUNK_ROWS + 8 : CHUNK_ROWS + 16]
    coarse = value.astype(BF16).astype(F32)
    return jnp.concatenate([total[:CHUNK_ROWS], coarse, value - coarse], axis=0).astype(BF16)


def core_sum_kernel(taps, received, kept, send):
    for k in range(2):
        for slab in range(taps.shape[1]):
            kept[k, slab] = taps[k, slab].astype(F32) + received[k, slab].astype(F32)
            send[k, slab] = (
                taps[k + 2, slab].astype(F32) + received[k + 2, slab].astype(F32)
            ).astype(BF16)


def head_sum_kernel(head, received, kept, send):
    for zq in range(4):
        kept[zq] = head[0, zq].astype(F32) + received[0, zq].astype(F32)
        send[zq] = split_rows(head[1, zq].astype(F32) + received[1, zq].astype(F32))


def tap_sum_kernel(before, received, kept, send):
    for slab in range(before.shape[1]):
        kept[slab] = before[0, slab] + received[0, slab].astype(F32)
        send[slab] = (before[1, slab] + received[1, slab].astype(F32)).astype(BF16)


def join_kernel(head, head_in, taps, taps_in, both):
    chunk_rows = head.shape[1]
    for zq in range(4):
        both[zq, :chunk_rows, :] = split_rows(head[zq] + head_in[zq].astype(F32))
        here = slice(zq * 24, (zq + 1) * 24)
        parts = [taps[k, here] + taps_in[k, here].astype(F32) for k in range(taps.shape[0])]
        parts.append(jnp.zeros((8, 128), F32))
        both[zq, chunk_rows:, :] = jnp.concatenate(parts, axis=0).astype(BF16)


def line_sum_kernel(place, parts, pick, send, mine):
    total = parts[0].astype(F32)
    for zq in range(1, 4):
        total = total + parts[zq].astype(F32)
    chunk_rows = CHUNK_ROWS + EXTRA_ROWS
    send[:chunk_rows, :] = split_rows(total[:chunk_rows])
    taps = total[chunk_rows:].astype(BF16)
    half = mine.shape[0]
    zb = place[2]

    def picked(which):
        return dot(pick[pl.ds(pl.multiple_of(which * half, half), half), :], taps).astype(BF16)

    send[chunk_rows:, :] = picked(1 - zb)
    mine[...] = picked(zb)


def far_sum_kernel(sent, received, mine, one, two, head, taps):
    chunk_rows = head.shape[1]
    total = split_rows(sent[:chunk_rows, :].astype(F32) + received[:chunk_rows, :].astype(F32))
    for zq in range(head.shape[0]):
        head[zq] = total
    near = mine[...].astype(F32) + received[chunk_rows:, :].astype(F32)
    taps[...] = (near + (one[...].astype(F32) + two[...].astype(F32))).astype(BF16)


def add_kernel(one, two, total):
    total[...] = (one[...].astype(F32) + two[...].astype(F32)).astype(total.dtype)


def finish_kernel(
    place, own, behind, ahead, low, high, donor_w, accept_w,
    grad_donor, grad_accept, grad_point, gain, loss, held, act_donor, act_accept,
):
    count = held.shape[0]
    for step, part in ((0, own), (3, behind), (1, ahead)):
        held[lax.rem(place[1] + step, count)] = part[...]
    opposite = lax.rem(place[1] + 2, count)
    middle = low.shape[0]
    held[opposite, :middle, :] = low[...]
    held[opposite, middle:, :] = high[...]
    channels = grad_donor.shape[0]
    inner = act_donor.shape[0]
    chunk_rows = CHUNK_ROWS + EXTRA_ROWS
    piece = 0
    for into in (grad_donor, grad_accept, act_donor, act_accept):
        for lane in range(2):
            for k in range(into.shape[0] // PIECE):
                chunk, third = piece // 3, piece % 3
                at = (chunk % 4) * chunk_rows + third * PIECE
                into[k * PIECE : (k + 1) * PIECE, lane * 128 : (lane + 1) * 128] = held[
                    chunk // 4, at : at + PIECE, :
                ]
                piece += 1

    grad_point[...] = (
        dot_t(act_donor[...], donor_w[...]) + dot_t(act_accept[...], accept_w[...])
    ).astype(BF16)

    for chunk in range(channels // 128 + 1):
        at = (chunk % 4) * chunk_rows + CHUNK_ROWS
        block = held[chunk // 4, at : at + EXTRA_ROWS, :].astype(F32)
        value = block[0:1, :] + block[8:9, :]
        if chunk < channels // 128:
            gain[:, chunk * 128 : (chunk + 1) * 128] = value
        else:
            loss[...] = value


def swapped(block, first, between_lines=True):
    count = lax.axis_size(SEQ)
    pairs = [(i, i + 1) for i in range(first, count - 1, 2) if between_lines or i % 8 < 7]
    return lax.ppermute(block, SEQ, pairs + [(j, i) for i, j in pairs])


def swap_parts(parts, axis):
    return lax.all_to_all(parts, axis, 0, 0, tiled=True)


def on_device(
    activations, norm_gain, dilated_tap_weight, point_weight, donor_weight, acceptor_weight,
    pair_sites, pair_count, order, eye, pick,
):
    tokens = activations[0]
    rows, channels = tokens.shape
    tap_count, _, inner = dilated_tap_weight.shape
    heads = donor_weight.shape[1]
    blocks = rows // PANEL
    shape = jax.ShapeDtypeStruct
    here = lax.axis_index(SEQ)
    line = lax.axis_index(("zb", "zq"))
    is_odd = (lax.axis_index("zq") & 1) > 0
    odd = is_odd.astype(jnp.int32)[None]
    start, end = tokens[:STEP], tokens[rows - STEP :]
    even_edge = swapped(jnp.where(is_odd, start, end), 0)
    odd_edge = swapped(jnp.where(is_odd, end, start), 1)
    gain = norm_gain[None]
    sites = pair_sites[0]
    first = here * blocks
    live = (jnp.arange(SLOTS, dtype=jnp.int32) < pair_count[0, 0]).astype(jnp.int32)
    meta = jnp.stack(
        [
            sites[:, 0] // PANEL - first,
            sites[:, 0] % PANEL,
            sites[:, 1] // PANEL - first,
            sites[:, 1] % PANEL,
            live,
        ]
        + [jnp.zeros_like(live)] * 3,
        axis=1,
    )
    meta_rows = jnp.pad(meta.astype(BF16), ((0, 0), (0, heads - meta.shape[1])))

    mine, factor = call(
        own_kernel, [shape((rows, channels), BF16)] * 2, [VM] * 2, 12, 2_000_000_000
    )(tokens, gain)
    (odd_hidden,) = call(edge_kernel, [shape((STEP, channels), BF16)], [VM] * 2, 8, 2_000_000_000)(odd_edge, gain)
    feat = shape((rows + SLOTS, heads), BF16)
    hidden, conv, act, embed, even_feat, odd_feat = call(
        forward_kernel,
        [
            shape((rows + 2 * STEP, channels), BF16),
            shape((rows, inner), F32),
            shape((rows, inner), BF16),
            shape((rows, channels), BF16),
            feat,
            feat,
        ],
        [SM] + [VM] * 10,
        20,
        4_000_000_000,
    )(
        odd, tokens, mine, even_edge, odd_hidden, gain, dilated_tap_weight, point_weight,
        donor_weight, acceptor_weight, meta_rows,
    )

    acc_shapes = [shape((rows, heads), F32), shape((rows, heads), F32), shape((PANEL, PANEL), F32)]
    acc = call(
        lambda *refs: pair_kernel(0, *refs), acc_shapes, [SM] * 2 + [VM] * 2, 12, 2_000_000_000
    )(1 - odd, meta, even_feat, odd_feat)
    edge_factor, slope, hidden_t, act_t, embed_t = call(
        side_kernel,
        [
            shape((2 * STEP, channels), BF16),
            shape((rows, inner), F32),
            shape((channels, rows + 2 * STEP), BF16),
            shape((inner, rows), BF16),
            shape((channels, rows), BF16),
        ],
        [SM] + [VM] * 9,
        20,
        6_000_000_000,
    )(odd, even_edge, odd_edge, gain, hidden, conv, act, embed, order, eye)
    count = lax.axis_size(SEQ)
    starts = range(0, count, 8)
    wide_pairs = [(i + k, i - 4 + k) for i in starts if i > 0 for k in (2, 3)]
    wide_pairs += [(i + k, i + 4 + k) for i in starts if i + 8 < count for k in (4, 5)]
    relay_pairs = [(i + 6, i + 7) for i in starts] + [(i + 1, i) for i in starts]
    wide_feat = jnp.where((line == 2) | (line == 5), even_feat, odd_feat)
    wide = lax.ppermute(wide_feat, SEQ, wide_pairs)
    relay = lax.ppermute(wide, SEQ, relay_pairs)
    at_end = (line == 0) | (line == 7)
    near_end = (line == 1) | (line == 6)
    short_far, long_far = odd_feat, even_feat
    for distance in range(1, SPAN + 1):
        if distance == 1:
            short_far, long_far = swapped(odd_feat, 0), swapped(even_feat, 1)
        else:
            short_far, long_far = swapped(long_far, 0), swapped(short_far, 1, distance <= 2)
        short_use, long_use = short_far, long_far
        if distance == 3:
            long_use = jnp.where(at_end, relay, long_far)
        if distance == 4:
            short_use = jnp.where(near_end, wide, short_far)
            long_use = jnp.where(at_end, wide, long_far)
        far_meta = jnp.where(is_odd, short_use[rows:, :8], long_use[rows:, :8]).astype(jnp.int32)
        acc = call(
            lambda *refs, distance=distance: pair_kernel(distance, *refs),
            acc_shapes,
            [SM] * 3 + [VM] * 7,
            12,
            2_500_000_000,
        )(1 - odd, meta, far_meta, even_feat, odd_feat, long_use, short_use, *acc)

    chunk = CHUNK_ROWS + EXTRA_ROWS
    lanes = inner // 128
    slabs = tap_count * lanes
    y = lax.axis_index("y")
    place = jnp.stack([lax.axis_index("core"), y, lax.axis_index("zb")]).astype(jnp.int32)
    half = shape((4, slabs, PIECE, 128), BF16)
    keep, send, d_conv, d_feat = call(
        tap_grad_kernel,
        [half, half, shape((rows, inner), BF16), shape((rows, 2 * heads), BF16)],
        [SM] + [VM] * 7,
        24,
        4_000_000_000,
    )(place, acc[0], acc[1], point_weight, donor_weight, acceptor_weight, slope, hidden_t)
    received = lax.ppermute(send, "core", [(0, 1), (1, 0)])
    (head_sum,) = call(
        head_grad_kernel, [shape((4, 4, chunk, 128), BF16)], [SM] + [VM] * 8, 20, 4_000_000_000
    )(place, d_conv, d_feat, acc[2], dilated_tap_weight, factor, edge_factor, act_t, embed_t)

    first_pairs = [(0, 1), (1, 0), (2, 3), (3, 2)]
    second_pairs = [(1, 2), (2, 1), (3, 0), (0, 3)]
    quick = 1_000_000
    conv_kept, conv_send = call(
        core_sum_kernel, [shape((2, slabs, PIECE, 128), F32), shape((2, slabs, PIECE, 128), BF16)],
        [VM] * 2, 12, quick,
    )(keep, received)
    other = lax.ppermute(head_sum[2:], "y", first_pairs)
    heads_kept, heads_send = call(
        head_sum_kernel, [shape((4, chunk, 128), F32), shape((4, chunk, 128), BF16)], [VM] * 2, 12, quick
    )(head_sum, other)
    other = lax.ppermute(conv_send, "y", second_pairs)
    conv_kept, conv_send = call(
        tap_sum_kernel, [shape((slabs, PIECE, 128), F32), shape((slabs, PIECE, 128), BF16)],
        [VM] * 2, 12, quick,
    )(conv_kept, other)
    heads_in = lax.ppermute(heads_send, "y", second_pairs)
    conv_in = lax.ppermute(conv_send, "y", first_pairs)

    joint = chunk + 224
    (both,) = call(join_kernel, [shape((4, joint, 128), BF16)], [VM] * 4, 12, quick)(
        heads_kept, heads_in, conv_kept, conv_in
    )
    parts = swap_parts(both, "zq")
    sent, mine = call(
        line_sum_kernel, [shape((chunk + 112, 128), BF16), shape((112, 128), BF16)],
        [SM] + [VM] * 2, 8, quick,
    )(place, parts, pick)
    received = lax.ppermute(sent, "zb", [(0, 1), (1, 0)])
    across = lax.ppermute(mine, "zhi", [(0, 1), (1, 0)])
    corner = lax.ppermute(
        sent[chunk:], ("zb", "zhi"), [(0, 3), (3, 0), (1, 2), (2, 1)]
    )
    head_parts, conv_sum = call(
        far_sum_kernel, [shape((4, chunk, 128), BF16), shape((112, 128), BF16)], [VM] * 5, 8, quick
    )(sent, received, mine, across, corner)

    head_rows = 4 * chunk
    head_sum = swap_parts(head_parts, "zq").reshape(head_rows, 128)
    other = lax.ppermute(conv_sum, "x", first_pairs)
    (conv_sum,) = call(add_kernel, [shape((112, 128), BF16)], [VM] * 2, 8, quick)(conv_sum, other)
    other = lax.ppermute(conv_sum, "x", second_pairs)
    (conv_sum,) = call(add_kernel, [shape((112, 128), F32)], [VM] * 2, 8, quick)(conv_sum, other)
    head_sum, conv_sum = lax.optimization_barrier((head_sum, conv_sum))
    other = lax.ppermute(conv_sum, "core", [(0, 1), (1, 0)])
    around = [(i, (i + 1) % 4) for i in range(4)]
    back = [(j, i) for i, j in around]
    behind = lax.ppermute(head_sum, "y", around)
    ahead = lax.ppermute(head_sum, "y", back)
    low = lax.ppermute(behind[: head_rows // 2], "y", around)
    high = lax.ppermute(ahead[head_rows // 2 :], "y", back)
    is_first = lax.axis_index("core") == 0
    pieces = jnp.stack([jnp.where(is_first, conv_sum, other), jnp.where(is_first, other, conv_sum)])
    pieces = pieces[:, : slabs * 12].reshape(2, tap_count, lanes, 12, 128)
    grad_conv = pieces.transpose(1, 0, 3, 2, 4).reshape(tap_count, 24, inner)
    head_weight = shape((channels, heads), BF16)
    grad_donor, grad_accept, grad_point, grad_gain, loss = call(
        finish_kernel,
        [head_weight, head_weight, shape((inner, channels), BF16), shape((1, channels), F32), shape((1, 128), F32)],
        [SM] + [VM] * 7,
        20,
        1_000_000_000,
        [
            pltpu.VMEM((4, head_rows, 128), BF16),
            pltpu.VMEM((inner, heads), BF16),
            pltpu.VMEM((inner, heads), BF16),
        ],
    )(place, head_sum, behind, ahead, low, high, donor_weight, acceptor_weight)
    return grad_conv, grad_point[None], grad_donor[None], grad_accept[None], grad_gain, loss[0, :1]


def channel_order():
    core, y, zq, zb, k = np.meshgrid(*[np.arange(n) for n in (2, 4, 4, 2, 12)], indexing="ij")
    channel = (24 * (8 * y + 4 * zb + zq) + 12 * core + k).reshape(-1)
    return np.eye(channel.size, dtype=np.float32)[channel]


def zb_halves():
    pick = np.zeros((224, 224), np.float32)
    for zb in range(2):
        for slab in range(9):
            for k in range(12):
                pick[112 * zb + 12 * slab + k, 24 * slab + 12 * zb + k] = 1.0
    return pick


def solution(mesh):
    fine = Mesh(mesh.devices.reshape(4, 2, 4, 2, 4, 2), SEQ + BATCH)
    placed = jax.shard_map(
        on_device,
        mesh=fine,
        in_specs=(
            P(BATCH, SEQ, None),
            P(),
            P(),
            P(),
            P(),
            P(),
            P(BATCH, SEQ, None),
            P(BATCH, SEQ),
            P(),
            P(),
            P(),
        ),
        out_specs=(
            P(None, SEQ, None),
            P(BATCH, None, None),
            P(BATCH, None, None),
            P(BATCH, None, None),
            P(BATCH, None),
            P(BATCH),
        ),
        check_vma=False,
    )

    def run(*arrays):
        order = jnp.asarray(channel_order(), BF16)
        eye = jnp.eye(order.shape[0], dtype=BF16)
        return placed(*arrays, order, eye, jnp.asarray(zb_halves(), BF16))

    return run
```
